256 devices in a mesh: seq: 64 (over y_hi, x, z), head: 4 (over y_lo, core).
Axes of the slice: x: 4, y: 4 (y_hi: 2, y_lo: 2; y = y_hi * 2 + y_lo), z: 8, core: 2. Of those that a mesh axis runs over, the one named last changes fastest.
Arguments:
- queries: bfloat16 [16384, 1024], P('seq', 'head'), may hold values from -40 to 40
- keys: bfloat16 [16384, 1024], P('seq', 'head'), may hold values from -12 to 12
- values: bfloat16 [16384, 1024], P('seq', 'head'), may hold values from -6 to 6
- residual: bfloat16 [16384, 1024], P('seq', 'head'), may hold values from -3 to 3
- reg_weight: bfloat16 [1024, 1024], P('head'), may hold values from -0.1875 to 0.1875
- targets: bfloat16 [256, 16, 1024], P('seq'), may hold values from -3 to 3
- block_track: int32 [128], replicated, may hold values from 0 to 255
- row_count: int32 [128], P('seq'), may hold values from 1 to 128, 12288 in all
- pool_slot: int32 [128, 128], P('seq'), may hold values from 0 to 15
Outputs:
- grad_reg: bfloat16 [1024, 1024], P('head')
- context_grad: bfloat16 [16384, 1024], P('seq', 'head')
The draws below stay inside these ranges and needn't reach their ends.
All inputs are finite; a program needn't handle non-finite values. No bound on the sum of `row_count` on one device may be relied on, other than what follows from the above.
Results may differ from the reference program's by a relative error of at most 0.019.
Values may be sent and summed in bfloat16 or wider, within the bound.
No kernel may reach another device: no remote copies, remote signals or barrier semaphores. Data moves between devices by JAX's collectives and lax.ppermute only.
A program may use at most 128 MiB of HBM per device.

```python
import math
import jax
import jax.numpy as jnp
import numpy as np
from jax import lax

D = 1024
HEADS = 16
HEAD_DIM = 64
TARGET_D = 1024
BLK = 128
POOL = 16
TOKENS = 16384
BLOCKS = 128
TRACKS = 256


def shared_attention(key):
    base = jax.random.fold_in(key, 101)
    query_key, key_key = jax.random.split(base, 2)
    query_draw = jnp.clip(1.6 * jax.random.normal(query_key, (TOKENS, D), jnp.float32), -11.0, 11.0)
    key_draw = jnp.clip(1.6 * jax.random.normal(key_key, (TOKENS, D), jnp.float32), -11.0, 11.0)
    return (query_draw, key_draw)


def draw_queries(key, part):
    return shared_attention(key)[0].astype(jnp.bfloat16)


def draw_keys(key, part):
    return shared_attention(key)[1].astype(jnp.bfloat16)


def plant(drawn, stream_key, smallest, top_value):
    spot = [jax.random.randint(jax.random.fold_in(stream_key, axis), (), 0, length) for axis, length in enumerate(drawn.shape)]
    widest = drawn.shape.index(max(drawn.shape))
    neighbour = spot[:widest] + [(spot[widest] + 1) % drawn.shape[widest]] + spot[widest + 1:]
    return drawn.at[tuple(spot)].set(smallest).at[tuple(neighbour)].set(top_value)


def shard_levels(key, shape, cuts, smallest, high):
    loudness, own = 1.0, jax.random.fold_in(key, 6)
    for dim, shards_of in cuts:
        steps = jnp.exp(jax.random.uniform(jax.random.fold_in(own, dim), (shards_of,), jnp.float32, smallest / len(cuts), high / len(cuts)))
        loudness = loudness * jnp.repeat(steps, shape[dim] // shards_of).reshape([-1 if axis == dim else 1 for axis in range(len(shape))])
    return loudness


def cumulative_ranks(count, skew):
    loads = [(1 << 20) // math.isqrt(standing ** skew) + 1 for standing in range(1, count + 1)]
    scale = 1 + sum(loads) // (1 << 30)
    return np.cumsum(np.array([max(1, weight // scale) for weight in loads]))


def skewed_ids(own_key, dims, amount, lean):
    listing = cumulative_ranks(amount, lean)
    lot = jax.random.randint(jax.random.fold_in(own_key, 1), dims, 0, int(listing[amount - 1]))
    standing = jnp.searchsorted(jnp.asarray(listing, jnp.int32), lot, side="right")
    return jax.random.permutation(jax.random.fold_in(own_key, 2), amount)[standing].astype(jnp.int32)


def split_up(count, total, limit, skew):
    portions = [(1 << 20) // math.isqrt(standing ** skew) + 1 for standing in range(2, count + 1)]
    rest, holding = total - limit - (count - 1), [1] * (count - 1)
    while rest > 0:
        free = [i for i in range(count - 1) if holding[i] < limit]
        mass, budget = sum([portions[i] for i in free]), rest
        for i in free:
            addition = min(limit - holding[i], max(1, budget * portions[i] // mass), rest)
            holding[i] = holding[i] + addition
            rest = rest - addition
    return np.array([limit] + holding)


def ragged_sizes(own_key, amount, total, limit, slope):
    if amount == 2:
        one = jax.random.randint(own_key, (), max(1, total - limit), min(limit, total - 1) + 1)
        return jnp.stack([one, total - one])
    lengths = jnp.asarray(split_up(amount, total, limit, slope), jnp.int32)
    pairs = (amount - 1) // 2
    source_of, taker = lengths[1:1 + 2 * pairs:2], lengths[2:2 + 2 * pairs:2]
    slack = jnp.minimum(source_of - 1, limit - taker)
    passed = jax.random.randint(jax.random.fold_in(own_key, 1), (pairs,), 0, 1 << 20) % (slack + 1)
    lengths = lengths.at[1:1 + 2 * pairs:2].set(source_of - passed).at[2:2 + 2 * pairs:2].set(taker + passed)
    return lengths[jax.random.permutation(jax.random.fold_in(own_key, 2), amount)]


def centred(key, extent, spread, reach, cuts=(), kind=jnp.bfloat16):
    drawn = spread * jax.random.normal(key, extent, jnp.float32)
    if cuts:
        drawn = drawn * shard_levels(key, extent, cuts, -0.22, 0.18)
    return jnp.clip(drawn, -reach, reach).astype(kind)


def setup_inputs(seed: int = 0) -> dict:
    seeds = jax.random.split(jax.random.key(seed), 10)
    return {
        "queries": draw_queries(jax.random.fold_in(seeds[9], 71), 0),
        "keys": draw_keys(jax.random.fold_in(seeds[9], 71), 0),
        "values": centred(seeds[2], (TOKENS, D), 1.0, 6.0, ((0, 64), (1, 4))),
        "residual": centred(seeds[3], (TOKENS, D), 0.5, 3.0, ((0, 64), (1, 4))),
        "reg_weight": centred(seeds[4], (D, TARGET_D), D ** -0.5, 0.1875, ((0, 4),)),
        "targets": centred(seeds[5], (TRACKS, POOL, TARGET_D), 0.5, 3.0, ((0, 64),)),
        "block_track": plant(skewed_ids(seeds[6], (BLOCKS,), TRACKS, 2), jax.random.fold_in(seeds[6], 3), 0, TRACKS - 1).astype(jnp.int32),
        "row_count": ragged_sizes(seeds[7], BLOCKS, 3 * BLK * BLOCKS // 4, BLK, 1).astype(jnp.int32),
        "pool_slot": plant(jax.random.randint(seeds[8], (BLOCKS, BLK), 0, POOL), jax.random.fold_in(seeds[8], 1), 0, POOL - 1).astype(jnp.int32),
    }


def attend(queries, keys, values):
    scale = HEAD_DIM ** -0.5
    block_size = min(512, TOKENS)
    query_heads = queries.reshape(TOKENS, HEADS, HEAD_DIM).transpose(1, 0, 2)
    key_heads = keys.reshape(TOKENS, HEADS, HEAD_DIM).transpose(1, 0, 2)
    value_heads = values.reshape(TOKENS, HEADS, HEAD_DIM).transpose(1, 0, 2)

    def per_head(operands):
        query_one, key_one, value_one = operands

        def per_block(query_block):
            scores = jnp.dot(query_block, key_one.T, preferred_element_type=jnp.float32) * scale
            largest = jnp.max(scores, axis=1, keepdims=True)
            exp_terms = jnp.exp(scores - largest)
            totals = jnp.sum(exp_terms, axis=1, keepdims=True)
            weighted = jnp.dot(exp_terms.astype(jnp.bfloat16), value_one, preferred_element_type=jnp.float32)
            return (weighted / totals).astype(jnp.bfloat16)

        blocks = query_one.reshape(TOKENS // block_size, block_size, HEAD_DIM)
        return lax.map(per_block, blocks).reshape(TOKENS, HEAD_DIM)

    context = lax.map(per_head, (query_heads, key_heads, value_heads))
    return context.transpose(1, 0, 2).reshape(TOKENS, D)


def reference(queries, keys, values, residual, reg_weight, targets, block_track, row_count, pool_slot):
    context = attend(queries, keys, values)
    stream = (residual.astype(jnp.float32) + context.astype(jnp.float32)).astype(jnp.bfloat16)
    stream_blocks = stream.reshape(BLOCKS, BLK, D).astype(jnp.float32)
    valid = jnp.arange(BLK, dtype=jnp.int32)[None, :] < row_count[:, None]
    match = pool_slot[:, None, :] == jnp.arange(POOL, dtype=jnp.int32)[None, :, None]
    selector = jnp.where(match & valid[:, None, :], 1.0, 0.0).astype(jnp.float32)
    pooled = jnp.einsum("bpr,brc->bpc", selector, stream_blocks, precision=lax.Precision.HIGHEST)
    slot_rows = jnp.sum(selector, axis=2)
    track_select = jnp.where(block_track[:, None] == jnp.arange(TRACKS, dtype=jnp.int32)[None, :], 1.0, 0.0).astype(jnp.float32)
    sums = jnp.einsum("bt,bpc->tpc", track_select, pooled, precision=lax.Precision.HIGHEST)
    counts = jnp.einsum("bt,bp->tp", track_select, slot_rows, precision=lax.Precision.HIGHEST)
    divisor = jnp.maximum(counts, 1.0)
    mean = (sums / divisor[:, :, None]).astype(jnp.bfloat16).reshape(TRACKS * POOL, D)
    prediction = jnp.dot(mean, reg_weight, preferred_element_type=jnp.float32)
    error = (prediction - targets.reshape(TRACKS * POOL, TARGET_D).astype(jnp.float32)).astype(jnp.bfloat16)
    grad_reg = jnp.dot(mean.T, error, preferred_element_type=jnp.float32).astype(jnp.bfloat16)
    mean_grad = jnp.dot(error, reg_weight.T, preferred_element_type=jnp.float32)
    track_grad = (mean_grad.reshape(TRACKS, POOL, D) / divisor[:, :, None]).astype(jnp.bfloat16)
    pooled_grad = jnp.einsum("bt,tpc->bpc", track_select, track_grad.astype(jnp.float32), precision=lax.Precision.HIGHEST)
    row_grad = jnp.einsum("bpr,bpc->brc", selector, pooled_grad, precision=lax.Precision.HIGHEST)
    context_grad = row_grad.reshape(TOKENS, D).astype(jnp.bfloat16)
    return grad_reg, context_grad
```

```python
import jax
import jax.numpy as jnp
from jax import lax
from jax.experimental import pallas as pl
from jax.experimental.pallas import tpu as pltpu
from jax.sharding import PartitionSpec as P

HEAD_DIM = 64
BLK = 128
POOL = 16
SIDE = 8
LOG2E = 1.4426950408889634
STAT = 16

GROUP_Z = [[g * SIDE + i for i in range(SIDE)] for g in range(SIDE)]
GROUP_YX = [[g * SIDE + i for g in range(SIDE)] for i in range(SIDE)]


def spread(x, groups):
    wide = jnp.broadcast_to(x[None], (SIDE, *x.shape))
    return lax.all_to_all(wide, "seq", 0, 0, axis_index_groups=groups)


def attend_kernel(q_ref, k_ref, v_ref, o_ref, k_own, v_own):
    rows = q_ref.shape[0]
    lane = lax.broadcasted_iota(jnp.int32, (1, 128), 1)
    first = lane < HEAD_DIM

    @pl.when(pl.program_id(1) == 0)
    def _():
        zero = jnp.zeros((), jnp.bfloat16)
        one = jnp.ones((), jnp.bfloat16)
        k = k_ref[...]
        v = v_ref[...]
        k_own[0] = jnp.where(first, k, zero)
        k_own[1] = jnp.where(first, zero, k)
        v_own[0] = jnp.where(first, v, one)
        v_own[1] = jnp.where(first, one, v)

    scale = LOG2E * HEAD_DIM ** (-0.5)
    q = q_ref[...]
    tops, sums = [], []
    for h in range(2):
        s = lax.dot_general(
            q, k_own[h], (((1,), (1,)), ((), ())), preferred_element_type=jnp.float32
        )
        top = jnp.max(s, axis=1, keepdims=True)
        p = jnp.exp2((s - top) * scale).astype(jnp.bfloat16)
        sums.append(jnp.dot(p, v_own[h], preferred_element_type=jnp.float32))
        tops.append(top * scale)
    num = jnp.where(first, sums[0], sums[1])
    den_other = jnp.where(first, sums[1], sums[0])
    den = pltpu.roll(den_other, HEAD_DIM, 1)
    o_ref[0, :rows] = (num / den).astype(jnp.bfloat16)
    lse = jnp.where(first, tops[1], tops[0]) + jnp.log2(den_other)
    turned = lse.T
    left = jnp.concatenate([turned[HEAD_DIM : HEAD_DIM + 1], turned[0:1]], axis=0)
    left = jnp.concatenate([left[:, :128], left[:, 128:]], axis=0)
    hi = left.astype(jnp.bfloat16)
    rest = left - hi.astype(jnp.float32)
    mid = rest.astype(jnp.bfloat16)
    rest = rest - mid.astype(jnp.float32)
    pad = jnp.zeros_like(left)
    o_ref[0, rows:] = jnp.concatenate(
        [hi.astype(jnp.float32), mid.astype(jnp.float32), rest, pad], axis=0
    ).astype(jnp.bfloat16)


def attend(queries, keys, values):
    n, width = queries.shape
    rows = n // SIDE
    keys_n = keys.shape[0]
    pairs = width // 128
    return pl.pallas_call(
        attend_kernel,
        grid=(pairs, SIDE),
        in_specs=[
            pl.BlockSpec((rows, 128), lambda p, i: (i, p)),
            pl.BlockSpec((keys_n, 128), lambda p, i: (0, p)),
            pl.BlockSpec((keys_n, 128), lambda p, i: (0, p)),
        ],
        out_specs=pl.BlockSpec((1, rows + STAT, 128), lambda p, i: (i, 0, p)),
        out_shape=jax.ShapeDtypeStruct((SIDE, rows + STAT, width), jnp.bfloat16),
        scratch_shapes=[
            pltpu.VMEM((2, keys_n, 128), jnp.bfloat16),
            pltpu.VMEM((2, keys_n, 128), jnp.bfloat16),
        ],
        compiler_params=pltpu.CompilerParams(vmem_limit_bytes=40 * 1024 * 1024),
        name="attend",
    )(queries, keys, values)


def merge_kernel(part_ref, residual_ref, sel_ref, out_ref):
    rows, width = residual_ref.shape
    heads = width // HEAD_DIM
    stats = part_ref[:, rows:, :].astype(jnp.float32)
    merged = stats[:, 0:4] + stats[:, 4:8] + stats[:, 8:12]
    per_head = []
    for p in range(heads // 2):
        cols = slice(p * 128, p * 128 + 128)
        for h in range(2):
            per_head.append(
                jnp.concatenate([merged[:, h, cols], merged[:, 2 + h, cols]], axis=1)
            )
    scaled = []
    for x in per_head:
        w = jnp.exp2(x - jnp.max(x, axis=0, keepdims=True))
        scaled.append(w / jnp.sum(w, axis=0, keepdims=True))
    weights = jnp.concatenate(scaled, axis=0)
    weights = jnp.concatenate(
        [weights, jnp.zeros((128 - weights.shape[0], rows), jnp.float32)], axis=0
    ).T
    lane = lax.broadcasted_iota(jnp.int32, (1, 128), 1)
    first = lane < HEAD_DIM
    streams = []
    for p in range(heads // 2):
        cols = slice(p * 128, p * 128 + 128)
        total = jnp.zeros((rows, 128), jnp.float32)
        for j in range(SIDE):
            a = (2 * p) * SIDE + j
            b = (2 * p + 1) * SIDE + j
            w = jnp.where(first, weights[:, a : a + 1], weights[:, b : b + 1])
            total = total + w * part_ref[j, :rows, cols].astype(jnp.float32)
        context = total.astype(jnp.bfloat16).astype(jnp.float32)
        streams.append(
            (residual_ref[:, cols].astype(jnp.float32) + context).astype(jnp.bfloat16)
        )
    streams.append(jnp.ones((rows, 128), jnp.bfloat16))
    stream = jnp.concatenate(streams, axis=1)
    out_ref[...] = jnp.dot(sel_ref[...], stream, preferred_element_type=jnp.float32).astype(
        jnp.bfloat16
    )


def merge(parts, residual, sel):
    rows, width = residual.shape
    return pl.pallas_call(
        merge_kernel,
        out_shape=jax.ShapeDtypeStruct((sel.shape[0], width + 128), jnp.bfloat16),
        compiler_params=pltpu.CompilerParams(vmem_limit_bytes=40 * 1024 * 1024),
        name="merge",
    )(parts, residual, sel)


def local(queries, keys, values, residual, reg_weight, targets, block_track, row_count, pool_slot):
    tok_rows, width = queries.shape
    here = tok_rows // BLK
    seq_count = lax.axis_size("seq")
    head_count = lax.axis_size("head")
    seq_index = lax.axis_index("seq")
    head_index = lax.axis_index("head")
    blocks = here * seq_count
    target_d = reg_weight.shape[1]
    chunk = target_d // seq_count
    quarter = target_d // head_count
    chunks_per_quarter = quarter // chunk

    target_part = lax.dynamic_slice_in_dim(targets, head_index * quarter, quarter, axis=2)
    every_target = lax.all_gather(target_part, "seq", axis=0, tiled=True)

    query_all = spread(queries, GROUP_Z).reshape(SIDE * tok_rows, width)
    pair = spread(jnp.stack([keys, values]), GROUP_YX)
    key_all = pair[:, 0].reshape(SIDE * tok_rows, width)
    value_all = pair[:, 1].reshape(SIDE * tok_rows, width)
    parts = attend(query_all, key_all, value_all)
    parts = lax.all_to_all(parts, "seq", 0, 0, axis_index_groups=GROUP_Z)

    valid = jnp.arange(BLK, dtype=jnp.int32)[None, :] < row_count[:, None]
    match = pool_slot[:, None, :] == jnp.arange(POOL, dtype=jnp.int32)[None, :, None]
    sel = match & valid[:, None, :]
    same_block = jnp.arange(here)[:, None] == jnp.arange(here)[None, :]
    selector = (
        jnp.where(sel[:, :, None, :] & same_block[:, None, :, None], 1.0, 0.0)
        .astype(jnp.bfloat16)
        .reshape(here * POOL, tok_rows)
    )
    pooled = merge(parts, residual, selector)

    every = spread(spread(pooled, GROUP_Z), GROUP_YX).reshape(blocks, POOL, width + 128)
    same = block_track[:, None] == block_track[None, :]
    same_track = jnp.where(same, 1.0, 0.0).astype(jnp.bfloat16)
    sums = jnp.einsum("ab,bpc->apc", same_track, every, preferred_element_type=jnp.float32)
    divisor = jnp.maximum(sums[:, :, width : width + 1], 1.0)
    mean = (sums[:, :, :width] / divisor).astype(jnp.bfloat16)
    earlier = jnp.arange(blocks)[None, :] < jnp.arange(blocks)[:, None]
    leader = ~jnp.any(same & earlier, axis=1)

    block_start = seq_index * here
    own_track = lax.dynamic_slice_in_dim(block_track, block_start, here)
    own_mean = lax.dynamic_slice_in_dim(mean, block_start, here, axis=0).reshape(here * POOL, width)
    own_divisor = lax.dynamic_slice_in_dim(divisor, block_start, here, axis=0).reshape(
        here * POOL, 1
    )
    own_target = jnp.concatenate(
        [lax.dynamic_slice_in_dim(every_target, own_track[b], 1, axis=0) for b in range(here)]
    ).reshape(here * POOL, quarter)
    weight_groups = reg_weight.reshape(width, head_count, quarter)
    own_part = jnp.einsum(
        "rc,cgn->grn", own_mean, weight_groups, preferred_element_type=jnp.float32
    )
    mine = jnp.arange(head_count)[:, None, None] == head_index
    own_part = own_part - jnp.where(mine, own_target[None].astype(jnp.float32), 0.0)
    own_part = own_part.astype(jnp.bfloat16).reshape(head_count * here * POOL, quarter)

    chunk_weight = lax.dynamic_slice_in_dim(reg_weight, seq_index * chunk, chunk, axis=1)
    mean_groups = mean.reshape(SIDE, blocks * POOL // SIDE, width)
    chunk_part = jnp.einsum(
        "cn,grc->gnr", chunk_weight, mean_groups, preferred_element_type=jnp.float32
    )
    chunk_home = seq_index // chunks_per_quarter == head_index
    chunk_target = lax.dynamic_slice_in_dim(
        every_target, lax.rem(seq_index, chunks_per_quarter) * chunk, chunk, axis=2
    )
    track_of = block_track[:, None] == jnp.arange(targets.shape[0] * seq_count)[None, :]
    chunk_target = jnp.einsum(
        "bt,tpn->bpn", jnp.where(track_of, 1.0, 0.0).astype(jnp.bfloat16), chunk_target
    ).reshape(SIDE, blocks * POOL // SIDE, chunk)
    chunk_part = chunk_part - jnp.where(
        chunk_home, chunk_target.transpose(0, 2, 1).astype(jnp.float32), 0.0
    )
    chunk_part = chunk_part.astype(jnp.bfloat16).reshape(SIDE * chunk, blocks * POOL // SIDE)

    both = jnp.concatenate([own_part, chunk_part], axis=0)
    both = lax.all_to_all(
        jnp.broadcast_to(both[None], (head_count, *both.shape)), "head", 0, 0
    )
    error = jnp.sum(both.astype(jnp.float32), axis=0).astype(jnp.bfloat16)
    own_error = error[: own_part.shape[0]].reshape(head_count, here * POOL, quarter)
    chunk_error = error[own_part.shape[0] :].reshape(chunk_part.shape).reshape(
        SIDE, chunk, blocks * POOL // SIDE
    )

    counted = jnp.where(leader[:, None, None], mean, jnp.zeros((), jnp.bfloat16)).reshape(
        SIDE, blocks * POOL // SIDE, width
    )
    grad_chunk = jnp.einsum(
        "gnr,grc->nc", chunk_error, counted, preferred_element_type=jnp.float32
    ).astype(jnp.bfloat16)
    grad_turned = spread(spread(grad_chunk, GROUP_Z), GROUP_YX).reshape(target_d, width)
    grad_reg = grad_turned.T

    mean_grad = jnp.einsum(
        "grn,cgn->rc", own_error, weight_groups, preferred_element_type=jnp.float32
    )
    track_grad = (mean_grad / own_divisor).astype(jnp.bfloat16)
    context_grad = lax.dot_general(
        selector, track_grad, (((0,), (0,)), ((), ())), preferred_element_type=jnp.float32
    ).astype(jnp.bfloat16)
    return (grad_reg, context_grad)


def solution(mesh):
    return jax.shard_map(
        local,
        mesh=mesh,
        in_specs=(
            P("seq", "head"),
            P("seq", "head"),
            P("seq", "head"),
            P("seq", "head"),
            P("head", None),
            P("seq", None, None),
            P(),
            P("seq"),
            P("seq", None),
        ),
        out_specs=(P("head", None), P("seq", "head")),
        check_vma=False,
    )
```

```python
import jax
import jax.numpy as jnp
from jax import lax
from jax.experimental import pallas as pl
from jax.experimental.pallas import tpu as pltpu
from jax.sharding import PartitionSpec as P

HEAD_DIM = 64
BLK = 128
POOL = 16
SIDE = 8
LOG2E = 1.4426950408889634
STAT = 16

GROUP_Z = [[g * SIDE + i for i in range(SIDE)] for g in range(SIDE)]
GROUP_YX = [[g * SIDE + i for g in range(SIDE)] for i in range(SIDE)]


def spread(x, groups):
    wide = jnp.broadcast_to(x[None], (SIDE, *x.shape))
    return lax.all_to_all(wide, "seq", 0, 0, axis_index_groups=groups)


def shift(seq_count, dg):
    dy, dx = dg // 4, dg % 4
    pairs = []
    for g in range(seq_count // SIDE):
        to = (g // 4 + dy) % 2 * 4 + (g % 4 + dx) % 4
        pairs += [(g * SIDE + i, to * SIDE + i) for i in range(SIDE)]
    return pairs


def attend_kernel(q_ref, *refs):
    kv_refs, (o_ref, k_own, v_own) = refs[:-3], refs[-3:]
    rows = q_ref.shape[0]
    lane = lax.broadcasted_iota(jnp.int32, (1, 128), 1)
    first = lane < HEAD_DIM

    @pl.when(pl.program_id(0) == 0)
    def _():
        zero = jnp.zeros((), jnp.bfloat16)
        one = jnp.ones((), jnp.bfloat16)
        for i, kv_ref in enumerate(kv_refs):
            n = kv_ref.shape[0] // 2
            span = pl.ds(i * n, n)
            k = kv_ref[:n]
            v = kv_ref[n:]
            k_own[0, span] = jnp.where(first, k, zero)
            k_own[1, span] = jnp.where(first, zero, k)
            v_own[0, span] = jnp.where(first, v, one)
            v_own[1, span] = jnp.where(first, one, v)

    scale = LOG2E * HEAD_DIM ** (-0.5)
    q = q_ref[...]
    tops, sums = [], []
    for h in range(2):
        s = lax.dot_general(
            q, k_own[h], (((1,), (1,)), ((), ())), preferred_element_type=jnp.float32
        )
        top = jnp.max(s, axis=1, keepdims=True)
        p = jnp.exp2((s - top) * scale).astype(jnp.bfloat16)
        sums.append(jnp.dot(p, v_own[h], preferred_element_type=jnp.float32))
        tops.append(top * scale)
    num = jnp.where(first, sums[0], sums[1])
    den_other = jnp.where(first, sums[1], sums[0])
    den = pltpu.roll(den_other, HEAD_DIM, 1)
    o_ref[0, :rows] = (num / den).astype(jnp.bfloat16)
    lse = jnp.where(first, tops[1], tops[0]) + jnp.log2(den_other)
    turned = lse.T
    left = jnp.concatenate([turned[HEAD_DIM : HEAD_DIM + 1], turned[0:1]], axis=0)
    left = jnp.concatenate([left[:, :128], left[:, 128:]], axis=0)
    hi = left.astype(jnp.bfloat16)
    rest = left - hi.astype(jnp.float32)
    mid = rest.astype(jnp.bfloat16)
    rest = rest - mid.astype(jnp.float32)
    pad = jnp.zeros_like(left)
    o_ref[0, rows:] = jnp.concatenate(
        [hi.astype(jnp.float32), mid.astype(jnp.float32), rest, pad], axis=0
    ).astype(jnp.bfloat16)


def attend(queries, pieces, pair):
    n = queries.shape[0]
    rows = n // SIDE
    keys_n = sum(x.shape[0] for x in pieces) // 2
    return pl.pallas_call(
        attend_kernel,
        grid=(SIDE,),
        in_specs=[pl.BlockSpec((rows, 128), lambda i: (i, pair))]
        + [pl.BlockSpec((x.shape[0], 128), lambda i: (0, pair)) for x in pieces],
        out_specs=pl.BlockSpec((1, rows + STAT, 128), lambda i: (i, 0, 0)),
        out_shape=jax.ShapeDtypeStruct((SIDE, rows + STAT, 128), jnp.bfloat16),
        scratch_shapes=[
            pltpu.VMEM((2, keys_n, 128), jnp.bfloat16),
            pltpu.VMEM((2, keys_n, 128), jnp.bfloat16),
        ],
        compiler_params=pltpu.CompilerParams(vmem_limit_bytes=40 * 1024 * 1024),
        cost_estimate=pl.CostEstimate(
            flops=2 * 2 * 2 * n * keys_n * 256,
            bytes_accessed=8 * n * 128,
            transcendentals=2 * n * keys_n,
        ),
        name="attend",
    )(queries, *pieces)


def merge_kernel(*refs):
    part_refs, (residual_ref, sel_ref, out_ref) = refs[:-3], refs[-3:]
    rows = residual_ref.shape[0]
    lane = lax.broadcasted_iota(jnp.int32, (1, 128), 1)
    first = lane < HEAD_DIM
    scaled = []
    for part_ref in part_refs:
        stats = part_ref[:, rows:, :].astype(jnp.float32)
        merged = stats[:, 0:4] + stats[:, 4:8] + stats[:, 8:12]
        for h in range(2):
            x = jnp.concatenate([merged[:, h], merged[:, 2 + h]], axis=1)
            w = jnp.exp2(x - jnp.max(x, axis=0, keepdims=True))
            scaled.append(w / jnp.sum(w, axis=0, keepdims=True))
    weights = jnp.concatenate(scaled, axis=0)
    weights = jnp.concatenate(
        [weights, jnp.zeros((128 - weights.shape[0], rows), jnp.float32)], axis=0
    ).T
    streams = []
    for p, part_ref in enumerate(part_refs):
        cols = slice(p * 128, p * 128 + 128)
        total = jnp.zeros((rows, 128), jnp.float32)
        for j in range(SIDE):
            a = (2 * p) * SIDE + j
            b = (2 * p + 1) * SIDE + j
            w = jnp.where(first, weights[:, a : a + 1], weights[:, b : b + 1])
            total = total + w * part_ref[j, :rows].astype(jnp.float32)
        context = total.astype(jnp.bfloat16).astype(jnp.float32)
        streams.append(
            (residual_ref[:, cols].astype(jnp.float32) + context).astype(jnp.bfloat16)
        )
    stream = jnp.concatenate(streams, axis=1)
    out_ref[...] = jnp.dot(sel_ref[...], stream, preferred_element_type=jnp.float32).astype(
        jnp.bfloat16
    )


def merge(parts, residual, sel):
    return pl.pallas_call(
        merge_kernel,
        out_shape=jax.ShapeDtypeStruct((sel.shape[0], residual.shape[1]), jnp.bfloat16),
        compiler_params=pltpu.CompilerParams(vmem_limit_bytes=40 * 1024 * 1024),
        name="merge",
    )(*parts, residual, sel)


def track_kernel(id_col_ref, id_row_ref, every_ref, divisor_ref, weight_ref, mean_ref, part_ref):
    match = jnp.where(id_col_ref[...] == id_row_ref[...], 1.0, 0.0).astype(jnp.bfloat16)
    sums = jnp.dot(match, every_ref[...], preferred_element_type=jnp.float32)
    mean = (sums / divisor_ref[...]).astype(jnp.bfloat16)
    mean_ref[...] = mean
    part = lax.dot_general(
        weight_ref[...], mean, (((1,), (1,)), ((), ())), preferred_element_type=jnp.float32
    ).astype(jnp.bfloat16)
    for h in range(part_ref.shape[0]):
        part_ref[h] = part


def track_means(ids, every, divisor, weight, head_count):
    rows, width = every.shape
    chunk = weight.shape[0]
    step = rows // SIDE
    return pl.pallas_call(
        track_kernel,
        grid=(SIDE,),
        in_specs=[
            pl.BlockSpec((step, 1), lambda i: (i, 0)),
            pl.BlockSpec((1, rows), lambda i: (0, 0)),
            pl.BlockSpec((rows, width), lambda i: (0, 0)),
            pl.BlockSpec((step, 1), lambda i: (i, 0)),
            pl.BlockSpec((chunk, width), lambda i: (0, 0)),
        ],
        out_specs=[
            pl.BlockSpec((step, width), lambda i: (i, 0)),
            pl.BlockSpec((head_count, chunk, step), lambda i: (0, 0, i)),
        ],
        out_shape=[
            jax.ShapeDtypeStruct((rows, width), jnp.bfloat16),
            jax.ShapeDtypeStruct((head_count, chunk, rows), jnp.bfloat16),
        ],
        compiler_params=pltpu.CompilerParams(vmem_limit_bytes=40 * 1024 * 1024),
        name="track_means",
    )(ids.reshape(rows, 1), ids.reshape(1, rows), every, divisor, weight)


def error_kernel(part_ref, target_ref, leader_ref, mean_ref, out_ref):
    back = part_ref.shape[2] // out_ref.shape[0]
    width = mean_ref.shape[1]
    total = part_ref[0].astype(jnp.float32)
    for h in range(1, part_ref.shape[0]):
        total = total + part_ref[h].astype(jnp.float32)
    error = (total - target_ref[...]).astype(jnp.bfloat16).astype(jnp.float32)
    grad = jnp.dot(
        (error * leader_ref[...]).astype(jnp.bfloat16),
        mean_ref[...],
        preferred_element_type=jnp.float32,
    ).astype(jnp.bfloat16)
    per = 128 // back
    for s in range(out_ref.shape[0]):
        tile = error[:, s // per * 128 : s // per * 128 + 128]
        turn = s % per * back
        rows = pltpu.roll(tile, 128 - turn, 1) if turn else tile
        out_ref[s, :, :width] = grad
        out_ref[s, :, width:] = rows.astype(jnp.bfloat16)


def error_messages(partial, target, leader, mean, seq_count):
    chunk = partial.shape[1]
    return pl.pallas_call(
        error_kernel,
        out_shape=jax.ShapeDtypeStruct((seq_count, chunk, mean.shape[1] + 128), jnp.bfloat16),
        compiler_params=pltpu.CompilerParams(vmem_limit_bytes=40 * 1024 * 1024),
        name="error_messages",
    )(partial, target, leader, mean)


def local(queries, keys, values, residual, reg_weight, targets, block_track, row_count, pool_slot):
    tok_rows, width = queries.shape
    here = tok_rows // BLK
    seq_count = lax.axis_size("seq")
    head_count = lax.axis_size("head")
    seq_index = lax.axis_index("seq")
    blocks = here * seq_count
    target_d = reg_weight.shape[1]
    chunk = target_d // seq_count
    owned = targets.shape[0]
    tracks = owned * seq_count

    own_kv = jnp.concatenate([keys, values], axis=0)
    pieces = [own_kv] + [
        lax.ppermute(own_kv, "seq", shift(seq_count, d)) for d in (6, 5, 7, 2, 4, 1, 3)
    ]
    query_all = spread(queries, GROUP_Z).reshape(SIDE * tok_rows, width)

    valid = jnp.arange(BLK, dtype=jnp.int32)[None, :] < row_count[:, None]
    match = pool_slot[:, None, :] == jnp.arange(POOL, dtype=jnp.int32)[None, :, None]
    sel = match & valid[:, None, :]
    same_block = jnp.arange(here)[:, None] == jnp.arange(here)[None, :]
    selector = (
        jnp.where(sel[:, :, None, :] & same_block[:, None, :, None], 1.0, 0.0)
        .astype(jnp.bfloat16)
        .reshape(here * POOL, tok_rows)
    )
    slot_rows = jnp.sum(jnp.where(sel, 1.0, 0.0), axis=2).astype(jnp.bfloat16)
    turned = targets.reshape(owned * POOL, target_d).T.reshape(seq_count, chunk, owned * POOL)
    extra = jnp.concatenate(
        [slot_rows.T, jnp.zeros((POOL, 128 - owned * POOL - here), jnp.bfloat16)], axis=1
    )
    early = jnp.concatenate(
        [turned, jnp.broadcast_to(extra[None], (seq_count, *extra.shape))], axis=2
    )
    early, query_all = lax.optimization_barrier((early, query_all))
    early = lax.all_to_all(early, "seq", 0, 0)

    parts = []
    for pair in range(width // 128):
        part = attend(query_all, pieces, pair)
        if pair == 0:
            early, part = lax.optimization_barrier((early, part))
        parts.append(lax.all_to_all(part, "seq", 0, 0, axis_index_groups=GROUP_Z))

    same = block_track[:, None] == block_track[None, :]
    same_track = jnp.where(same, 1.0, 0.0).astype(jnp.bfloat16)
    earlier = jnp.arange(blocks)[None, :] < jnp.arange(blocks)[:, None]
    leader = jnp.where(jnp.any(same & earlier, axis=1), 0.0, 1.0)
    leader = jnp.repeat(leader, POOL).reshape(1, blocks * POOL)
    ids = (
        block_track[:, None] * POOL + jnp.arange(POOL, dtype=jnp.int32)[None, :]
    ).reshape(blocks * POOL)
    every_count = (
        early[:, :, owned * POOL : owned * POOL + here].transpose(0, 2, 1).reshape(blocks, POOL)
    )
    counts = jnp.dot(same_track, every_count, preferred_element_type=jnp.float32)
    divisor = jnp.maximum(counts, 1.0)
    track_of = block_track[:, None] == jnp.arange(tracks, dtype=jnp.int32)[None, :]
    track_of = jnp.where(track_of, 1.0, 0.0).astype(jnp.bfloat16)
    chunk_target = (
        early[:, :, : owned * POOL]
        .reshape(seq_count, chunk, owned, POOL)
        .transpose(1, 0, 2, 3)
        .reshape(chunk, tracks, POOL)
    )
    chunk_target = jnp.einsum(
        "bt,ntp->nbp", track_of, chunk_target, preferred_element_type=jnp.float32
    ).reshape(chunk, blocks * POOL)
    rows_divisor = divisor.reshape(blocks * POOL, 1)
    chunk_weight = lax.dynamic_slice_in_dim(reg_weight, seq_index * chunk, chunk, axis=1).T
    own_divisor = lax.dynamic_slice_in_dim(divisor, seq_index * here, here, axis=0).reshape(
        here * POOL, 1
    )

    pooled = merge(parts, residual, selector)
    chunk_target, rows_divisor, leader, ids, chunk_weight, own_divisor, pooled = (
        lax.optimization_barrier(
            (chunk_target, rows_divisor, leader, ids, chunk_weight, own_divisor, pooled)
        )
    )
    every = spread(spread(pooled, GROUP_Z), GROUP_YX).reshape(blocks * POOL, width)
    mean, partial = track_means(ids, every, rows_divisor, chunk_weight, head_count)
    partial = lax.all_to_all(partial, "head", 0, 0)
    back = here * POOL
    final = error_messages(partial, chunk_target, leader, mean, seq_count)
    final = lax.all_to_all(final, "seq", 0, 0).reshape(target_d, width + 128)
    grad_reg = final[:, :width].T
    mean_grad = lax.dot_general(
        final[:, width : width + back],
        reg_weight,
        (((0,), (1,)), ((), ())),
        preferred_element_type=jnp.float32,
    )
    track_grad = (mean_grad / own_divisor).astype(jnp.bfloat16)
    context_grad = lax.dot_general(
        selector, track_grad, (((0,), (0,)), ((), ())), preferred_element_type=jnp.float32
    ).astype(jnp.bfloat16)
    return (grad_reg, context_grad)


def solution(mesh):
    return jax.shard_map(
        local,
        mesh=mesh,
        in_specs=(
            P("seq", "head"),
            P("seq", "head"),
            P("seq", "head"),
            P("seq", "head"),
            P("head", None),
            P("seq", None, None),
            P(),
            P("seq"),
            P("seq", None),
        ),
        out_specs=(P("head", None), P("seq", "head")),
        check_vma=False,
    )
```

```python
import functools

import jax
import jax.numpy as jnp
from jax import lax
from jax.experimental import pallas as pl
from jax.experimental.pallas import tpu as pltpu
from jax.sharding import PartitionSpec as P

HEAD_DIM = 64
BLK = 128
POOL = 16
SIDE = 8
LOG2E = 1.4426950408889634
STAT = 16
VMEM_BYTES = 24 * 1024 * 1024

GROUP_Z = [[g * SIDE + i for i in range(SIDE)] for g in range(SIDE)]
GROUP_YX = [[g * SIDE + i for g in range(SIDE)] for i in range(SIDE)]


def spread(x, groups):
    wide = jnp.broadcast_to(x[None], (SIDE, *x.shape))
    return lax.all_to_all(wide, "seq", 0, 0, axis_index_groups=groups)


def shift(seq_count, dg):
    dy, dx = dg // 4, dg % 4
    pairs = []
    for g in range(seq_count // SIDE):
        to = (g // 4 + dy) % 2 * 4 + (g % 4 + dx) % 4
        pairs += [(g * SIDE + i, to * SIDE + i) for i in range(SIDE)]
    return pairs


def attend_kernel(riders, q_ref, *refs):
    extra_refs, kv_refs, (o_ref, k_own, v_own) = refs[:riders], refs[riders:-3], refs[-3:]
    rows = q_ref.shape[0]
    lane = lax.broadcasted_iota(jnp.int32, (1, 128), 1)
    first = lane < HEAD_DIM

    @pl.when(pl.program_id(0) == 0)
    def _():
        zero = jnp.zeros((), jnp.bfloat16)
        one = jnp.ones((), jnp.bfloat16)
        for i, kv_ref in enumerate(kv_refs):
            n = kv_ref.shape[0] // 2
            span = pl.ds(i * n, n)
            k = kv_ref[:n]
            v = kv_ref[n:]
            k_own[0, span] = jnp.where(first, k, zero)
            k_own[1, span] = jnp.where(first, zero, k)
            v_own[0, span] = jnp.where(first, v, one)
            v_own[1, span] = jnp.where(first, one, v)

    scale = LOG2E * HEAD_DIM ** (-0.5)
    q = q_ref[...]
    tops, sums = [], []
    for h in range(2):
        s = lax.dot_general(
            q, k_own[h], (((1,), (1,)), ((), ())), preferred_element_type=jnp.float32
        )
        top = jnp.max(s, axis=1, keepdims=True)
        p = jnp.exp2((s - top) * scale).astype(jnp.bfloat16)
        sums.append(jnp.dot(p, v_own[h], preferred_element_type=jnp.float32))
        tops.append(top * scale)
    num = jnp.where(first, sums[0], sums[1])
    den_other = jnp.where(first, sums[1], sums[0])
    den = pltpu.roll(den_other, HEAD_DIM, 1)
    o_ref[0, :rows] = (num / den).astype(jnp.bfloat16)
    lse = jnp.where(first, tops[1], tops[0]) + jnp.log2(den_other)
    turned = lse.T
    left = jnp.concatenate([turned[HEAD_DIM : HEAD_DIM + 1], turned[0:1]], axis=0)
    left = jnp.concatenate([left[:, :128], left[:, 128:]], axis=0)
    hi = left.astype(jnp.bfloat16)
    rest = left - hi.astype(jnp.float32)
    mid = rest.astype(jnp.bfloat16)
    rest = rest - mid.astype(jnp.float32)
    pad = jnp.zeros_like(left)
    if riders:
        piece_ref, count_ref = extra_refs
        pad = jnp.concatenate([count_ref[...], pad[1:]], axis=0)
        o_ref[0, rows + STAT :] = piece_ref[0]
    o_ref[0, rows : rows + STAT] = jnp.concatenate(
        [hi.astype(jnp.float32), mid.astype(jnp.float32), rest, pad], axis=0
    ).astype(jnp.bfloat16)


def attend(queries, pieces, pair, riders):
    n = queries.shape[0]
    rows = n // SIDE
    keys_n = sum(x.shape[0] for x in pieces) // 2
    out_rows = rows + STAT
    rider_specs = []
    if riders:
        rider_specs = [
            pl.BlockSpec((1, *riders[0].shape[1:]), lambda i: (i, 0, 0)),
            pl.BlockSpec(riders[1].shape, lambda i: (0, 0)),
        ]
        out_rows = out_rows + riders[0].shape[1]
    return pl.pallas_call(
        functools.partial(attend_kernel, len(riders)),
        grid=(SIDE,),
        in_specs=[pl.BlockSpec((rows, 128), lambda i: (i, pair))]
        + rider_specs
        + [pl.BlockSpec((x.shape[0], 128), lambda i: (0, pair)) for x in pieces],
        out_specs=pl.BlockSpec((1, out_rows, 128), lambda i: (i, 0, 0)),
        out_shape=jax.ShapeDtypeStruct((SIDE, out_rows, 128), jnp.bfloat16),
        scratch_shapes=[
            pltpu.VMEM((2, keys_n, 128), jnp.bfloat16),
            pltpu.VMEM((2, keys_n, 128), jnp.bfloat16),
        ],
        compiler_params=pltpu.CompilerParams(vmem_limit_bytes=VMEM_BYTES),
        cost_estimate=pl.CostEstimate(
            flops=2 * 2 * 2 * n * keys_n * 256,
            bytes_accessed=8 * n * 128,
            transcendentals=2 * n * keys_n,
        ),
        name="attend",
    )(queries, *riders, *pieces)


def merge_kernel(*refs):
    part_refs, (residual_ref, sel_ref, out_ref, rider_ref) = refs[:-4], refs[-4:]
    rows = residual_ref.shape[0]
    lane = lax.broadcasted_iota(jnp.int32, (1, 128), 1)
    first = lane < HEAD_DIM
    scaled = []
    for part_ref in part_refs:
        stats = part_ref[:, rows : rows + STAT, :].astype(jnp.float32)
        merged = stats[:, 0:4] + stats[:, 4:8] + stats[:, 8:12]
        for h in range(2):
            x = jnp.concatenate([merged[:, h], merged[:, 2 + h]], axis=1)
            w = jnp.exp2(x - jnp.max(x, axis=0, keepdims=True))
            scaled.append(w / jnp.sum(w, axis=0, keepdims=True))
    weights = jnp.concatenate(scaled, axis=0)
    weights = jnp.concatenate(
        [weights, jnp.zeros((128 - weights.shape[0], rows), jnp.float32)], axis=0
    ).T
    streams = []
    for p, part_ref in enumerate(part_refs):
        cols = slice(p * 128, p * 128 + 128)
        total = jnp.zeros((rows, 128), jnp.float32)
        for j in range(SIDE):
            a = (2 * p) * SIDE + j
            b = (2 * p + 1) * SIDE + j
            w = jnp.where(first, weights[:, a : a + 1], weights[:, b : b + 1])
            total = total + w * part_ref[j, :rows].astype(jnp.float32)
        context = total.astype(jnp.bfloat16).astype(jnp.float32)
        streams.append(
            (residual_ref[:, cols].astype(jnp.float32) + context).astype(jnp.bfloat16)
        )
    stream = jnp.concatenate(streams, axis=1)
    pooled = jnp.dot(sel_ref[...], stream, preferred_element_type=jnp.float32).astype(jnp.bfloat16)
    for j in range(SIDE):
        out_ref[j] = pooled

    carried = part_refs[0][:, rows + STAT :].astype(jnp.float32)
    counts = part_refs[0][:, rows : rows + STAT].astype(jnp.float32)[:, 12:13]
    back = sel_ref.shape[0]
    per = 128 // back
    count_tiles = []
    for half in range(SIDE // per):
        tile = jnp.zeros((1, 128), jnp.float32)
        for q in range(per):
            row = counts[half * per + q]
            row = pltpu.roll(row, q * back, 1) if q else row
            tile = jnp.where(lane // back == q, row, tile)
        count_tiles.append(tile)
    count_row = jnp.concatenate(count_tiles, axis=1)
    tail = jnp.concatenate([count_row, jnp.zeros((15, count_row.shape[1]), jnp.float32)], axis=0)
    for g in range(SIDE):
        span = slice(g * 8, g * 8 + 8)
        halves = [
            jnp.concatenate([carried[half * 4 + q, span] for q in range(4)], axis=0)
            for half in range(2)
        ]
        rider_ref[g] = jnp.concatenate(
            [jnp.concatenate(halves, axis=1), tail], axis=0
        ).astype(jnp.bfloat16)


def merge(parts, residual, sel):
    back, width = sel.shape[0], residual.shape[1]
    return pl.pallas_call(
        merge_kernel,
        out_shape=[
            jax.ShapeDtypeStruct((SIDE, back, width), jnp.bfloat16),
            jax.ShapeDtypeStruct((SIDE, 48, 256), jnp.bfloat16),
        ],
        compiler_params=pltpu.CompilerParams(vmem_limit_bytes=VMEM_BYTES),
        name="merge",
    )(*parts, residual, sel)


def column(row):
    return jnp.broadcast_to(row, (128, row.shape[1])).T[:, :1]


def track_kernel(ids_here_ref, ids_ref, every_ref, weight_ref, mean_ref, part_ref, divisor_ref):
    step = mean_ref.shape[0]
    here = column(ids_here_ref[...])
    sums = jnp.zeros(mean_ref.shape, jnp.float32)
    counts = jnp.zeros((step, step), jnp.float32)
    for g in range(SIDE):
        match = here == ids_ref[:, g * step : g * step + step]
        sums = sums + jnp.dot(
            jnp.where(match, 1.0, 0.0).astype(jnp.bfloat16),
            every_ref[g, :step],
            preferred_element_type=jnp.float32,
        )
        count_row = every_ref[g, step + 32 :].astype(jnp.float32)[:1]
        counts = counts + jnp.where(match, count_row, 0.0)
    divisor = jnp.maximum(jnp.sum(counts, axis=1, keepdims=True), 1.0)
    divisor_ref[...] = jnp.broadcast_to(divisor, divisor_ref.shape)
    mean = (sums / divisor).astype(jnp.bfloat16)
    mean_ref[...] = mean
    part = lax.dot_general(
        weight_ref[...], mean, (((1,), (1,)), ((), ())), preferred_element_type=jnp.float32
    ).astype(jnp.bfloat16)
    for h in range(part_ref.shape[0]):
        part_ref[h] = part


def track_means(ids, every, weight, head_count):
    width = every.shape[2]
    rows = ids.shape[1]
    chunk = weight.shape[0]
    step = rows // SIDE
    return pl.pallas_call(
        track_kernel,
        grid=(SIDE,),
        in_specs=[
            pl.BlockSpec((1, step), lambda i: (0, i)),
            pl.BlockSpec((1, rows), lambda i: (0, 0)),
            pl.BlockSpec(every.shape, lambda i: (0, 0, 0)),
            pl.BlockSpec((chunk, width), lambda i: (0, 0)),
        ],
        out_specs=[
            pl.BlockSpec((step, width), lambda i: (i, 0)),
            pl.BlockSpec((head_count, chunk, step), lambda i: (0, 0, i)),
            pl.BlockSpec((step, 128), lambda i: (i, 0)),
        ],
        out_shape=[
            jax.ShapeDtypeStruct((rows, width), jnp.bfloat16),
            jax.ShapeDtypeStruct((head_count, chunk, rows), jnp.bfloat16),
            jax.ShapeDtypeStruct((rows, 128), jnp.float32),
        ],
        compiler_params=pltpu.CompilerParams(vmem_limit_bytes=VMEM_BYTES),
        name="track_means",
    )(ids, ids, every, weight)


def error_kernel(track_ref, part_ref, every_ref, leader_ref, mean_ref, out_ref, target_buf):
    back = part_ref.shape[2] // out_ref.shape[0]
    width = mean_ref.shape[1]
    step = part_ref.shape[2] // SIDE
    for g in range(SIDE):
        carried = every_ref[g, step : step + 32].astype(jnp.float32)
        for z in range(SIDE):
            target_buf[g * SIDE + z] = carried[
                z % 4 * 8 : z % 4 * 8 + 8, z // 4 * 128 : z // 4 * 128 + 128
            ]
    lane = lax.broadcasted_iota(jnp.int32, (8, 128), 1)
    tiles = []
    for group in range(part_ref.shape[2] // 128):
        low = jnp.zeros((8, 128), jnp.float32)
        high = jnp.zeros((8, 128), jnp.float32)
        for j in range(8):
            track = track_ref[group * 8 + j]
            tile = target_buf[track // 4]
            turn = j * POOL + 128 - track % 4 * POOL
            here = lane // POOL == j
            low = jnp.where(here, pltpu.roll(tile, lax.rem(turn, 128), 1), low)
            high = jnp.where(here, pltpu.roll(tile, lax.rem(turn + 64, 128), 1), high)
        tiles.append(jnp.concatenate([low, high], axis=0))
    target = jnp.concatenate(tiles, axis=1)
    total = part_ref[0].astype(jnp.float32)
    for h in range(1, part_ref.shape[0]):
        total = total + part_ref[h].astype(jnp.float32)
    error = (total - target).astype(jnp.bfloat16).astype(jnp.float32)
    grad = jnp.dot(
        (error * leader_ref[...]).astype(jnp.bfloat16),
        mean_ref[...],
        preferred_element_type=jnp.float32,
    ).astype(jnp.bfloat16)
    per = 128 // back
    for s in range(out_ref.shape[0]):
        tile = error[:, s // per * 128 : s // per * 128 + 128]
        turn = s % per * back
        rows = pltpu.roll(tile, 128 - turn, 1) if turn else tile
        out_ref[s, :, :width] = grad
        out_ref[s, :, width:] = rows.astype(jnp.bfloat16)


def error_messages(tracks, partial, every, leader, mean, seq_count):
    chunk = partial.shape[1]
    vmem = pl.BlockSpec(memory_space=pltpu.VMEM)
    return pl.pallas_call(
        error_kernel,
        in_specs=[pl.BlockSpec(memory_space=pltpu.SMEM), vmem, vmem, vmem, vmem],
        out_shape=jax.ShapeDtypeStruct((seq_count, chunk, mean.shape[1] + 128), jnp.bfloat16),
        scratch_shapes=[pltpu.VMEM((seq_count, 8, 128), jnp.float32)],
        compiler_params=pltpu.CompilerParams(vmem_limit_bytes=VMEM_BYTES),
        name="error_messages",
    )(tracks, partial, every, leader, mean)


def finish_kernel(index_ref, final_ref, weight_ref, sel_ref, divisor_ref, grad_ref, context_ref):
    width = weight_ref.shape[0]
    back = sel_ref.shape[0]
    for i in range(final_ref.shape[0] // width):
        span = slice(i * width, i * width + width)
        grad_ref[:, span] = final_ref[span, :width].T
    mean_grad = jnp.dot(
        weight_ref[...], final_ref[:, width:], preferred_element_type=jnp.float32
    ).T[:back]
    track_grad = (mean_grad / divisor_ref[:, :1]).astype(jnp.bfloat16)
    context_ref[...] = lax.dot_general(
        sel_ref[...], track_grad, (((0,), (0,)), ((), ())), preferred_element_type=jnp.float32
    ).astype(jnp.bfloat16)


def finish(index, final, weight, sel, divisor):
    width, target_d = weight.shape
    back, tok_rows = sel.shape
    whole = lambda *shape: pl.BlockSpec(shape, lambda i, at: (0, 0))
    return pl.pallas_call(
        finish_kernel,
        grid_spec=pltpu.PrefetchScalarGridSpec(
            num_scalar_prefetch=1,
            grid=(1,),
            in_specs=[
                whole(*final.shape),
                whole(*weight.shape),
                whole(*sel.shape),
                pl.BlockSpec((back, 128), lambda i, at: (at[0], 0)),
            ],
            out_specs=[whole(width, target_d), whole(tok_rows, width)],
        ),
        out_shape=[
            jax.ShapeDtypeStruct((width, target_d), jnp.bfloat16),
            jax.ShapeDtypeStruct((tok_rows, width), jnp.bfloat16),
        ],
        compiler_params=pltpu.CompilerParams(vmem_limit_bytes=VMEM_BYTES),
        name="finish",
    )(index.reshape(1).astype(jnp.int32), final, weight, sel, divisor)


def local(queries, keys, values, residual, reg_weight, targets, block_track, row_count, pool_slot):
    tok_rows, width = queries.shape
    here = tok_rows // BLK
    seq_count = lax.axis_size("seq")
    head_count = lax.axis_size("head")
    seq_index = lax.axis_index("seq")
    blocks = here * seq_count
    target_d = reg_weight.shape[1]
    chunk = target_d // seq_count
    owned = targets.shape[0]

    own_kv = jnp.concatenate([keys, values], axis=0)
    pieces = [own_kv] + [
        lax.ppermute(own_kv, "seq", shift(seq_count, d)) for d in (6, 5, 7, 2, 4, 1, 3)
    ]
    query_all = spread(queries, GROUP_Z).reshape(SIDE * tok_rows, width)

    valid = jnp.arange(BLK, dtype=jnp.int32)[None, :] < row_count[:, None]
    match = pool_slot[:, None, :] == jnp.arange(POOL, dtype=jnp.int32)[None, :, None]
    sel = match & valid[:, None, :]
    same_block = jnp.arange(here)[:, None] == jnp.arange(here)[None, :]
    selector = (
        jnp.where(sel[:, :, None, :] & same_block[:, None, :, None], 1.0, 0.0)
        .astype(jnp.bfloat16)
        .reshape(here * POOL, tok_rows)
    )
    slot_rows = jnp.sum(jnp.where(sel, 1.0, 0.0), axis=2).reshape(1, here * POOL)
    slot_rows = jnp.pad(slot_rows, ((0, 0), (0, 128 - here * POOL)))
    turned = targets.reshape(owned * POOL, target_d).T
    turned = turned.reshape(SIDE, SIDE, 2, chunk // 2, owned * POOL).transpose(1, 0, 2, 3, 4)
    carried = jnp.concatenate([turned[:, :, 0], turned[:, :, 1]], axis=3)
    carried = carried.reshape(SIDE, SIDE * chunk // 2, 128)
    same = block_track[:, None] == block_track[None, :]
    earlier = jnp.arange(blocks)[None, :] < jnp.arange(blocks)[:, None]
    leader = jnp.where(jnp.any(same & earlier, axis=1), 0.0, 1.0)
    leader = jnp.repeat(leader, POOL).reshape(1, blocks * POOL)
    ids = (
        (block_track[:, None] * POOL + jnp.arange(POOL, dtype=jnp.int32)[None, :])
        .reshape(1, blocks * POOL)
        .astype(jnp.float32)
    )
    chunk_weight = lax.dynamic_slice_in_dim(reg_weight, seq_index * chunk, chunk, axis=1).T

    part = attend(query_all, pieces, 0, (carried, slot_rows))
    part, query_all, selector, leader, ids, chunk_weight = lax.optimization_barrier(
        (part, query_all, selector, leader, ids, chunk_weight)
    )
    parts = [lax.all_to_all(part, "seq", 0, 0, axis_index_groups=GROUP_Z)]
    for pair in range(1, width // 128):
        part = attend(query_all, pieces, pair, ())
        parts[-1], part = lax.optimization_barrier((parts[-1], part))
        parts.append(lax.all_to_all(part, "seq", 0, 0, axis_index_groups=GROUP_Z))

    pooled, rider = merge(parts, residual, selector)
    pooled = lax.all_to_all(pooled, "seq", 0, 0, axis_index_groups=GROUP_Z)
    pooled = pooled.reshape(1, blocks * POOL // SIDE, width)
    every = jnp.concatenate(
        [jnp.broadcast_to(pooled, (SIDE, *pooled.shape[1:])), rider], axis=1
    )
    every = lax.all_to_all(every, "seq", 0, 0, axis_index_groups=GROUP_YX)
    mean, partial, divisor = track_means(ids, every, chunk_weight, head_count)
    partial = lax.all_to_all(partial, "head", 0, 0)
    final = error_messages(block_track, partial, every, leader, mean, seq_count)
    final = lax.all_to_all(final, "seq", 0, 0).reshape(target_d, width + 128)
    return finish(seq_index, final, reg_weight, selector, divisor)


def solution(mesh):
    return jax.shard_map(
        local,
        mesh=mesh,
        in_specs=(
            P("seq", "head"),
            P("seq", "head"),
            P("seq", "head"),
            P("seq", "head"),
            P("head", None),
            P("seq", None, None),
            P(),
            P("seq"),
            P("seq", None),
        ),
        out_specs=(P("head", None), P("seq", "head")),
        check_vma=False,
    )
```

```python
import functools

import jax
import jax.numpy as jnp
from jax import lax
from jax.experimental import pallas as pl
from jax.experimental.pallas import tpu as pltpu
from jax.sharding import PartitionSpec as P

HEAD_DIM = 64
BLK = 128
POOL = 16
SIDE = 8
LOG2E = 1.4426950408889634
STAT = 16
VMEM_BYTES = 24 * 1024 * 1024

GROUP_Z = [[g * SIDE + i for i in range(SIDE)] for g in range(SIDE)]
GROUP_YX = [[g * SIDE + i for g in range(SIDE)] for i in range(SIDE)]


def spread(x, groups):
    wide = jnp.broadcast_to(x[None], (SIDE, *x.shape))
    return lax.all_to_all(wide, "seq", 0, 0, axis_index_groups=groups)


def shift(seq_count, dg):
    dy, dx = dg // 4, dg % 4
    pairs = []
    for g in range(seq_count // SIDE):
        to = (g // 4 + dy) % 2 * 4 + (g % 4 + dx) % 4
        pairs += [(g * SIDE + i, to * SIDE + i) for i in range(SIDE)]
    return pairs


def attend_kernel(q_ref, piece_ref, count_ref, *refs):
    kv_refs, (o_ref, k_own, v_own) = refs[:-3], refs[-3:]
    rows = q_ref.shape[0] // o_ref.shape[0]
    lane = lax.broadcasted_iota(jnp.int32, (1, 128), 1)
    first = lane < HEAD_DIM

    @pl.when(pl.program_id(1) == 0)
    def _():
        zero = jnp.zeros((), jnp.bfloat16)
        one = jnp.ones((), jnp.bfloat16)
        for i, kv_ref in enumerate(kv_refs):
            n = kv_ref.shape[0] // 2
            span = pl.ds(i * n, n)
            k = kv_ref[:n]
            v = kv_ref[n:]
            k_own[0, :, span] = jnp.where(first, k, zero).T
            k_own[1, :, span] = jnp.where(first, zero, k).T
            v_own[0, span] = jnp.where(first, v, one)
            v_own[1, span] = jnp.where(first, one, v)

    scale = LOG2E * HEAD_DIM ** (-0.5)
    q = q_ref[...]
    scores = [jnp.dot(q, k_own[h], preferred_element_type=jnp.float32) for h in range(2)]
    tops = [jnp.max(s, axis=1, keepdims=True) for s in scores]
    weights = [
        jnp.exp2((s - top) * scale).astype(jnp.bfloat16) for s, top in zip(scores, tops)
    ]
    sums = [
        jnp.dot(w, v_own[h], preferred_element_type=jnp.float32) for h, w in enumerate(weights)
    ]
    num = jnp.where(first, sums[0], sums[1])
    den_other = jnp.where(first, sums[1], sums[0])
    den = pltpu.roll(den_other, HEAD_DIM, 1)
    context = (num / den).astype(jnp.bfloat16)
    lse = jnp.where(first, tops[1], tops[0]) * scale + jnp.log2(den_other)
    pad = jnp.concatenate([count_ref[...], jnp.zeros((3, 128), jnp.float32)], axis=0)
    for i in range(o_ref.shape[0]):
        span = slice(i * rows, i * rows + rows)
        turned = lse[span].T
        left = jnp.concatenate([turned[HEAD_DIM : HEAD_DIM + 1], turned[0:1]], axis=0)
        left = jnp.concatenate([left[:, :128], left[:, 128:]], axis=0)
        hi = left.astype(jnp.bfloat16)
        rest = left - hi.astype(jnp.float32)
        mid = rest.astype(jnp.bfloat16)
        rest = rest - mid.astype(jnp.float32)
        o_ref[i, :rows] = context[span]
        o_ref[i, rows : rows + STAT] = jnp.concatenate(
            [hi.astype(jnp.float32), mid.astype(jnp.float32), rest, pad], axis=0
        ).astype(jnp.bfloat16)
        o_ref[i, rows + STAT :] = piece_ref[i]


def attend(queries, pieces, carried, counts):
    n, width = queries.shape
    rows = n // SIDE
    keys_n = sum(x.shape[0] for x in pieces) // 2
    pairs = width // 128
    out_rows = rows + STAT + carried.shape[1]
    return pl.pallas_call(
        attend_kernel,
        grid=(pairs, SIDE // 2),
        in_specs=[
            pl.BlockSpec((2 * rows, 128), lambda p, i: (i, p)),
            pl.BlockSpec((2, carried.shape[1], 128), lambda p, i: (i, 0, p)),
            pl.BlockSpec(counts.shape, lambda p, i: (0, 0)),
        ]
        + [pl.BlockSpec((x.shape[0], 128), lambda p, i: (0, p)) for x in pieces],
        out_specs=pl.BlockSpec((2, out_rows, 128), lambda p, i: (i, 0, p)),
        out_shape=jax.ShapeDtypeStruct((SIDE, out_rows, width), jnp.bfloat16),
        scratch_shapes=[
            pltpu.VMEM((2, 128, keys_n), jnp.bfloat16),
            pltpu.VMEM((2, keys_n, 128), jnp.bfloat16),
        ],
        compiler_params=pltpu.CompilerParams(vmem_limit_bytes=40 * 1024 * 1024),
        name="attend",
    )(queries, carried, counts, *pieces)


def merge_kernel(part_ref, residual_ref, sel_ref, out_ref, rider_ref):
    rows, width = residual_ref.shape
    lane = lax.broadcasted_iota(jnp.int32, (1, 128), 1)
    first = lane < HEAD_DIM
    stats = part_ref[:, rows : rows + STAT].astype(jnp.float32)
    merged = stats[:, 0:4] + stats[:, 4:8] + stats[:, 8:12]
    scaled = []
    for p in range(width // 128):
        cols = slice(p * 128, p * 128 + 128)
        for h in range(2):
            x = jnp.concatenate([merged[:, h, cols], merged[:, 2 + h, cols]], axis=1)
            w = jnp.exp2(x - jnp.max(x, axis=0, keepdims=True))
            scaled.append(w / jnp.sum(w, axis=0, keepdims=True))
    weights = jnp.concatenate(scaled, axis=0)
    weights = jnp.concatenate(
        [weights, jnp.zeros((128 - weights.shape[0], rows), jnp.float32)], axis=0
    ).T
    streams = []
    for p in range(width // 128):
        cols = slice(p * 128, p * 128 + 128)
        total = jnp.zeros((rows, 128), jnp.float32)
        for j in range(SIDE):
            a = (2 * p) * SIDE + j
            b = (2 * p + 1) * SIDE + j
            w = jnp.where(first, weights[:, a : a + 1], weights[:, b : b + 1])
            total = total + w * part_ref[j, :rows, cols].astype(jnp.float32)
        context = total.astype(jnp.bfloat16).astype(jnp.float32)
        streams.append(
            (residual_ref[:, cols].astype(jnp.float32) + context).astype(jnp.bfloat16)
        )
    stream = jnp.concatenate(streams, axis=1)
    pooled = jnp.dot(sel_ref[...], stream, preferred_element_type=jnp.float32).astype(jnp.bfloat16)
    for j in range(SIDE):
        out_ref[j] = pooled

    carried = part_ref[:, rows + STAT :].astype(jnp.float32)
    counts = stats[:, 12:13, :128]
    back = sel_ref.shape[0]
    per = 128 // back
    count_tiles = []
    for half in range(SIDE // per):
        tile = jnp.zeros((1, 128), jnp.float32)
        for q in range(per):
            row = counts[half * per + q]
            row = pltpu.roll(row, q * back, 1) if q else row
            tile = jnp.where(lane // back == q, row, tile)
        count_tiles.append(tile)
    count_row = jnp.concatenate(count_tiles, axis=1)
    tail = jnp.concatenate([count_row, jnp.zeros((15, count_row.shape[1]), jnp.float32)], axis=0)
    for g in range(SIDE):
        span = slice(g % 4 * 8, g % 4 * 8 + 8)
        cols = slice(g // 4 * 128, g // 4 * 128 + 128)
        halves = [
            jnp.concatenate([carried[half * 4 + q, span, cols] for q in range(4)], axis=0)
            for half in range(2)
        ]
        rider_ref[g] = jnp.concatenate(
            [jnp.concatenate(halves, axis=1), tail], axis=0
        ).astype(jnp.bfloat16)


def merge(part, residual, sel):
    back, width = sel.shape[0], residual.shape[1]
    return pl.pallas_call(
        merge_kernel,
        out_shape=[
            jax.ShapeDtypeStruct((SIDE, back, width), jnp.bfloat16),
            jax.ShapeDtypeStruct((SIDE, 48, 256), jnp.bfloat16),
        ],
        compiler_params=pltpu.CompilerParams(vmem_limit_bytes=VMEM_BYTES),
        name="merge",
    )(part, residual, sel)


def column(row):
    return jnp.broadcast_to(row, (128, row.shape[1])).T[:, :1]


def track_kernel(ids_here_ref, ids_ref, every_ref, weight_ref, mean_ref, part_ref, divisor_ref):
    step = mean_ref.shape[0]
    here = column(ids_here_ref[...])
    sums = jnp.zeros(mean_ref.shape, jnp.float32)
    counts = jnp.zeros((step, step), jnp.float32)
    for g in range(SIDE):
        match = here == ids_ref[:, g * step : g * step + step]
        sums = sums + jnp.dot(
            jnp.where(match, 1.0, 0.0).astype(jnp.bfloat16),
            every_ref[g, :step],
            preferred_element_type=jnp.float32,
        )
        count_row = every_ref[g, step + 32 :].astype(jnp.float32)[:1]
        counts = counts + jnp.where(match, count_row, 0.0)
    divisor = jnp.maximum(jnp.sum(counts, axis=1, keepdims=True), 1.0)
    divisor_ref[...] = jnp.broadcast_to(divisor, divisor_ref.shape)
    mean = (sums / divisor).astype(jnp.bfloat16)
    mean_ref[...] = mean
    part_ref[...] = lax.dot_general(
        weight_ref[...], mean, (((1,), (1,)), ((), ())), preferred_element_type=jnp.float32
    ).astype(jnp.bfloat16)


def track_means(ids, every, weight):
    width = every.shape[2]
    rows = ids.shape[1]
    chunk = weight.shape[0]
    step = rows // SIDE
    return pl.pallas_call(
        track_kernel,
        grid=(SIDE,),
        in_specs=[
            pl.BlockSpec((1, step), lambda i: (0, i)),
            pl.BlockSpec((1, rows), lambda i: (0, 0)),
            pl.BlockSpec(every.shape, lambda i: (0, 0, 0)),
            pl.BlockSpec((chunk, width), lambda i: (0, 0)),
        ],
        out_specs=[
            pl.BlockSpec((step, width), lambda i: (i, 0)),
            pl.BlockSpec((chunk, step), lambda i: (0, i)),
            pl.BlockSpec((step, 128), lambda i: (i, 0)),
        ],
        out_shape=[
            jax.ShapeDtypeStruct((rows, width), jnp.bfloat16),
            jax.ShapeDtypeStruct((chunk, rows), jnp.bfloat16),
            jax.ShapeDtypeStruct((rows, 128), jnp.float32),
        ],
        compiler_params=pltpu.CompilerParams(vmem_limit_bytes=VMEM_BYTES),
        name="track_means",
    )(ids, ids, every, weight)


def error_kernel(track_ref, part_ref, other_ref, every_ref, leader_ref, mean_ref, out_ref, target_buf):
    back = part_ref.shape[1] // out_ref.shape[0]
    width = mean_ref.shape[1]
    step = part_ref.shape[1] // SIDE
    for g in range(SIDE):
        carried = every_ref[g, step : step + 32].astype(jnp.float32)
        for z in range(SIDE):
            target_buf[g * SIDE + z] = carried[
                z % 4 * 8 : z % 4 * 8 + 8, z // 4 * 128 : z // 4 * 128 + 128
            ]
    lane = lax.broadcasted_iota(jnp.int32, (8, 128), 1)
    tiles = []
    for group in range(part_ref.shape[1] // 128):
        low = jnp.zeros((8, 128), jnp.float32)
        high = jnp.zeros((8, 128), jnp.float32)
        for j in range(8):
            track = track_ref[group * 8 + j]
            tile = target_buf[track // 4]
            turn = j * POOL + 128 - track % 4 * POOL
            here = lane // POOL == j
            low = jnp.where(here, pltpu.roll(tile, lax.rem(turn, 128), 1), low)
            high = jnp.where(here, pltpu.roll(tile, lax.rem(turn + 64, 128), 1), high)
        tiles.append(jnp.concatenate([low, high], axis=0))
    target = jnp.concatenate(tiles, axis=1)
    total = part_ref[...].astype(jnp.float32) + other_ref[...].astype(jnp.float32)
    error = (total - target).astype(jnp.bfloat16).astype(jnp.float32)
    grad = jnp.dot(
        (error * leader_ref[...]).astype(jnp.bfloat16),
        mean_ref[...],
        preferred_element_type=jnp.float32,
    ).astype(jnp.bfloat16)
    per = 128 // back
    for s in range(out_ref.shape[0]):
        tile = error[:, s // per * 128 : s // per * 128 + 128]
        turn = s % per * back
        rows = pltpu.roll(tile, 128 - turn, 1) if turn else tile
        out_ref[s, :, :width] = grad
        out_ref[s, :, width:] = rows.astype(jnp.bfloat16)


def error_messages(tracks, partial, other, every, leader, mean, seq_count):
    chunk = partial.shape[0]
    vmem = pl.BlockSpec(memory_space=pltpu.VMEM)
    return pl.pallas_call(
        error_kernel,
        in_specs=[pl.BlockSpec(memory_space=pltpu.SMEM), vmem, vmem, vmem, vmem, vmem],
        out_shape=jax.ShapeDtypeStruct((seq_count, chunk, mean.shape[1] + 128), jnp.bfloat16),
        scratch_shapes=[pltpu.VMEM((seq_count, 8, 128), jnp.float32)],
        compiler_params=pltpu.CompilerParams(vmem_limit_bytes=VMEM_BYTES),
        name="error_messages",
    )(tracks, partial, other, every, leader, mean)


def finish_kernel(index_ref, final_ref, weight_ref, sel_ref, divisor_ref, grad_ref, context_ref):
    width = weight_ref.shape[0]
    back = sel_ref.shape[0]
    for i in range(final_ref.shape[0] // width):
        span = slice(i * width, i * width + width)
        grad_ref[:, span] = final_ref[span, :width].T
    mean_grad = jnp.dot(
        weight_ref[...], final_ref[:, width:], preferred_element_type=jnp.float32
    ).T[:back]
    track_grad = (mean_grad / divisor_ref[:, :1]).astype(jnp.bfloat16)
    context_ref[...] = lax.dot_general(
        sel_ref[...], track_grad, (((0,), (0,)), ((), ())), preferred_element_type=jnp.float32
    ).astype(jnp.bfloat16)


def finish(index, final, weight, sel, divisor):
    width, target_d = weight.shape
    back, tok_rows = sel.shape
    whole = lambda *shape: pl.BlockSpec(shape, lambda i, at: (0, 0))
    return pl.pallas_call(
        finish_kernel,
        grid_spec=pltpu.PrefetchScalarGridSpec(
            num_scalar_prefetch=1,
            grid=(1,),
            in_specs=[
                whole(*final.shape),
                whole(*weight.shape),
                whole(*sel.shape),
                pl.BlockSpec((back, 128), lambda i, at: (at[0], 0)),
            ],
            out_specs=[whole(width, target_d), whole(tok_rows, width)],
        ),
        out_shape=[
            jax.ShapeDtypeStruct((width, target_d), jnp.bfloat16),
            jax.ShapeDtypeStruct((tok_rows, width), jnp.bfloat16),
        ],
        compiler_params=pltpu.CompilerParams(vmem_limit_bytes=VMEM_BYTES),
        name="finish",
    )(index.reshape(1).astype(jnp.int32), final, weight, sel, divisor)


def local(queries, keys, values, residual, reg_weight, targets, block_track, row_count, pool_slot):
    tok_rows, width = queries.shape
    here = tok_rows // BLK
    seq_count = lax.axis_size("seq")
    seq_index = lax.axis_index("seq")
    blocks = here * seq_count
    target_d = reg_weight.shape[1]
    chunk = target_d // seq_count
    owned = targets.shape[0]

    own_kv = jnp.concatenate([keys, values], axis=0)
    pieces = [own_kv] + [
        lax.ppermute(own_kv, "seq", shift(seq_count, d)) for d in (6, 5, 7, 2, 4, 1, 3)
    ]
    query_all = spread(queries, GROUP_Z).reshape(SIDE * tok_rows, width)

    valid = jnp.arange(BLK, dtype=jnp.int32)[None, :] < row_count[:, None]
    match = pool_slot[:, None, :] == jnp.arange(POOL, dtype=jnp.int32)[None, :, None]
    sel = match & valid[:, None, :]
    same_block = jnp.arange(here)[:, None] == jnp.arange(here)[None, :]
    selector = (
        jnp.where(sel[:, :, None, :] & same_block[:, None, :, None], 1.0, 0.0)
        .astype(jnp.bfloat16)
        .reshape(here * POOL, tok_rows)
    )
    slot_rows = jnp.sum(jnp.where(sel, 1.0, 0.0), axis=2).reshape(1, here * POOL)
    slot_rows = jnp.pad(slot_rows, ((0, 0), (0, 128 - here * POOL)))
    turned = targets.reshape(owned * POOL, target_d).T
    turned = turned.reshape(SIDE, SIDE, 2, chunk // 2, owned * POOL).transpose(1, 0, 2, 3, 4)
    carried = jnp.concatenate([turned[:, :, 0], turned[:, :, 1]], axis=3)
    carried = carried.reshape(SIDE, 2, SIDE * chunk // 4, 128)
    carried = jnp.concatenate([carried[:, 0], carried[:, 1]], axis=2)
    same = block_track[:, None] == block_track[None, :]
    earlier = jnp.arange(blocks)[None, :] < jnp.arange(blocks)[:, None]
    leader = jnp.where(jnp.any(same & earlier, axis=1), 0.0, 1.0)
    leader = jnp.repeat(leader, POOL).reshape(1, blocks * POOL)
    ids = (
        (block_track[:, None] * POOL + jnp.arange(POOL, dtype=jnp.int32)[None, :])
        .reshape(1, blocks * POOL)
        .astype(jnp.float32)
    )
    chunk_weight = lax.dynamic_slice_in_dim(reg_weight, seq_index * chunk, chunk, axis=1).T

    part = attend(query_all, pieces, carried, slot_rows)
    part, selector, leader, ids, chunk_weight = lax.optimization_barrier(
        (part, selector, leader, ids, chunk_weight)
    )
    part = lax.all_to_all(part, "seq", 0, 0, axis_index_groups=GROUP_Z)
    pooled, rider = merge(part, residual, selector)
    pooled = lax.all_to_all(pooled, "seq", 0, 0, axis_index_groups=GROUP_Z)
    pooled = pooled.reshape(1, blocks * POOL // SIDE, width)
    every = jnp.concatenate(
        [jnp.broadcast_to(pooled, (SIDE, *pooled.shape[1:])), rider], axis=1
    )
    every = lax.all_to_all(every, "seq", 0, 0, axis_index_groups=GROUP_YX)
    mean, partial, divisor = track_means(ids, every, chunk_weight)
    core_mate = lax.ppermute(partial, "head", [(0, 1), (1, 0), (2, 3), (3, 2)])
    partial = (partial.astype(jnp.float32) + core_mate.astype(jnp.float32)).astype(jnp.bfloat16)
    other = lax.ppermute(partial, "head", [(0, 2), (2, 0), (1, 3), (3, 1)])
    final = error_messages(block_track, partial, other, every, leader, mean, seq_count)
    final = lax.all_to_all(final, "seq", 0, 0).reshape(target_d, width + 128)
    return finish(seq_index, final, reg_weight, selector, divisor)


def solution(mesh):
    return jax.shard_map(
        local,
        mesh=mesh,
        in_specs=(
            P("seq", "head"),
            P("seq", "head"),
            P("seq", "head"),
            P("seq", "head"),
            P("head", None),
            P("seq", None, None),
            P(),
            P("seq"),
            P("seq", None),
        ),
        out_specs=(P("head", None), P("seq", "head")),
        check_vma=False,
    )
```

```python
import functools

import jax
import jax.numpy as jnp
from jax import lax
from jax.experimental import pallas as pl
from jax.experimental.pallas import tpu as pltpu
from jax.sharding import PartitionSpec as P

HEAD_DIM = 64
BLK = 128
POOL = 16
SIDE = 8
LOG2E = 1.4426950408889634
STAT = 16
VMEM_BYTES = 24 * 1024 * 1024

GROUP_Z = [[g * SIDE + i for i in range(SIDE)] for g in range(SIDE)]
GROUP_YX = [[g * SIDE + i for g in range(SIDE)] for i in range(SIDE)]


def spread(x, groups):
    wide = jnp.broadcast_to(x[None], (SIDE, *x.shape))
    return lax.all_to_all(wide, "seq", 0, 0, axis_index_groups=groups)


def ring(seq_count, step):
    return [
        (g * SIDE + i, g * SIDE + (i + step) % SIDE)
        for g in range(seq_count // SIDE)
        for i in range(SIDE)
    ]


def gather_ring(x, seq_count):
    pieces, up, down = [x], x, x
    for i in range(SIDE // 2):
        up = lax.ppermute(up, "seq", ring(seq_count, 1))
        pieces.append(up)
        if i + 1 < SIDE // 2:
            down = lax.ppermute(down, "seq", ring(seq_count, -1))
            pieces.append(down)
    return pieces


def attend_kernel(q_ref, piece_ref, count_ref, *refs):
    kv_refs, (o_ref, k_own, v_own) = refs[:-3], refs[-3:]
    rows = q_ref.shape[0] // o_ref.shape[0]
    lane = lax.broadcasted_iota(jnp.int32, (1, 128), 1)
    first = lane < HEAD_DIM

    @pl.when(pl.program_id(1) == 0)
    def _():
        zero = jnp.zeros((), jnp.bfloat16)
        one = jnp.ones((), jnp.bfloat16)
        for i, kv_ref in enumerate(kv_refs):
            n = kv_ref.shape[0] // 2
            span = pl.ds(i * n, n)
            k = kv_ref[:n]
            v = kv_ref[n:]
            k_own[0, :, span] = jnp.where(first, k, zero).T
            k_own[1, :, span] = jnp.where(first, zero, k).T
            v_own[0, span] = jnp.where(first, v, one)
            v_own[1, span] = jnp.where(first, one, v)

    scale = LOG2E * HEAD_DIM ** (-0.5)
    q = q_ref[...]
    scores = [jnp.dot(q, k_own[h], preferred_element_type=jnp.float32) for h in range(2)]
    tops = [jnp.max(s, axis=1, keepdims=True) for s in scores]
    weights = [
        jnp.exp2((s - top) * scale).astype(jnp.bfloat16) for s, top in zip(scores, tops)
    ]
    sums = [
        jnp.dot(w, v_own[h], preferred_element_type=jnp.float32) for h, w in enumerate(weights)
    ]
    num = jnp.where(first, sums[0], sums[1])
    den_other = jnp.where(first, sums[1], sums[0])
    den = pltpu.roll(den_other, HEAD_DIM, 1)
    context = (num / den).astype(jnp.bfloat16)
    lse = jnp.where(first, tops[1], tops[0]) * scale + jnp.log2(den_other)
    pad = jnp.concatenate([count_ref[...], jnp.zeros((3, 128), jnp.float32)], axis=0)
    for i in range(o_ref.shape[0]):
        span = slice(i * rows, i * rows + rows)
        turned = lse[span].T
        left = jnp.concatenate([turned[HEAD_DIM : HEAD_DIM + 1], turned[0:1]], axis=0)
        left = jnp.concatenate([left[:, :128], left[:, 128:]], axis=0)
        hi = left.astype(jnp.bfloat16)
        rest = left - hi.astype(jnp.float32)
        mid = rest.astype(jnp.bfloat16)
        rest = rest - mid.astype(jnp.float32)
        o_ref[i, :rows] = context[span]
        o_ref[i, rows : rows + STAT] = jnp.concatenate(
            [hi.astype(jnp.float32), mid.astype(jnp.float32), rest, pad], axis=0
        ).astype(jnp.bfloat16)
        o_ref[i, rows + STAT :] = piece_ref[i]


def attend(queries, pieces, carried, counts):
    n, width = queries.shape
    rows = n // SIDE
    keys_n = sum(x.shape[0] for x in pieces) // 2
    pairs = width // 128
    out_rows = rows + STAT + carried.shape[1]
    return pl.pallas_call(
        attend_kernel,
        grid=(pairs, SIDE // 2),
        in_specs=[
            pl.BlockSpec((2 * rows, 128), lambda p, i: (i, p)),
            pl.BlockSpec((2, carried.shape[1], 128), lambda p, i: (i, 0, p)),
            pl.BlockSpec(counts.shape, lambda p, i: (0, 0)),
        ]
        + [pl.BlockSpec((x.shape[0], 128), lambda p, i: (0, p)) for x in pieces],
        out_specs=pl.BlockSpec((2, out_rows, 128), lambda p, i: (i, 0, p)),
        out_shape=jax.ShapeDtypeStruct((SIDE, out_rows, width), jnp.bfloat16),
        scratch_shapes=[
            pltpu.VMEM((2, 128, keys_n), jnp.bfloat16),
            pltpu.VMEM((2, keys_n, 128), jnp.bfloat16),
        ],
        compiler_params=pltpu.CompilerParams(vmem_limit_bytes=40 * 1024 * 1024),
        name="attend",
    )(queries, carried, counts, *pieces)


def merge_kernel(part_ref, residual_ref, sel_ref, out_ref):
    rows, width = residual_ref.shape
    lane = lax.broadcasted_iota(jnp.int32, (1, 128), 1)
    first = lane < HEAD_DIM
    stats = part_ref[:, rows : rows + STAT].astype(jnp.float32)
    merged = stats[:, 0:4] + stats[:, 4:8] + stats[:, 8:12]
    scaled = []
    for p in range(width // 128):
        cols = slice(p * 128, p * 128 + 128)
        for h in range(2):
            x = jnp.concatenate([merged[:, h, cols], merged[:, 2 + h, cols]], axis=1)
            w = jnp.exp2(x - jnp.max(x, axis=0, keepdims=True))
            scaled.append(w / jnp.sum(w, axis=0, keepdims=True))
    weights = jnp.concatenate(scaled, axis=0)
    weights = jnp.concatenate(
        [weights, jnp.zeros((128 - weights.shape[0], rows), jnp.float32)], axis=0
    ).T
    streams = []
    for p in range(width // 128):
        cols = slice(p * 128, p * 128 + 128)
        total = jnp.zeros((rows, 128), jnp.float32)
        for j in range(SIDE):
            a = (2 * p) * SIDE + j
            b = (2 * p + 1) * SIDE + j
            w = jnp.where(first, weights[:, a : a + 1], weights[:, b : b + 1])
            total = total + w * part_ref[j, :rows, cols].astype(jnp.float32)
        context = total.astype(jnp.bfloat16).astype(jnp.float32)
        streams.append(
            (residual_ref[:, cols].astype(jnp.float32) + context).astype(jnp.bfloat16)
        )
    stream = jnp.concatenate(streams, axis=1)
    pooled = jnp.dot(sel_ref[...], stream, preferred_element_type=jnp.float32).astype(jnp.bfloat16)
    back = sel_ref.shape[0]
    for j in range(SIDE):
        out_ref[j, :back] = pooled

    carried = part_ref[:, rows + STAT :].astype(jnp.float32)
    counts = stats[:, 12:13, :128]
    per = 128 // back
    count_tiles = []
    for half in range(SIDE // per):
        tile = jnp.zeros((1, 128), jnp.float32)
        for q in range(per):
            row = counts[half * per + q]
            row = pltpu.roll(row, q * back, 1) if q else row
            tile = jnp.where(lane // back == q, row, tile)
        count_tiles.append(tile)
    count_row = jnp.concatenate(count_tiles, axis=1)
    tail = jnp.concatenate([count_row, jnp.zeros((15, count_row.shape[1]), jnp.float32)], axis=0)
    for g in range(SIDE):
        span = slice(g % 4 * 8, g % 4 * 8 + 8)
        cols = slice(g // 4 * 128, g // 4 * 128 + 128)
        halves = [
            jnp.concatenate([carried[half * 4 + q, span, cols] for q in range(4)], axis=0)
            for half in range(2)
        ]
        out_ref[g, back:] = jnp.concatenate(
            [jnp.concatenate(halves, axis=1), tail], axis=0
        ).astype(jnp.bfloat16)


def merge(part, residual, sel):
    back, width = sel.shape[0], residual.shape[1]
    return pl.pallas_call(
        merge_kernel,
        out_shape=jax.ShapeDtypeStruct((SIDE, back + 48, width), jnp.bfloat16),
        compiler_params=pltpu.CompilerParams(vmem_limit_bytes=VMEM_BYTES),
        name="merge",
    )(part, residual, sel)


def column(row):
    return jnp.broadcast_to(row, (128, row.shape[1])).T[:, :1]


def track_kernel(
    ids_here_ref, ids_ref, every_ref, both_ref, weight_ref, mean_ref, part_ref, divisor_ref, count_buf
):
    step = mean_ref.shape[0]

    @pl.when(pl.program_id(0) == 0)
    def _():
        lane = lax.broadcasted_iota(jnp.int32, (1, 128), 1)
        rows = [
            both_ref[z, both_ref.shape[1] - 16 :].astype(jnp.float32)[:1] for z in range(SIDE)
        ]
        for g in range(SIDE):
            for half in range(2):
                tile = jnp.zeros((1, 128), jnp.float32)
                for q in range(4):
                    row = rows[half * 4 + q][:, g // 4 * 128 : g // 4 * 128 + 128]
                    turn = (q - g % 4) % 4 * 32
                    row = pltpu.roll(row, turn, 1) if turn else row
                    tile = jnp.where(lane // 32 == q, row, tile)
                count_buf[g : g + 1, half * 128 : half * 128 + 128] = tile

    here = column(ids_here_ref[...])
    sums = jnp.zeros(mean_ref.shape, jnp.float32)
    counts = jnp.zeros((step, step), jnp.float32)
    for g in range(SIDE):
        match = here == ids_ref[:, g * step : g * step + step]
        sums = sums + jnp.dot(
            jnp.where(match, 1.0, 0.0).astype(jnp.bfloat16),
            every_ref[g],
            preferred_element_type=jnp.float32,
        )
        counts = counts + jnp.where(match, count_buf[g : g + 1], 0.0)
    divisor = jnp.maximum(jnp.sum(counts, axis=1, keepdims=True), 1.0)
    divisor_ref[...] = jnp.broadcast_to(divisor, divisor_ref.shape)
    mean = (sums / divisor).astype(jnp.bfloat16)
    mean_ref[...] = mean
    part_ref[...] = lax.dot_general(
        weight_ref[...], mean, (((1,), (1,)), ((), ())), preferred_element_type=jnp.float32
    ).astype(jnp.bfloat16)


def track_means(ids, every, both, weight):
    width = every.shape[2]
    rows = ids.shape[1]
    chunk = weight.shape[0]
    step = rows // SIDE
    return pl.pallas_call(
        track_kernel,
        grid=(SIDE,),
        in_specs=[
            pl.BlockSpec((1, step), lambda i: (0, i)),
            pl.BlockSpec((1, rows), lambda i: (0, 0)),
            pl.BlockSpec(every.shape, lambda i: (0, 0, 0)),
            pl.BlockSpec(both.shape, lambda i: (0, 0, 0)),
            pl.BlockSpec((chunk, width), lambda i: (0, 0)),
        ],
        out_specs=[
            pl.BlockSpec((step, width), lambda i: (i, 0)),
            pl.BlockSpec((chunk, step), lambda i: (0, i)),
            pl.BlockSpec((step, 128), lambda i: (i, 0)),
        ],
        out_shape=[
            jax.ShapeDtypeStruct((rows, width), jnp.bfloat16),
            jax.ShapeDtypeStruct((chunk, rows), jnp.bfloat16),
            jax.ShapeDtypeStruct((rows, 128), jnp.float32),
        ],
        scratch_shapes=[pltpu.VMEM((SIDE, step), jnp.float32)],
        compiler_params=pltpu.CompilerParams(vmem_limit_bytes=VMEM_BYTES),
        name="track_means",
    )(ids, ids, every, both, weight)


def error_kernel(track_ref, part_ref, other_ref, both_ref, leader_ref, mean_ref, out_ref, target_buf):
    back = part_ref.shape[1] // out_ref.shape[0]
    width = mean_ref.shape[1]
    for z in range(SIDE):
        carried = both_ref[z, back : back + 32].astype(jnp.float32)
        for g in range(SIDE):
            target_buf[g * SIDE + z] = carried[
                g % 4 * 8 : g % 4 * 8 + 8, g // 4 * 128 : g // 4 * 128 + 128
            ]
    lane = lax.broadcasted_iota(jnp.int32, (8, 128), 1)
    tiles = []
    for group in range(part_ref.shape[1] // 128):
        low = jnp.zeros((8, 128), jnp.float32)
        high = jnp.zeros((8, 128), jnp.float32)
        for j in range(8):
            track = track_ref[group * 8 + j]
            tile = target_buf[track // 4]
            turn = j * POOL + 128 - track % 4 * POOL
            here = lane // POOL == j
            low = jnp.where(here, pltpu.roll(tile, lax.rem(turn, 128), 1), low)
            high = jnp.where(here, pltpu.roll(tile, lax.rem(turn + 64, 128), 1), high)
        tiles.append(jnp.concatenate([low, high], axis=0))
    target = jnp.concatenate(tiles, axis=1)
    total = part_ref[...].astype(jnp.float32) + other_ref[...].astype(jnp.float32)
    error = (total - target).astype(jnp.bfloat16).astype(jnp.float32)
    grad = jnp.dot(
        (error * leader_ref[...]).astype(jnp.bfloat16),
        mean_ref[...],
        preferred_element_type=jnp.float32,
    ).astype(jnp.bfloat16)
    per = 128 // back
    for s in range(out_ref.shape[0]):
        tile = error[:, s // per * 128 : s // per * 128 + 128]
        turn = s % per * back
        rows = pltpu.roll(tile, 128 - turn, 1) if turn else tile
        out_ref[s, :, :width] = grad
        out_ref[s, :, width:] = rows.astype(jnp.bfloat16)


def error_messages(tracks, partial, other, both, leader, mean, seq_count):
    chunk = partial.shape[0]
    vmem = pl.BlockSpec(memory_space=pltpu.VMEM)
    return pl.pallas_call(
        error_kernel,
        in_specs=[pl.BlockSpec(memory_space=pltpu.SMEM), vmem, vmem, vmem, vmem, vmem],
        out_shape=jax.ShapeDtypeStruct((seq_count, chunk, mean.shape[1] + 128), jnp.bfloat16),
        scratch_shapes=[pltpu.VMEM((seq_count, 8, 128), jnp.float32)],
        compiler_params=pltpu.CompilerParams(vmem_limit_bytes=VMEM_BYTES),
        name="error_messages",
    )(tracks, partial, other, both, leader, mean)


def finish_kernel(index_ref, final_ref, weight_ref, sel_ref, divisor_ref, grad_ref, context_ref):
    width = weight_ref.shape[0]
    back = sel_ref.shape[0]
    for i in range(final_ref.shape[0] // width):
        span = slice(i * width, i * width + width)
        grad_ref[:, span] = final_ref[span, :width].T
    mean_grad = jnp.dot(
        weight_ref[...], final_ref[:, width:], preferred_element_type=jnp.float32
    ).T[:back]
    track_grad = (mean_grad / divisor_ref[:, :1]).astype(jnp.bfloat16)
    context_ref[...] = lax.dot_general(
        sel_ref[...], track_grad, (((0,), (0,)), ((), ())), preferred_element_type=jnp.float32
    ).astype(jnp.bfloat16)


def finish(index, final, weight, sel, divisor):
    width, target_d = weight.shape
    back, tok_rows = sel.shape
    whole = lambda *shape: pl.BlockSpec(shape, lambda i, at: (0, 0))
    return pl.pallas_call(
        finish_kernel,
        grid_spec=pltpu.PrefetchScalarGridSpec(
            num_scalar_prefetch=1,
            grid=(1,),
            in_specs=[
                whole(*final.shape),
                whole(*weight.shape),
                whole(*sel.shape),
                pl.BlockSpec((back, 128), lambda i, at: (at[0], 0)),
            ],
            out_specs=[whole(width, target_d), whole(tok_rows, width)],
        ),
        out_shape=[
            jax.ShapeDtypeStruct((width, target_d), jnp.bfloat16),
            jax.ShapeDtypeStruct((tok_rows, width), jnp.bfloat16),
        ],
        compiler_params=pltpu.CompilerParams(vmem_limit_bytes=VMEM_BYTES),
        name="finish",
    )(index.reshape(1).astype(jnp.int32), final, weight, sel, divisor)


def local(queries, keys, values, residual, reg_weight, targets, block_track, row_count, pool_slot):
    tok_rows, width = queries.shape
    here = tok_rows // BLK
    seq_count = lax.axis_size("seq")
    seq_index = lax.axis_index("seq")
    blocks = here * seq_count
    target_d = reg_weight.shape[1]
    chunk = target_d // seq_count
    owned = targets.shape[0]

    own_kv = jnp.concatenate([keys, values], axis=0)
    pieces = gather_ring(own_kv, seq_count)
    query_all = spread(queries, GROUP_YX).reshape(SIDE * tok_rows, width)

    valid = jnp.arange(BLK, dtype=jnp.int32)[None, :] < row_count[:, None]
    match = pool_slot[:, None, :] == jnp.arange(POOL, dtype=jnp.int32)[None, :, None]
    sel = match & valid[:, None, :]
    same_block = jnp.arange(here)[:, None] == jnp.arange(here)[None, :]
    selector = (
        jnp.where(sel[:, :, None, :] & same_block[:, None, :, None], 1.0, 0.0)
        .astype(jnp.bfloat16)
        .reshape(here * POOL, tok_rows)
    )
    slot_rows = jnp.sum(jnp.where(sel, 1.0, 0.0), axis=2).reshape(1, here * POOL)
    slot_rows = jnp.pad(slot_rows, ((0, 0), (0, 128 - here * POOL)))
    turned = targets.reshape(owned * POOL, target_d).T
    turned = turned.reshape(SIDE, SIDE, 2, chunk // 2, owned * POOL)
    carried = jnp.concatenate([turned[:, :, 0], turned[:, :, 1]], axis=3)
    carried = carried.reshape(SIDE, 2, SIDE * chunk // 4, 128)
    carried = jnp.concatenate([carried[:, 0], carried[:, 1]], axis=2)
    same = block_track[:, None] == block_track[None, :]
    earlier = jnp.arange(blocks)[None, :] < jnp.arange(blocks)[:, None]
    leader = jnp.where(jnp.any(same & earlier, axis=1), 0.0, 1.0)
    leader = jnp.repeat(leader, POOL).reshape(1, blocks * POOL)
    ids = (
        (block_track[:, None] * POOL + jnp.arange(POOL, dtype=jnp.int32)[None, :])
        .reshape(1, blocks * POOL)
        .astype(jnp.float32)
    )
    chunk_weight = lax.dynamic_slice_in_dim(reg_weight, seq_index * chunk, chunk, axis=1).T

    part = attend(query_all, pieces, carried, slot_rows)
    part, selector, leader, ids, chunk_weight = lax.optimization_barrier(
        (part, selector, leader, ids, chunk_weight)
    )
    part = lax.all_to_all(part, "seq", 0, 0, axis_index_groups=GROUP_YX)
    both = merge(part, residual, selector)
    both = lax.all_to_all(both, "seq", 0, 0, axis_index_groups=GROUP_Z)
    pooled = both[:, : here * POOL].reshape(blocks * POOL // SIDE, width)
    every = spread(pooled, GROUP_YX)
    mean, partial, divisor = track_means(ids, every, both, chunk_weight)
    core_mate = lax.ppermute(partial, "head", [(0, 1), (1, 0), (2, 3), (3, 2)])
    partial = (partial.astype(jnp.float32) + core_mate.astype(jnp.float32)).astype(jnp.bfloat16)
    other = lax.ppermute(partial, "head", [(0, 2), (2, 0), (1, 3), (3, 1)])
    final = error_messages(block_track, partial, other, both, leader, mean, seq_count)
    final = lax.all_to_all(final, "seq", 0, 0).reshape(target_d, width + 128)
    return finish(seq_index, final, reg_weight, selector, divisor)


def solution(mesh):
    return jax.shard_map(
        local,
        mesh=mesh,
        in_specs=(
            P("seq", "head"),
            P("seq", "head"),
            P("seq", "head"),
            P("seq", "head"),
            P("head", None),
            P("seq", None, None),
            P(),
            P("seq"),
            P("seq", None),
        ),
        out_specs=(P("head", None), P("seq", "head")),
        check_vma=False,
    )
```

```python
import functools

import jax
import jax.numpy as jnp
from jax import lax
from jax.experimental import pallas as pl
from jax.experimental.pallas import tpu as pltpu
from jax.sharding import PartitionSpec as P

HEAD_DIM = 64
BLK = 128
POOL = 16
SIDE = 8
LOG2E = 1.4426950408889634
STAT = 16
EARLIER = 32768.0
VMEM_BYTES = 24 * 1024 * 1024

GROUP_Z = [[g * SIDE + i for i in range(SIDE)] for g in range(SIDE)]
GROUP_YX = [[g * SIDE + i for g in range(SIDE)] for i in range(SIDE)]


def spread(x, groups):
    wide = jnp.broadcast_to(x[None], (SIDE, *x.shape))
    return lax.all_to_all(wide, "seq", 0, 0, axis_index_groups=groups)


def ring(seq_count, step):
    return [
        (g * SIDE + i, g * SIDE + (i + step) % SIDE)
        for g in range(seq_count // SIDE)
        for i in range(SIDE)
    ]


def gather_ring(x, seq_count):
    pieces, up, down = [x], x, x
    for i in range(SIDE // 2):
        up = lax.ppermute(up, "seq", ring(seq_count, 1))
        pieces.append(up)
        if i + 1 < SIDE // 2:
            down = lax.ppermute(down, "seq", ring(seq_count, -1))
            pieces.append(down)
    return pieces


def prepare_kernel(row_count_ref, slot_ref, target_ref, carried_ref, sel_ref, count_ref):
    here = slot_ref.shape[0]
    slots = slot_ref[...]
    sub = lax.broadcasted_iota(jnp.int32, (POOL, BLK), 0)
    lane = lax.broadcasted_iota(jnp.int32, (POOL, BLK), 1)
    zero = jnp.zeros((POOL, BLK), jnp.float32)
    picks = []
    for b in range(here):
        hit = (slots[b : b + 1] == sub) & (lane < row_count_ref[b])
        hit = jnp.where(hit, 1.0, 0.0)
        picks.append(jnp.concatenate([hit if i == b else zero for i in range(here)], axis=1))
    sel = jnp.concatenate(picks, axis=0)
    sel_ref[...] = sel.astype(jnp.bfloat16)
    counts = jnp.broadcast_to(jnp.sum(sel, axis=1, keepdims=True), (sel.shape[0], 128))
    counts = jnp.concatenate(
        [counts, jnp.zeros((128 - counts.shape[0], 128), jnp.float32)], axis=0
    )
    count_ref[...] = counts.T[:1]
    rows = target_ref.shape[0]
    blank = jnp.zeros((128 - rows, 128), jnp.float32)
    for g in range(SIDE):
        tile = target_ref[:, g * 128 : g * 128 + 128].astype(jnp.float32)
        tile = jnp.concatenate([tile, blank], axis=0).T
        eights = [
            tile[z * 16 : z * 16 + 8] + pltpu.roll(tile[z * 16 + 8 : z * 16 + 16], 64, 1)
            for z in range(SIDE)
        ]
        carried_ref[g] = jnp.concatenate(
            [jnp.concatenate(eights[:4], axis=0), jnp.concatenate(eights[4:], axis=0)], axis=1
        ).astype(jnp.bfloat16)


def prepare(row_count, pool_slot, targets):
    here = pool_slot.shape[0]
    vmem = pl.BlockSpec(memory_space=pltpu.VMEM)
    return pl.pallas_call(
        prepare_kernel,
        in_specs=[pl.BlockSpec(memory_space=pltpu.SMEM), vmem, vmem],
        out_shape=[
            jax.ShapeDtypeStruct((SIDE, 32, 256), jnp.bfloat16),
            jax.ShapeDtypeStruct((here * POOL, here * BLK), jnp.bfloat16),
            jax.ShapeDtypeStruct((1, 128), jnp.float32),
        ],
        compiler_params=pltpu.CompilerParams(vmem_limit_bytes=VMEM_BYTES),
        name="prepare",
    )(row_count, pool_slot, targets)


def attend_kernel(q_ref, piece_ref, count_ref, *refs):
    kv_refs, (o_ref, k_own, v_own) = refs[:-3], refs[-3:]
    rows = q_ref.shape[0] // o_ref.shape[0]
    lane = lax.broadcasted_iota(jnp.int32, (1, 128), 1)
    first = lane < HEAD_DIM

    @pl.when(pl.program_id(1) == 0)
    def _():
        zero = jnp.zeros((), jnp.bfloat16)
        one = jnp.ones((), jnp.bfloat16)
        for i, kv_ref in enumerate(kv_refs):
            n = kv_ref.shape[0] // 2
            span = pl.ds(i * n, n)
            k = kv_ref[:n]
            v = kv_ref[n:]
            k_own[0, :, span] = jnp.where(first, k, zero).T
            k_own[1, :, span] = jnp.where(first, zero, k).T
            v_own[0, span] = jnp.where(first, v, one)
            v_own[1, span] = jnp.where(first, one, v)

    scale = LOG2E * HEAD_DIM ** (-0.5)
    q = q_ref[...]
    scores = [jnp.dot(q, k_own[h], preferred_element_type=jnp.float32) for h in range(2)]
    tops = [jnp.max(s, axis=1, keepdims=True) for s in scores]
    weights = [
        jnp.exp2((s - top) * scale).astype(jnp.bfloat16) for s, top in zip(scores, tops)
    ]
    sums = [
        jnp.dot(w, v_own[h], preferred_element_type=jnp.float32) for h, w in enumerate(weights)
    ]
    num = jnp.where(first, sums[0], sums[1])
    den_other = jnp.where(first, sums[1], sums[0])
    den = pltpu.roll(den_other, HEAD_DIM, 1)
    context = (num / den).astype(jnp.bfloat16)
    lse = jnp.where(first, tops[1], tops[0]) * scale + jnp.log2(den_other)
    pad = jnp.concatenate([count_ref[...], jnp.zeros((3, 128), jnp.float32)], axis=0)
    for i in range(o_ref.shape[0]):
        span = slice(i * rows, i * rows + rows)
        turned = lse[span].T
        left = jnp.concatenate([turned[HEAD_DIM : HEAD_DIM + 1], turned[0:1]], axis=0)
        left = jnp.concatenate([left[:, :128], left[:, 128:]], axis=0)
        hi = left.astype(jnp.bfloat16)
        rest = left - hi.astype(jnp.float32)
        mid = rest.astype(jnp.bfloat16)
        rest = rest - mid.astype(jnp.float32)
        o_ref[i, :rows] = context[span]
        o_ref[i, rows : rows + STAT] = jnp.concatenate(
            [hi.astype(jnp.float32), mid.astype(jnp.float32), rest, pad], axis=0
        ).astype(jnp.bfloat16)
        o_ref[i, rows + STAT :] = piece_ref[i]


def attend(queries, pieces, carried, counts):
    n, width = queries.shape
    rows = n // SIDE
    keys_n = sum(x.shape[0] for x in pieces) // 2
    pairs = width // 128
    out_rows = rows + STAT + carried.shape[1]
    return pl.pallas_call(
        attend_kernel,
        grid=(pairs, SIDE // 2),
        in_specs=[
            pl.BlockSpec((2 * rows, 128), lambda p, i: (i, p)),
            pl.BlockSpec((2, carried.shape[1], 128), lambda p, i: (i, 0, p)),
            pl.BlockSpec(counts.shape, lambda p, i: (0, 0)),
        ]
        + [pl.BlockSpec((x.shape[0], 128), lambda p, i: (0, p)) for x in pieces],
        out_specs=pl.BlockSpec((2, out_rows, 128), lambda p, i: (i, 0, p)),
        out_shape=jax.ShapeDtypeStruct((SIDE, out_rows, width), jnp.bfloat16),
        scratch_shapes=[
            pltpu.VMEM((2, 128, keys_n), jnp.bfloat16),
            pltpu.VMEM((2, keys_n, 128), jnp.bfloat16),
        ],
        compiler_params=pltpu.CompilerParams(vmem_limit_bytes=40 * 1024 * 1024),
        name="attend",
    )(queries, carried, counts, *pieces)


def merge_kernel(part_ref, residual_ref, sel_ref, out_ref):
    rows, width = residual_ref.shape
    lane = lax.broadcasted_iota(jnp.int32, (1, 128), 1)
    first = lane < HEAD_DIM
    stats = part_ref[:, rows : rows + STAT].astype(jnp.float32)
    merged = stats[:, 0:4] + stats[:, 4:8] + stats[:, 8:12]
    scaled = []
    for p in range(width // 128):
        cols = slice(p * 128, p * 128 + 128)
        for h in range(2):
            x = jnp.concatenate([merged[:, h, cols], merged[:, 2 + h, cols]], axis=1)
            w = jnp.exp2(x - jnp.max(x, axis=0, keepdims=True))
            scaled.append(w / jnp.sum(w, axis=0, keepdims=True))
    weights = jnp.concatenate(scaled, axis=0)
    weights = jnp.concatenate(
        [weights, jnp.zeros((128 - weights.shape[0], rows), jnp.float32)], axis=0
    ).T
    streams = []
    for p in range(width // 128):
        cols = slice(p * 128, p * 128 + 128)
        total = jnp.zeros((rows, 128), jnp.float32)
        for j in range(SIDE):
            a = (2 * p) * SIDE + j
            b = (2 * p + 1) * SIDE + j
            w = jnp.where(first, weights[:, a : a + 1], weights[:, b : b + 1])
            total = total + w * part_ref[j, :rows, cols].astype(jnp.float32)
        context = total.astype(jnp.bfloat16).astype(jnp.float32)
        streams.append(
            (residual_ref[:, cols].astype(jnp.float32) + context).astype(jnp.bfloat16)
        )
    stream = jnp.concatenate(streams, axis=1)
    pooled = jnp.dot(sel_ref[...], stream, preferred_element_type=jnp.float32).astype(jnp.bfloat16)
    back = sel_ref.shape[0]
    for j in range(SIDE):
        out_ref[j, :back] = pooled

    carried = part_ref[:, rows + STAT :].astype(jnp.float32)
    counts = stats[:, 12:13, :128]
    per = 128 // back
    count_tiles = []
    for half in range(SIDE // per):
        tile = jnp.zeros((1, 128), jnp.float32)
        for q in range(per):
            row = counts[half * per + q]
            row = pltpu.roll(row, q * back, 1) if q else row
            tile = jnp.where(lane // back == q, row, tile)
        count_tiles.append(tile)
    count_row = jnp.concatenate(count_tiles, axis=1)
    tail = jnp.concatenate([count_row, jnp.zeros((15, count_row.shape[1]), jnp.float32)], axis=0)
    for g in range(SIDE):
        span = slice(g % 4 * 8, g % 4 * 8 + 8)
        cols = slice(g // 4 * 128, g // 4 * 128 + 128)
        halves = [
            jnp.concatenate([carried[half * 4 + q, span, cols] for q in range(4)], axis=0)
            for half in range(2)
        ]
        out_ref[g, back:] = jnp.concatenate(
            [jnp.concatenate(halves, axis=1), tail], axis=0
        ).astype(jnp.bfloat16)


def merge(part, residual, sel):
    back, width = sel.shape[0], residual.shape[1]
    return pl.pallas_call(
        merge_kernel,
        out_shape=jax.ShapeDtypeStruct((SIDE, back + 48, width), jnp.bfloat16),
        compiler_params=pltpu.CompilerParams(vmem_limit_bytes=VMEM_BYTES),
        name="merge",
    )(part, residual, sel)


def column(row):
    return jnp.broadcast_to(row, (128, row.shape[1])).T[:, :1]


def track_kernel(
    track_ref,
    index_ref,
    every_ref,
    both_ref,
    weight_ref,
    mean_ref,
    part_ref,
    divisor_ref,
    count_buf,
    id_buf,
    weight_buf,
):
    step = mean_ref.shape[0]
    at = pl.program_id(0)

    @pl.when(at == 0)
    def _():
        lane = lax.broadcasted_iota(jnp.int32, (1, 128), 1)
        rows = [
            both_ref[z, both_ref.shape[1] - 16 :].astype(jnp.float32)[:1] for z in range(SIDE)
        ]
        for g in range(SIDE):
            for half in range(2):
                tile = jnp.zeros((1, 128), jnp.float32)
                for q in range(4):
                    row = rows[half * 4 + q][:, g // 4 * 128 : g // 4 * 128 + 128]
                    turn = (q - g % 4) % 4 * 32
                    row = pltpu.roll(row, turn, 1) if turn else row
                    tile = jnp.where(lane // 32 == q, row, tile)
                count_buf[g : g + 1, half * 128 : half * 128 + 128] = tile
                track = jnp.zeros((1, 128), jnp.int32)
                for j in range(8):
                    track = jnp.where(lane // POOL == j, track_ref[g * 16 + half * 8 + j], track)
                id_buf[g : g + 1, half * 128 : half * 128 + 128] = (
                    track * POOL + lane % POOL
                ).astype(jnp.float32)
        weight_buf[...] = weight_ref[...].T

    here = column(id_buf[pl.ds(at, 1)])
    sums = jnp.zeros(mean_ref.shape, jnp.float32)
    counts = jnp.zeros((step, step), jnp.float32)
    for g in range(SIDE):
        match = here == id_buf[g : g + 1]
        sums = sums + jnp.dot(
            jnp.where(match, 1.0, 0.0).astype(jnp.bfloat16),
            every_ref[g],
            preferred_element_type=jnp.float32,
        )
        seen = count_buf[g : g + 1] + jnp.where(g < at, EARLIER, 0.0)
        counts = counts + jnp.where(match, seen, 0.0)
    below = lax.broadcasted_iota(jnp.int32, (step, step), 1) < lax.broadcasted_iota(
        jnp.int32, (step, step), 0
    )
    counts = counts + jnp.where((here == id_buf[pl.ds(at, 1)]) & below, EARLIER, 0.0)
    total = jnp.sum(counts, axis=1, keepdims=True)
    before = jnp.floor(total * (1.0 / EARLIER))
    divisor = jnp.maximum(total - before * EARLIER, 1.0)
    divisor_ref[...] = jnp.broadcast_to(divisor, divisor_ref.shape)
    mean = sums / divisor
    mean_ref[...] = jnp.where(before > 0.0, 0.0, mean).astype(jnp.bfloat16)
    chunk = part_ref.shape[0]
    start = pl.multiple_of(lax.rem(index_ref[0], 128 // chunk) * chunk, chunk)
    part_ref[...] = lax.dot_general(
        weight_buf[pl.ds(start, chunk)],
        mean.astype(jnp.bfloat16),
        (((1,), (1,)), ((), ())),
        preferred_element_type=jnp.float32,
    ).astype(jnp.bfloat16)


def track_means(tracks, index, every, both, weight, chunk):
    step, width = every.shape[1:]
    rows = SIDE * step
    return pl.pallas_call(
        track_kernel,
        grid_spec=pltpu.PrefetchScalarGridSpec(
            num_scalar_prefetch=2,
            grid=(SIDE,),
            in_specs=[
                pl.BlockSpec(every.shape, lambda i, t, at: (0, 0, 0)),
                pl.BlockSpec(both.shape, lambda i, t, at: (0, 0, 0)),
                pl.BlockSpec((width, 128), lambda i, t, at: (0, at[0] // (128 // chunk))),
            ],
            out_specs=[
                pl.BlockSpec((step, width), lambda i, t, at: (i, 0)),
                pl.BlockSpec((chunk, step), lambda i, t, at: (0, i)),
                pl.BlockSpec((step, 128), lambda i, t, at: (i, 0)),
            ],
            scratch_shapes=[
                pltpu.VMEM((SIDE, step), jnp.float32),
                pltpu.VMEM((SIDE, step), jnp.float32),
                pltpu.VMEM((128, width), jnp.bfloat16),
            ],
        ),
        out_shape=[
            jax.ShapeDtypeStruct((rows, width), jnp.bfloat16),
            jax.ShapeDtypeStruct((chunk, rows), jnp.bfloat16),
            jax.ShapeDtypeStruct((rows, 128), jnp.float32),
        ],
        compiler_params=pltpu.CompilerParams(vmem_limit_bytes=VMEM_BYTES),
        name="track_means",
    )(tracks, index, every, both, weight)


def error_kernel(track_ref, part_ref, other_ref, both_ref, mean_ref, out_ref, target_buf):
    chunk = part_ref.shape[0]
    back = part_ref.shape[1] // target_buf.shape[0]
    for z in range(SIDE):
        carried = both_ref[z, back : back + 32].astype(jnp.float32)
        for g in range(SIDE):
            target_buf[g * SIDE + z] = carried[
                g % 4 * 8 : g % 4 * 8 + 8, g // 4 * 128 : g // 4 * 128 + 128
            ]
    lane = lax.broadcasted_iota(jnp.int32, (8, 128), 1)
    tiles = []
    for group in range(part_ref.shape[1] // 128):
        low = jnp.zeros((8, 128), jnp.float32)
        high = jnp.zeros((8, 128), jnp.float32)
        for j in range(8):
            track = track_ref[group * 8 + j]
            tile = target_buf[track // 4]
            turn = j * POOL + 128 - track % 4 * POOL
            here = lane // POOL == j
            low = jnp.where(here, pltpu.roll(tile, lax.rem(turn, 128), 1), low)
            high = jnp.where(here, pltpu.roll(tile, lax.rem(turn + 64, 128), 1), high)
        tiles.append(jnp.concatenate([low, high], axis=0))
    target = jnp.concatenate(tiles, axis=1)
    total = part_ref[...].astype(jnp.float32) + other_ref[...].astype(jnp.float32)
    error = (total - target).astype(jnp.bfloat16).astype(jnp.float32)
    grad = jnp.dot(
        error.astype(jnp.bfloat16), mean_ref[...], preferred_element_type=jnp.float32
    ).astype(jnp.bfloat16)
    wide = lax.broadcasted_iota(jnp.int32, (chunk, 128), 1)
    for z in range(SIDE):
        out_ref[z, :chunk] = grad
        for half in range(2):
            tile = jnp.zeros((chunk, 128), jnp.float32)
            for q in range(4):
                source = (half * 4 + q) * 2 + z // 4
                row = error[:, source * 128 : source * 128 + 128]
                turn = (q - z % 4) % 4 * 32
                row = pltpu.roll(row, turn, 1) if turn else row
                tile = jnp.where(wide // 32 == q, row, tile)
            out_ref[z, chunk:, half * 128 : half * 128 + 128] = tile.astype(jnp.bfloat16)


def error_messages(tracks, partial, other, both, mean, seq_count):
    chunk = partial.shape[0]
    vmem = pl.BlockSpec(memory_space=pltpu.VMEM)
    return pl.pallas_call(
        error_kernel,
        in_specs=[pl.BlockSpec(memory_space=pltpu.SMEM), vmem, vmem, vmem, vmem],
        out_shape=jax.ShapeDtypeStruct((SIDE, 2 * chunk, mean.shape[1]), jnp.bfloat16),
        scratch_shapes=[pltpu.VMEM((seq_count, 8, 128), jnp.float32)],
        compiler_params=pltpu.CompilerParams(vmem_limit_bytes=VMEM_BYTES),
        name="error_messages",
    )(tracks, partial, other, both, mean)


def relay_kernel(in_ref, out_ref):
    chunk, width = in_ref.shape[1] // 2, in_ref.shape[2]
    for z in range(SIDE):
        span = slice(z * chunk, z * chunk + chunk)
        grad = in_ref[z, :chunk]
        errors = in_ref[z, chunk:].astype(jnp.float32)
        for g in range(SIDE):
            tile = errors[:, g // 4 * 128 : g // 4 * 128 + 128]
            tile = pltpu.roll(tile, 128 - g % 4 * 32, 1) if g % 4 else tile
            out_ref[g, span, :width] = grad
            out_ref[g, span, width:] = tile.astype(jnp.bfloat16)


def relay(x):
    chunk, width = x.shape[1] // 2, x.shape[2]
    return pl.pallas_call(
        relay_kernel,
        out_shape=jax.ShapeDtypeStruct((SIDE, SIDE * chunk, width + 128), jnp.bfloat16),
        compiler_params=pltpu.CompilerParams(vmem_limit_bytes=VMEM_BYTES),
        name="relay",
    )(x)


def finish_kernel(index_ref, final_ref, weight_ref, sel_ref, divisor_ref, grad_ref, context_ref):
    width = weight_ref.shape[0]
    back = sel_ref.shape[0]
    for i in range(final_ref.shape[0] // width):
        span = slice(i * width, i * width + width)
        grad_ref[:, span] = final_ref[span, :width].T
    mean_grad = jnp.dot(
        weight_ref[...], final_ref[:, width:], preferred_element_type=jnp.float32
    ).T[:back]
    track_grad = (mean_grad / divisor_ref[:, :1]).astype(jnp.bfloat16)
    context_ref[...] = lax.dot_general(
        sel_ref[...], track_grad, (((0,), (0,)), ((), ())), preferred_element_type=jnp.float32
    ).astype(jnp.bfloat16)


def finish(index, final, weight, sel, divisor):
    width, target_d = weight.shape
    back, tok_rows = sel.shape
    whole = lambda *shape: pl.BlockSpec(shape, lambda i, at: (0, 0))
    return pl.pallas_call(
        finish_kernel,
        grid_spec=pltpu.PrefetchScalarGridSpec(
            num_scalar_prefetch=1,
            grid=(1,),
            in_specs=[
                whole(*final.shape),
                whole(*weight.shape),
                whole(*sel.shape),
                pl.BlockSpec((back, 128), lambda i, at: (at[0], 0)),
            ],
            out_specs=[whole(width, target_d), whole(tok_rows, width)],
        ),
        out_shape=[
            jax.ShapeDtypeStruct((width, target_d), jnp.bfloat16),
            jax.ShapeDtypeStruct((tok_rows, width), jnp.bfloat16),
        ],
        compiler_params=pltpu.CompilerParams(vmem_limit_bytes=VMEM_BYTES),
        name="finish",
    )(index, final, weight, sel, divisor)


def local(queries, keys, values, residual, reg_weight, targets, block_track, row_count, pool_slot):
    tok_rows, width = queries.shape
    seq_count = lax.axis_size("seq")
    index = lax.axis_index("seq").astype(jnp.int32).reshape(1)
    owned, pool, target_d = targets.shape

    pieces = gather_ring(jnp.concatenate([keys, values], axis=0), seq_count)
    query_all = spread(queries, GROUP_YX).reshape(SIDE * tok_rows, width)
    carried, selector, slot_rows = prepare(
        row_count, pool_slot, targets.reshape(owned * pool, target_d)
    )

    part = attend(query_all, pieces, carried, slot_rows)
    part, index = lax.optimization_barrier((part, index))
    part = lax.all_to_all(part, "seq", 0, 0, axis_index_groups=GROUP_YX)
    both = merge(part, residual, selector)
    both = lax.all_to_all(both, "seq", 0, 0, axis_index_groups=GROUP_Z)
    back = selector.shape[0]
    pooled = both[:, :back].reshape(SIDE * back, width)
    every = spread(pooled, GROUP_YX)
    mean, partial, divisor = track_means(
        block_track, index, every, both, reg_weight, target_d // seq_count
    )
    core_mate = lax.ppermute(partial, "head", [(0, 1), (1, 0), (2, 3), (3, 2)])
    partial = (partial.astype(jnp.float32) + core_mate.astype(jnp.float32)).astype(jnp.bfloat16)
    other = lax.ppermute(partial, "head", [(0, 2), (2, 0), (1, 3), (3, 1)])
    final = error_messages(block_track, partial, other, both, mean, seq_count)
    final = lax.all_to_all(final, "seq", 0, 0, axis_index_groups=GROUP_Z)
    final = lax.all_to_all(relay(final), "seq", 0, 0, axis_index_groups=GROUP_YX)
    return finish(index, final.reshape(target_d, width + 128), reg_weight, selector, divisor)


def solution(mesh):
    return jax.shard_map(
        local,
        mesh=mesh,
        in_specs=(
            P("seq", "head"),
            P("seq", "head"),
            P("seq", "head"),
            P("seq", "head"),
            P("head", None),
            P("seq", None, None),
            P(),
            P("seq"),
            P("seq", None),
        ),
        out_specs=(P("head", None), P("seq", "head")),
        check_vma=False,
    )
```

```python
import functools

import jax
import jax.numpy as jnp
from jax import lax
from jax.experimental import pallas as pl
from jax.experimental.pallas import tpu as pltpu
from jax.sharding import PartitionSpec as P

HEAD_DIM = 64
BLK = 128
POOL = 16
SIDE = 8
LOG2E = 1.4426950408889634
STAT = 16
EARLIER = 32768.0
VMEM_BYTES = 24 * 1024 * 1024

GROUP_Z = [[g * SIDE + i for i in range(SIDE)] for g in range(SIDE)]
GROUP_YX = [[g * SIDE + i for g in range(SIDE)] for i in range(SIDE)]


def spread(x, groups):
    wide = jnp.broadcast_to(x[None], (SIDE, *x.shape))
    return lax.all_to_all(wide, "seq", 0, 0, axis_index_groups=groups)


def ring(seq_count, step):
    return [
        (g * SIDE + i, g * SIDE + (i + step) % SIDE)
        for g in range(seq_count // SIDE)
        for i in range(SIDE)
    ]


def gather_ring(x, seq_count):
    pieces, up, down = [x], x, x
    for _ in range(SIDE // 2 - 1):
        up = lax.ppermute(up, "seq", ring(seq_count, 1))
        down = lax.ppermute(down, "seq", ring(seq_count, -1))
        pieces += [up, down]
    half = x.shape[0] // 2
    far_keys = lax.ppermute(up[:half], "seq", ring(seq_count, 1))
    far_values = lax.ppermute(down[half:], "seq", ring(seq_count, -1))
    return pieces + [far_keys, far_values]


def prepare_kernel(row_count_ref, slot_ref, target_ref, carried_ref, sel_ref, count_ref):
    here = slot_ref.shape[0]
    slots = slot_ref[...]
    sub = lax.broadcasted_iota(jnp.int32, (POOL, BLK), 0)
    lane = lax.broadcasted_iota(jnp.int32, (POOL, BLK), 1)
    zero = jnp.zeros((POOL, BLK), jnp.float32)
    picks = []
    for b in range(here):
        hit = (slots[b : b + 1] == sub) & (lane < row_count_ref[b])
        hit = jnp.where(hit, 1.0, 0.0)
        picks.append(jnp.concatenate([hit if i == b else zero for i in range(here)], axis=1))
    sel = jnp.concatenate(picks, axis=0)
    sel_ref[...] = sel.astype(jnp.bfloat16)
    counts = jnp.broadcast_to(jnp.sum(sel, axis=1, keepdims=True), (sel.shape[0], 128))
    counts = jnp.concatenate(
        [counts, jnp.zeros((128 - counts.shape[0], 128), jnp.float32)], axis=0
    )
    count_ref[...] = counts.T[:1]
    rows = target_ref.shape[0]
    blank = jnp.zeros((128 - rows, 128), jnp.float32)
    for g in range(SIDE):
        tile = target_ref[:, g * 128 : g * 128 + 128].astype(jnp.float32)
        tile = jnp.concatenate([tile, blank], axis=0).T
        eights = [
            tile[z * 16 : z * 16 + 8] + pltpu.roll(tile[z * 16 + 8 : z * 16 + 16], 64, 1)
            for z in range(SIDE)
        ]
        carried_ref[g] = jnp.concatenate(
            [jnp.concatenate(eights[:4], axis=0), jnp.concatenate(eights[4:], axis=0)], axis=1
        ).astype(jnp.bfloat16)


def prepare(row_count, pool_slot, targets):
    here = pool_slot.shape[0]
    vmem = pl.BlockSpec(memory_space=pltpu.VMEM)
    return pl.pallas_call(
        prepare_kernel,
        in_specs=[pl.BlockSpec(memory_space=pltpu.SMEM), vmem, vmem],
        out_shape=[
            jax.ShapeDtypeStruct((SIDE, 32, 256), jnp.bfloat16),
            jax.ShapeDtypeStruct((here * POOL, here * BLK), jnp.bfloat16),
            jax.ShapeDtypeStruct((1, 128), jnp.float32),
        ],
        compiler_params=pltpu.CompilerParams(vmem_limit_bytes=VMEM_BYTES),
        name="prepare",
    )(row_count, pool_slot, targets)


def attend_kernel(q_ref, piece_ref, count_ref, *refs):
    kv_refs, (o_ref, k_own, v_own) = refs[:-3], refs[-3:]
    rows = q_ref.shape[0] // o_ref.shape[0]
    lane = lax.broadcasted_iota(jnp.int32, (1, 128), 1)
    first = lane < HEAD_DIM

    @pl.when(pl.program_id(1) == 0)
    def _():
        zero = jnp.zeros((), jnp.bfloat16)
        one = jnp.ones((), jnp.bfloat16)
        n = kv_refs[-1].shape[0]
        pairs = [(ref[:n], ref[n:]) for ref in kv_refs[:-2]]
        for i, (k, v) in enumerate(pairs + [(kv_refs[-2][...], kv_refs[-1][...])]):
            span = pl.ds(i * n, n)
            k_own[0, :, span] = jnp.where(first, k, zero).T
            k_own[1, :, span] = jnp.where(first, zero, k).T
            v_own[0, span] = jnp.where(first, v, one)
            v_own[1, span] = jnp.where(first, one, v)

    scale = LOG2E * HEAD_DIM ** (-0.5)
    q = q_ref[...]
    scores = [jnp.dot(q, k_own[h], preferred_element_type=jnp.float32) for h in range(2)]
    tops = [jnp.max(s, axis=1, keepdims=True) for s in scores]
    weights = [
        jnp.exp2((s - top) * scale).astype(jnp.bfloat16) for s, top in zip(scores, tops)
    ]
    sums = [
        jnp.dot(w, v_own[h], preferred_element_type=jnp.float32) for h, w in enumerate(weights)
    ]
    num = jnp.where(first, sums[0], sums[1])
    den_other = jnp.where(first, sums[1], sums[0])
    den = pltpu.roll(den_other, HEAD_DIM, 1)
    context = (num / den).astype(jnp.bfloat16)
    lse = jnp.where(first, tops[1], tops[0]) * scale + jnp.log2(den_other)
    pad = jnp.concatenate([count_ref[...], jnp.zeros((3, 128), jnp.float32)], axis=0)
    for i in range(o_ref.shape[0]):
        span = slice(i * rows, i * rows + rows)
        turned = lse[span].T
        left = jnp.concatenate([turned[HEAD_DIM : HEAD_DIM + 1], turned[0:1]], axis=0)
        left = jnp.concatenate([left[:, :128], left[:, 128:]], axis=0)
        hi = left.astype(jnp.bfloat16)
        rest = left - hi.astype(jnp.float32)
        mid = rest.astype(jnp.bfloat16)
        rest = rest - mid.astype(jnp.float32)
        o_ref[i, :rows] = context[span]
        o_ref[i, rows : rows + STAT] = jnp.concatenate(
            [hi.astype(jnp.float32), mid.astype(jnp.float32), rest, pad], axis=0
        ).astype(jnp.bfloat16)
        o_ref[i, rows + STAT :] = piece_ref[i]


def attend(queries, pieces, carried, counts):
    n, width = queries.shape
    rows = n // SIDE
    keys_n = sum(x.shape[0] for x in pieces) // 2
    pairs = width // 128
    out_rows = rows + STAT + carried.shape[1]
    return pl.pallas_call(
        attend_kernel,
        grid=(pairs, SIDE // 2),
        in_specs=[
            pl.BlockSpec((2 * rows, 128), lambda p, i: (i, p)),
            pl.BlockSpec((2, carried.shape[1], 128), lambda p, i: (i, 0, p)),
            pl.BlockSpec(counts.shape, lambda p, i: (0, 0)),
        ]
        + [pl.BlockSpec((x.shape[0], 128), lambda p, i: (0, p)) for x in pieces],
        out_specs=pl.BlockSpec((2, out_rows, 128), lambda p, i: (i, 0, p)),
        out_shape=jax.ShapeDtypeStruct((SIDE, out_rows, width), jnp.bfloat16),
        scratch_shapes=[
            pltpu.VMEM((2, 128, keys_n), jnp.bfloat16),
            pltpu.VMEM((2, keys_n, 128), jnp.bfloat16),
        ],
        compiler_params=pltpu.CompilerParams(vmem_limit_bytes=40 * 1024 * 1024),
        name="attend",
    )(queries, carried, counts, *pieces)


def merge_kernel(part_ref, residual_ref, sel_ref, out_ref):
    rows, width = residual_ref.shape
    lane = lax.broadcasted_iota(jnp.int32, (1, 128), 1)
    first = lane < HEAD_DIM
    stats = part_ref[:, rows : rows + STAT].astype(jnp.float32)
    merged = stats[:, 0:4] + stats[:, 4:8] + stats[:, 8:12]
    scaled = []
    for p in range(width // 128):
        cols = slice(p * 128, p * 128 + 128)
        for h in range(2):
            x = jnp.concatenate([merged[:, h, cols], merged[:, 2 + h, cols]], axis=1)
            w = jnp.exp2(x - jnp.max(x, axis=0, keepdims=True))
            scaled.append(w / jnp.sum(w, axis=0, keepdims=True))
    weights = jnp.concatenate(scaled, axis=0)
    weights = jnp.concatenate(
        [weights, jnp.zeros((128 - weights.shape[0], rows), jnp.float32)], axis=0
    ).T
    streams = []
    for p in range(width // 128):
        cols = slice(p * 128, p * 128 + 128)
        total = jnp.zeros((rows, 128), jnp.float32)
        for j in range(SIDE):
            a = (2 * p) * SIDE + j
            b = (2 * p + 1) * SIDE + j
            w = jnp.where(first, weights[:, a : a + 1], weights[:, b : b + 1])
            total = total + w * part_ref[j, :rows, cols].astype(jnp.float32)
        context = total.astype(jnp.bfloat16).astype(jnp.float32)
        streams.append(
            (residual_ref[:, cols].astype(jnp.float32) + context).astype(jnp.bfloat16)
        )
    stream = jnp.concatenate(streams, axis=1)
    pooled = jnp.dot(sel_ref[...], stream, preferred_element_type=jnp.float32).astype(jnp.bfloat16)
    back = sel_ref.shape[0]
    for j in range(SIDE):
        out_ref[j, :back] = pooled

    carried = part_ref[:, rows + STAT :].astype(jnp.float32)
    counts = stats[:, 12:13, :128]
    per = 128 // back
    count_tiles = []
    for half in range(SIDE // per):
        tile = jnp.zeros((1, 128), jnp.float32)
        for q in range(per):
            row = counts[half * per + q]
            row = pltpu.roll(row, q * back, 1) if q else row
            tile = jnp.where(lane // back == q, row, tile)
        count_tiles.append(tile)
    count_row = jnp.concatenate(count_tiles, axis=1)
    tail = jnp.concatenate([count_row, jnp.zeros((15, count_row.shape[1]), jnp.float32)], axis=0)
    for g in range(SIDE):
        span = slice(g % 4 * 8, g % 4 * 8 + 8)
        cols = slice(g // 4 * 128, g // 4 * 128 + 128)
        halves = [
            jnp.concatenate([carried[half * 4 + q, span, cols] for q in range(4)], axis=0)
            for half in range(2)
        ]
        out_ref[g, back:] = jnp.concatenate(
            [jnp.concatenate(halves, axis=1), tail], axis=0
        ).astype(jnp.bfloat16)


def merge(part, residual, sel):
    back, width = sel.shape[0], residual.shape[1]
    return pl.pallas_call(
        merge_kernel,
        out_shape=jax.ShapeDtypeStruct((SIDE, back + 48, width), jnp.bfloat16),
        compiler_params=pltpu.CompilerParams(vmem_limit_bytes=VMEM_BYTES),
        name="merge",
    )(part, residual, sel)


def column(row):
    return jnp.broadcast_to(row, (128, row.shape[1])).T[:, :1]


def track_kernel(
    track_ref,
    index_ref,
    every_ref,
    both_ref,
    weight_ref,
    mean_ref,
    part_ref,
    divisor_ref,
    count_buf,
    id_buf,
    weight_buf,
):
    step = every_ref.shape[1]
    at = pl.program_id(0) * 2

    @pl.when(at == 0)
    def _():
        lane = lax.broadcasted_iota(jnp.int32, (1, 128), 1)
        rows = [
            both_ref[z, both_ref.shape[1] - 16 :].astype(jnp.float32)[:1] for z in range(SIDE)
        ]
        for g in range(SIDE):
            for half in range(2):
                tile = jnp.zeros((1, 128), jnp.float32)
                for q in range(4):
                    row = rows[half * 4 + q][:, g // 4 * 128 : g // 4 * 128 + 128]
                    turn = (q - g % 4) % 4 * 32
                    row = pltpu.roll(row, turn, 1) if turn else row
                    tile = jnp.where(lane // 32 == q, row, tile)
                count_buf[g : g + 1, half * 128 : half * 128 + 128] = tile
                track = jnp.zeros((1, 128), jnp.int32)
                for j in range(8):
                    track = jnp.where(lane // POOL == j, track_ref[g * 16 + half * 8 + j], track)
                id_buf[g : g + 1, half * 128 : half * 128 + 128] = (
                    track * POOL + lane % POOL
                ).astype(jnp.float32)
        weight_buf[...] = weight_ref[...].T

    here = jnp.concatenate([column(id_buf[pl.ds(at + i, 1)]) for i in range(2)], axis=0)
    sums = jnp.zeros(mean_ref.shape, jnp.float32)
    counts = jnp.zeros((2 * step, step), jnp.float32)
    for g in range(SIDE):
        match = here == id_buf[g : g + 1]
        sums = sums + jnp.dot(
            jnp.where(match, 1.0, 0.0).astype(jnp.bfloat16),
            every_ref[g],
            preferred_element_type=jnp.float32,
        )
        seen = count_buf[g : g + 1] + jnp.where(g < at, EARLIER, 0.0)
        counts = counts + jnp.where(match, seen, 0.0)
    below = lax.broadcasted_iota(jnp.int32, (2 * step, step), 0) - lax.broadcasted_iota(
        jnp.int32, (2 * step, step), 1
    )
    for i in range(2):
        match = (here == id_buf[pl.ds(at + i, 1)]) & (below > i * step)
        counts = counts + jnp.where(match, EARLIER, 0.0)
    total = jnp.sum(counts, axis=1, keepdims=True)
    before = jnp.floor(total * (1.0 / EARLIER))
    divisor = jnp.maximum(total - before * EARLIER, 1.0)
    divisor_ref[...] = jnp.broadcast_to(divisor, divisor_ref.shape)
    mean = sums / divisor
    mean_ref[...] = jnp.where(before > 0.0, 0.0, mean).astype(jnp.bfloat16)
    chunk = part_ref.shape[0]
    start = pl.multiple_of(lax.rem(index_ref[0], 128 // chunk) * chunk, chunk)
    part_ref[...] = lax.dot_general(
        weight_buf[pl.ds(start, chunk)],
        mean.astype(jnp.bfloat16),
        (((1,), (1,)), ((), ())),
        preferred_element_type=jnp.float32,
    ).astype(jnp.bfloat16)


def track_means(tracks, index, every, both, weight, chunk):
    step, width = every.shape[1:]
    rows = SIDE * step
    return pl.pallas_call(
        track_kernel,
        grid_spec=pltpu.PrefetchScalarGridSpec(
            num_scalar_prefetch=2,
            grid=(SIDE // 2,),
            in_specs=[
                pl.BlockSpec(every.shape, lambda i, t, at: (0, 0, 0)),
                pl.BlockSpec(both.shape, lambda i, t, at: (0, 0, 0)),
                pl.BlockSpec((width, 128), lambda i, t, at: (0, at[0] // (128 // chunk))),
            ],
            out_specs=[
                pl.BlockSpec((2 * step, width), lambda i, t, at: (i, 0)),
                pl.BlockSpec((chunk, 2 * step), lambda i, t, at: (0, i)),
                pl.BlockSpec((2 * step, 128), lambda i, t, at: (i, 0)),
            ],
            scratch_shapes=[
                pltpu.VMEM((SIDE, step), jnp.float32),
                pltpu.VMEM((SIDE, step), jnp.float32),
                pltpu.VMEM((128, width), jnp.bfloat16),
            ],
        ),
        out_shape=[
            jax.ShapeDtypeStruct((rows, width), jnp.bfloat16),
            jax.ShapeDtypeStruct((chunk, rows), jnp.bfloat16),
            jax.ShapeDtypeStruct((rows, 128), jnp.float32),
        ],
        compiler_params=pltpu.CompilerParams(vmem_limit_bytes=VMEM_BYTES),
        name="track_means",
    )(tracks, index, every, both, weight)


def error_kernel(track_ref, part_ref, other_ref, both_ref, mean_ref, out_ref, target_buf):
    chunk = part_ref.shape[0]
    back = part_ref.shape[1] // target_buf.shape[0]
    for z in range(SIDE):
        carried = both_ref[z, back : back + 32].astype(jnp.float32)
        for g in range(SIDE):
            target_buf[g * SIDE + z] = carried[
                g % 4 * 8 : g % 4 * 8 + 8, g // 4 * 128 : g // 4 * 128 + 128
            ]
    lane = lax.broadcasted_iota(jnp.int32, (8, 128), 1)
    tiles = []
    for group in range(part_ref.shape[1] // 128):
        low = jnp.zeros((8, 128), jnp.float32)
        high = jnp.zeros((8, 128), jnp.float32)
        for j in range(8):
            track = track_ref[group * 8 + j]
            tile = target_buf[track // 4]
            turn = j * POOL + 128 - track % 4 * POOL
            here = lane // POOL == j
            low = jnp.where(here, pltpu.roll(tile, lax.rem(turn, 128), 1), low)
            high = jnp.where(here, pltpu.roll(tile, lax.rem(turn + 64, 128), 1), high)
        tiles.append(jnp.concatenate([low, high], axis=0))
    target = jnp.concatenate(tiles, axis=1)
    total = part_ref[...].astype(jnp.float32) + other_ref[...].astype(jnp.float32)
    error = (total - target).astype(jnp.bfloat16).astype(jnp.float32)
    grad = jnp.dot(
        error.astype(jnp.bfloat16), mean_ref[...], preferred_element_type=jnp.float32
    ).astype(jnp.bfloat16)
    wide = lax.broadcasted_iota(jnp.int32, (chunk, 128), 1)
    for z in range(SIDE):
        out_ref[z, :chunk] = grad
        for half in range(2):
            tile = jnp.zeros((chunk, 128), jnp.float32)
            for q in range(4):
                source = (half * 4 + q) * 2 + z // 4
                row = error[:, source * 128 : source * 128 + 128]
                turn = (q - z % 4) % 4 * 32
                row = pltpu.roll(row, turn, 1) if turn else row
                tile = jnp.where(wide // 32 == q, row, tile)
            out_ref[z, chunk:, half * 128 : half * 128 + 128] = tile.astype(jnp.bfloat16)


def error_messages(tracks, partial, other, both, mean, seq_count):
    chunk = partial.shape[0]
    vmem = pl.BlockSpec(memory_space=pltpu.VMEM)
    return pl.pallas_call(
        error_kernel,
        in_specs=[pl.BlockSpec(memory_space=pltpu.SMEM), vmem, vmem, vmem, vmem],
        out_shape=jax.ShapeDtypeStruct((SIDE, 2 * chunk, mean.shape[1]), jnp.bfloat16),
        scratch_shapes=[pltpu.VMEM((seq_count, 8, 128), jnp.float32)],
        compiler_params=pltpu.CompilerParams(vmem_limit_bytes=VMEM_BYTES),
        name="error_messages",
    )(tracks, partial, other, both, mean)


def relay_kernel(in_ref, out_ref):
    chunk, width = in_ref.shape[1] // 2, in_ref.shape[2]
    for z in range(SIDE):
        span = slice(z * chunk, z * chunk + chunk)
        grad = in_ref[z, :chunk]
        errors = in_ref[z, chunk:].astype(jnp.float32)
        for g in range(SIDE):
            tile = errors[:, g // 4 * 128 : g // 4 * 128 + 128]
            tile = pltpu.roll(tile, 128 - g % 4 * 32, 1) if g % 4 else tile
            out_ref[g, span, :width] = grad
            out_ref[g, span, width:] = tile.astype(jnp.bfloat16)


def relay(x):
    chunk, width = x.shape[1] // 2, x.shape[2]
    return pl.pallas_call(
        relay_kernel,
        out_shape=jax.ShapeDtypeStruct((SIDE, SIDE * chunk, width + 128), jnp.bfloat16),
        compiler_params=pltpu.CompilerParams(vmem_limit_bytes=VMEM_BYTES),
        name="relay",
    )(x)


def finish_kernel(index_ref, final_ref, weight_ref, sel_ref, divisor_ref, grad_ref, context_ref):
    width = weight_ref.shape[0]
    back = sel_ref.shape[0]
    for i in range(final_ref.shape[0] // width):
        span = slice(i * width, i * width + width)
        grad_ref[:, span] = final_ref[span, :width].T
    mean_grad = jnp.dot(
        weight_ref[...], final_ref[:, width:], preferred_element_type=jnp.float32
    ).T[:back]
    track_grad = (mean_grad / divisor_ref[:, :1]).astype(jnp.bfloat16)
    context_ref[...] = lax.dot_general(
        sel_ref[...], track_grad, (((0,), (0,)), ((), ())), preferred_element_type=jnp.float32
    ).astype(jnp.bfloat16)


def finish(index, final, weight, sel, divisor):
    width, target_d = weight.shape
    back, tok_rows = sel.shape
    whole = lambda *shape: pl.BlockSpec(shape, lambda i, at: (0, 0))
    return pl.pallas_call(
        finish_kernel,
        grid_spec=pltpu.PrefetchScalarGridSpec(
            num_scalar_prefetch=1,
            grid=(1,),
            in_specs=[
                whole(*final.shape),
                whole(*weight.shape),
                whole(*sel.shape),
                pl.BlockSpec((back, 128), lambda i, at: (at[0], 0)),
            ],
            out_specs=[whole(width, target_d), whole(tok_rows, width)],
        ),
        out_shape=[
            jax.ShapeDtypeStruct((width, target_d), jnp.bfloat16),
            jax.ShapeDtypeStruct((tok_rows, width), jnp.bfloat16),
        ],
        compiler_params=pltpu.CompilerParams(vmem_limit_bytes=VMEM_BYTES),
        name="finish",
    )(index, final, weight, sel, divisor)


def local(queries, keys, values, residual, reg_weight, targets, block_track, row_count, pool_slot):
    tok_rows, width = queries.shape
    seq_count = lax.axis_size("seq")
    index = lax.axis_index("seq").astype(jnp.int32).reshape(1)
    owned, pool, target_d = targets.shape

    pieces = gather_ring(jnp.concatenate([keys, values], axis=0), seq_count)
    query_all = spread(queries, GROUP_YX).reshape(SIDE * tok_rows, width)
    carried, selector, slot_rows = prepare(
        row_count, pool_slot, targets.reshape(owned * pool, target_d)
    )

    part = attend(query_all, pieces, carried, slot_rows)
    part, index = lax.optimization_barrier((part, index))
    part = lax.all_to_all(part, "seq", 0, 0, axis_index_groups=GROUP_YX)
    both = merge(part, residual, selector)
    both = lax.all_to_all(both, "seq", 0, 0, axis_index_groups=GROUP_Z)
    back = selector.shape[0]
    pooled = both[:, :back].reshape(SIDE * back, width)
    every = spread(pooled, GROUP_YX)
    mean, partial, divisor = track_means(
        block_track, index, every, both, reg_weight, target_d // seq_count
    )
    core_mate = lax.ppermute(partial, "head", [(0, 1), (1, 0), (2, 3), (3, 2)])
    partial = (partial.astype(jnp.float32) + core_mate.astype(jnp.float32)).astype(jnp.bfloat16)
    other = lax.ppermute(partial, "head", [(0, 2), (2, 0), (1, 3), (3, 1)])
    final = error_messages(block_track, partial, other, both, mean, seq_count)
    final = lax.all_to_all(final, "seq", 0, 0, axis_index_groups=GROUP_Z)
    final = lax.all_to_all(relay(final), "seq", 0, 0, axis_index_groups=GROUP_YX)
    return finish(index, final.reshape(target_d, width + 128), reg_weight, selector, divisor)


def solution(mesh):
    return jax.shard_map(
        local,
        mesh=mesh,
        in_specs=(
            P("seq", "head"),
            P("seq", "head"),
            P("seq", "head"),
            P("seq", "head"),
            P("head", None),
            P("seq", None, None),
            P(),
            P("seq"),
            P("seq", None),
        ),
        out_specs=(P("head", None), P("seq", "head")),
        check_vma=False,
    )
```

```python
import functools

import jax
import jax.numpy as jnp
from jax import lax
from jax.experimental import pallas as pl
from jax.experimental.pallas import tpu as pltpu
from jax.sharding import PartitionSpec as P

HEAD_DIM = 64
BLK = 128
POOL = 16
SIDE = 8
LOG2E = 1.4426950408889634
STAT = 16
EARLIER = 32768.0
VMEM_BYTES = 24 * 1024 * 1024

GROUP_Z = [[g * SIDE + i for i in range(SIDE)] for g in range(SIDE)]
GROUP_YX = [[g * SIDE + i for g in range(SIDE)] for i in range(SIDE)]


def spread(x, groups):
    wide = jnp.broadcast_to(x[None], (SIDE, *x.shape))
    return lax.all_to_all(wide, "seq", 0, 0, axis_index_groups=groups)


def ring(seq_count, step):
    return [
        (g * SIDE + i, g * SIDE + (i + step) % SIDE)
        for g in range(seq_count // SIDE)
        for i in range(SIDE)
    ]


def gather_ring(x, seq_count):
    pieces, up, down = [x], x, x
    for _ in range(SIDE // 2 - 1):
        up = lax.ppermute(up, "seq", ring(seq_count, 1))
        down = lax.ppermute(down, "seq", ring(seq_count, -1))
        pieces += [up, down]
    half = x.shape[0] // 2
    far_keys = lax.ppermute(up[:half], "seq", ring(seq_count, 1))
    far_values = lax.ppermute(down[half:], "seq", ring(seq_count, -1))
    return pieces + [far_keys, far_values]


def lay_out_kernel(k_ref, v_ref, q_ref, kv_ref, wide_ref, sems):
    n = k_ref.shape[0]
    copies = [
        pltpu.make_async_copy(k_ref, kv_ref.at[pl.ds(0, n)], sems.at[0]),
        pltpu.make_async_copy(v_ref, kv_ref.at[pl.ds(n, n)], sems.at[1]),
    ]
    for i in range(SIDE):
        copies.append(pltpu.make_async_copy(q_ref, wide_ref.at[i], sems.at[2 + i]))
    for copy in copies:
        copy.start()
    for copy in copies:
        copy.wait()


def lay_out(keys, values, queries):
    n, width = keys.shape
    anywhere = pl.BlockSpec(memory_space=pl.ANY)
    return pl.pallas_call(
        lay_out_kernel,
        in_specs=[anywhere] * 3,
        out_specs=[anywhere] * 2,
        out_shape=[
            jax.ShapeDtypeStruct((2 * n, width), keys.dtype),
            jax.ShapeDtypeStruct((SIDE, n, width), queries.dtype),
        ],
        scratch_shapes=[pltpu.SemaphoreType.DMA((2 + SIDE,))],
        compiler_params=pltpu.CompilerParams(vmem_limit_bytes=60 * 1024 * 1024),
        name="lay_out",
    )(keys, values, queries)


def prepare_kernel(row_count_ref, slot_ref, target_ref, carried_ref, sel_ref, count_ref):
    here = slot_ref.shape[0]
    slots = slot_ref[...]
    sub = lax.broadcasted_iota(jnp.int32, (POOL, BLK), 0)
    lane = lax.broadcasted_iota(jnp.int32, (POOL, BLK), 1)
    zero = jnp.zeros((POOL, BLK), jnp.float32)
    picks = []
    for b in range(here):
        hit = (slots[b : b + 1] == sub) & (lane < row_count_ref[b])
        hit = jnp.where(hit, 1.0, 0.0)
        picks.append(jnp.concatenate([hit if i == b else zero for i in range(here)], axis=1))
    sel = jnp.concatenate(picks, axis=0)
    sel_ref[...] = sel.astype(jnp.bfloat16)
    counts = jnp.broadcast_to(jnp.sum(sel, axis=1, keepdims=True), (sel.shape[0], 128))
    counts = jnp.concatenate(
        [counts, jnp.zeros((128 - counts.shape[0], 128), jnp.float32)], axis=0
    )
    count_ref[...] = counts.T[:1]
    rows = target_ref.shape[0]
    blank = jnp.zeros((128 - rows, 128), jnp.float32)
    for g in range(SIDE):
        tile = target_ref[:, g * 128 : g * 128 + 128].astype(jnp.float32)
        tile = jnp.concatenate([tile, blank], axis=0).T
        eights = [
            tile[z * 16 : z * 16 + 8] + pltpu.roll(tile[z * 16 + 8 : z * 16 + 16], 64, 1)
            for z in range(SIDE)
        ]
        carried_ref[g] = jnp.concatenate(
            [jnp.concatenate(eights[:4], axis=0), jnp.concatenate(eights[4:], axis=0)], axis=1
        ).astype(jnp.bfloat16)


def prepare(row_count, pool_slot, targets):
    here = pool_slot.shape[0]
    vmem = pl.BlockSpec(memory_space=pltpu.VMEM)
    return pl.pallas_call(
        prepare_kernel,
        in_specs=[pl.BlockSpec(memory_space=pltpu.SMEM), vmem, vmem],
        out_shape=[
            jax.ShapeDtypeStruct((SIDE, 32, 256), jnp.bfloat16),
            jax.ShapeDtypeStruct((here * POOL, here * BLK), jnp.bfloat16),
            jax.ShapeDtypeStruct((1, 128), jnp.float32),
        ],
        compiler_params=pltpu.CompilerParams(vmem_limit_bytes=VMEM_BYTES),
        name="prepare",
    )(row_count, pool_slot, targets)


def attend_kernel(q_ref, piece_ref, count_ref, *refs):
    kv_refs, (o_ref, k_own, v_own) = refs[:-3], refs[-3:]
    rows = q_ref.shape[0] // o_ref.shape[0]
    lane = lax.broadcasted_iota(jnp.int32, (1, 128), 1)
    first = lane < HEAD_DIM

    @pl.when(pl.program_id(1) == 0)
    def _():
        zero = jnp.zeros((), jnp.bfloat16)
        one = jnp.ones((), jnp.bfloat16)
        n = kv_refs[-1].shape[0]
        pairs = [(ref[:n], ref[n:]) for ref in kv_refs[:-2]]
        for i, (k, v) in enumerate(pairs + [(kv_refs[-2][...], kv_refs[-1][...])]):
            span = pl.ds(i * n, n)
            k_own[0, :, span] = jnp.where(first, k, zero).T
            k_own[1, :, span] = jnp.where(first, zero, k).T
            v_own[0, span] = jnp.where(first, v, one)
            v_own[1, span] = jnp.where(first, one, v)

    scale = LOG2E * HEAD_DIM ** (-0.5)
    q = q_ref[...]
    scores = [jnp.dot(q, k_own[h], preferred_element_type=jnp.float32) for h in range(2)]
    tops = [jnp.max(s, axis=1, keepdims=True) for s in scores]
    weights = [
        jnp.exp2((s - top) * scale).astype(jnp.bfloat16) for s, top in zip(scores, tops)
    ]
    sums = [
        jnp.dot(w, v_own[h], preferred_element_type=jnp.float32) for h, w in enumerate(weights)
    ]
    num = jnp.where(first, sums[0], sums[1])
    den_other = jnp.where(first, sums[1], sums[0])
    den = pltpu.roll(den_other, HEAD_DIM, 1)
    context = (num / den).astype(jnp.bfloat16)
    lse = jnp.where(first, tops[1], tops[0]) * scale + jnp.log2(den_other)
    pad = jnp.concatenate([count_ref[...], jnp.zeros((3, 128), jnp.float32)], axis=0)
    for i in range(o_ref.shape[0]):
        span = slice(i * rows, i * rows + rows)
        turned = lse[span].T
        left = jnp.concatenate([turned[HEAD_DIM : HEAD_DIM + 1], turned[0:1]], axis=0)
        left = jnp.concatenate([left[:, :128], left[:, 128:]], axis=0)
        hi = left.astype(jnp.bfloat16)
        rest = left - hi.astype(jnp.float32)
        mid = rest.astype(jnp.bfloat16)
        rest = rest - mid.astype(jnp.float32)
        o_ref[i, :rows] = context[span]
        o_ref[i, rows : rows + STAT] = jnp.concatenate(
            [hi.astype(jnp.float32), mid.astype(jnp.float32), rest, pad], axis=0
        ).astype(jnp.bfloat16)
        o_ref[i, rows + STAT :] = piece_ref[i]


def attend(queries, pieces, carried, counts):
    n, width = queries.shape
    rows = n // SIDE
    keys_n = sum(x.shape[0] for x in pieces) // 2
    pairs = width // 128
    out_rows = rows + STAT + carried.shape[1]
    return pl.pallas_call(
        attend_kernel,
        grid=(pairs, SIDE // 2),
        in_specs=[
            pl.BlockSpec((2 * rows, 128), lambda p, i: (i, p)),
            pl.BlockSpec((2, carried.shape[1], 128), lambda p, i: (i, 0, p)),
            pl.BlockSpec(counts.shape, lambda p, i: (0, 0)),
        ]
        + [pl.BlockSpec((x.shape[0], 128), lambda p, i: (0, p)) for x in pieces],
        out_specs=pl.BlockSpec((2, out_rows, 128), lambda p, i: (i, 0, p)),
        out_shape=jax.ShapeDtypeStruct((SIDE, out_rows, width), jnp.bfloat16),
        scratch_shapes=[
            pltpu.VMEM((2, 128, keys_n), jnp.bfloat16),
            pltpu.VMEM((2, keys_n, 128), jnp.bfloat16),
        ],
        compiler_params=pltpu.CompilerParams(vmem_limit_bytes=40 * 1024 * 1024),
        name="attend",
    )(queries, carried, counts, *pieces)


def merge_kernel(part_ref, residual_ref, sel_ref, out_ref):
    rows, width = residual_ref.shape
    lane = lax.broadcasted_iota(jnp.int32, (1, 128), 1)
    first = lane < HEAD_DIM
    stats = part_ref[:, rows : rows + STAT].astype(jnp.float32)
    merged = stats[:, 0:4] + stats[:, 4:8] + stats[:, 8:12]
    scaled = []
    for p in range(width // 128):
        cols = slice(p * 128, p * 128 + 128)
        for h in range(2):
            x = jnp.concatenate([merged[:, h, cols], merged[:, 2 + h, cols]], axis=1)
            w = jnp.exp2(x - jnp.max(x, axis=0, keepdims=True))
            scaled.append(w / jnp.sum(w, axis=0, keepdims=True))
    weights = jnp.concatenate(scaled, axis=0)
    weights = jnp.concatenate(
        [weights, jnp.zeros((128 - weights.shape[0], rows), jnp.float32)], axis=0
    ).T
    streams = []
    for p in range(width // 128):
        cols = slice(p * 128, p * 128 + 128)
        total = jnp.zeros((rows, 128), jnp.float32)
        for j in range(SIDE):
            a = (2 * p) * SIDE + j
            b = (2 * p + 1) * SIDE + j
            w = jnp.where(first, weights[:, a : a + 1], weights[:, b : b + 1])
            total = total + w * part_ref[j, :rows, cols].astype(jnp.float32)
        context = total.astype(jnp.bfloat16).astype(jnp.float32)
        streams.append(
            (residual_ref[:, cols].astype(jnp.float32) + context).astype(jnp.bfloat16)
        )
    stream = jnp.concatenate(streams, axis=1)
    pooled = jnp.dot(sel_ref[...], stream, preferred_element_type=jnp.float32).astype(jnp.bfloat16)
    back = sel_ref.shape[0]
    for j in range(SIDE):
        out_ref[j, :back] = pooled

    carried = part_ref[:, rows + STAT :].astype(jnp.float32)
    counts = stats[:, 12:13, :128]
    per = 128 // back
    count_tiles = []
    for half in range(SIDE // per):
        tile = jnp.zeros((1, 128), jnp.float32)
        for q in range(per):
            row = counts[half * per + q]
            row = pltpu.roll(row, q * back, 1) if q else row
            tile = jnp.where(lane // back == q, row, tile)
        count_tiles.append(tile)
    count_row = jnp.concatenate(count_tiles, axis=1)
    tail = jnp.concatenate([count_row, jnp.zeros((15, count_row.shape[1]), jnp.float32)], axis=0)
    for g in range(SIDE):
        span = slice(g % 4 * 8, g % 4 * 8 + 8)
        cols = slice(g // 4 * 128, g // 4 * 128 + 128)
        halves = [
            jnp.concatenate([carried[half * 4 + q, span, cols] for q in range(4)], axis=0)
            for half in range(2)
        ]
        out_ref[g, back:] = jnp.concatenate(
            [jnp.concatenate(halves, axis=1), tail], axis=0
        ).astype(jnp.bfloat16)


def merge(part, residual, sel):
    back, width = sel.shape[0], residual.shape[1]
    return pl.pallas_call(
        merge_kernel,
        out_shape=jax.ShapeDtypeStruct((SIDE, back + 48, width), jnp.bfloat16),
        compiler_params=pltpu.CompilerParams(vmem_limit_bytes=VMEM_BYTES),
        name="merge",
    )(part, residual, sel)


def column(row):
    return jnp.broadcast_to(row, (128, row.shape[1])).T[:, :1]


def track_kernel(
    track_ref,
    index_ref,
    every_ref,
    both_ref,
    weight_ref,
    mean_ref,
    part_ref,
    divisor_ref,
    count_buf,
    id_buf,
    weight_buf,
):
    step = every_ref.shape[1]
    at = pl.program_id(0) * 2

    @pl.when(at == 0)
    def _():
        lane = lax.broadcasted_iota(jnp.int32, (1, 128), 1)
        rows = [
            both_ref[z, both_ref.shape[1] - 16 :].astype(jnp.float32)[:1] for z in range(SIDE)
        ]
        for g in range(SIDE):
            for half in range(2):
                tile = jnp.zeros((1, 128), jnp.float32)
                for q in range(4):
                    row = rows[half * 4 + q][:, g // 4 * 128 : g // 4 * 128 + 128]
                    turn = (q - g % 4) % 4 * 32
                    row = pltpu.roll(row, turn, 1) if turn else row
                    tile = jnp.where(lane // 32 == q, row, tile)
                count_buf[g : g + 1, half * 128 : half * 128 + 128] = tile
                track = jnp.zeros((1, 128), jnp.int32)
                for j in range(8):
                    track = jnp.where(lane // POOL == j, track_ref[g * 16 + half * 8 + j], track)
                id_buf[g : g + 1, half * 128 : half * 128 + 128] = (
                    track * POOL + lane % POOL
                ).astype(jnp.float32)
        weight_buf[...] = weight_ref[...].T

    here = jnp.concatenate([column(id_buf[pl.ds(at + i, 1)]) for i in range(2)], axis=0)
    sums = jnp.zeros(mean_ref.shape, jnp.float32)
    counts = jnp.zeros((2 * step, step), jnp.float32)
    for g in range(SIDE):
        match = here == id_buf[g : g + 1]
        sums = sums + jnp.dot(
            jnp.where(match, 1.0, 0.0).astype(jnp.bfloat16),
            every_ref[g],
            preferred_element_type=jnp.float32,
        )
        seen = count_buf[g : g + 1] + jnp.where(g < at, EARLIER, 0.0)
        counts = counts + jnp.where(match, seen, 0.0)
    below = lax.broadcasted_iota(jnp.int32, (2 * step, step), 0) - lax.broadcasted_iota(
        jnp.int32, (2 * step, step), 1
    )
    for i in range(2):
        match = (here == id_buf[pl.ds(at + i, 1)]) & (below > i * step)
        counts = counts + jnp.where(match, EARLIER, 0.0)
    total = jnp.sum(counts, axis=1, keepdims=True)
    before = jnp.floor(total * (1.0 / EARLIER))
    divisor = jnp.maximum(total - before * EARLIER, 1.0)
    divisor_ref[...] = jnp.broadcast_to(divisor, divisor_ref.shape)
    mean = sums / divisor
    mean_ref[...] = jnp.where(before > 0.0, 0.0, mean).astype(jnp.bfloat16)
    chunk = part_ref.shape[0]
    start = pl.multiple_of(lax.rem(index_ref[0], 128 // chunk) * chunk, chunk)
    part_ref[...] = lax.dot_general(
        weight_buf[pl.ds(start, chunk)],
        mean.astype(jnp.bfloat16),
        (((1,), (1,)), ((), ())),
        preferred_element_type=jnp.float32,
    ).astype(jnp.bfloat16)


def track_means(tracks, index, every, both, weight, chunk):
    step, width = every.shape[1:]
    rows = SIDE * step
    return pl.pallas_call(
        track_kernel,
        grid_spec=pltpu.PrefetchScalarGridSpec(
            num_scalar_prefetch=2,
            grid=(SIDE // 2,),
            in_specs=[
                pl.BlockSpec(every.shape, lambda i, t, at: (0, 0, 0)),
                pl.BlockSpec(both.shape, lambda i, t, at: (0, 0, 0)),
                pl.BlockSpec((width, 128), lambda i, t, at: (0, at[0] // (128 // chunk))),
            ],
            out_specs=[
                pl.BlockSpec((2 * step, width), lambda i, t, at: (i, 0)),
                pl.BlockSpec((chunk, 2 * step), lambda i, t, at: (0, i)),
                pl.BlockSpec((2 * step, 128), lambda i, t, at: (i, 0)),
            ],
            scratch_shapes=[
                pltpu.VMEM((SIDE, step), jnp.float32),
                pltpu.VMEM((SIDE, step), jnp.float32),
                pltpu.VMEM((128, width), jnp.bfloat16),
            ],
        ),
        out_shape=[
            jax.ShapeDtypeStruct((rows, width), jnp.bfloat16),
            jax.ShapeDtypeStruct((chunk, rows), jnp.bfloat16),
            jax.ShapeDtypeStruct((rows, 128), jnp.float32),
        ],
        compiler_params=pltpu.CompilerParams(vmem_limit_bytes=VMEM_BYTES),
        name="track_means",
    )(tracks, index, every, both, weight)


def error_kernel(track_ref, part_ref, other_ref, both_ref, mean_ref, out_ref, target_buf):
    chunk = part_ref.shape[0]
    back = part_ref.shape[1] // target_buf.shape[0]
    for z in range(SIDE):
        carried = both_ref[z, back : back + 32].astype(jnp.float32)
        for g in range(SIDE):
            target_buf[g * SIDE + z] = carried[
                g % 4 * 8 : g % 4 * 8 + 8, g // 4 * 128 : g // 4 * 128 + 128
            ]
    lane = lax.broadcasted_iota(jnp.int32, (8, 128), 1)
    tiles = []
    for group in range(part_ref.shape[1] // 128):
        low = jnp.zeros((8, 128), jnp.float32)
        high = jnp.zeros((8, 128), jnp.float32)
        for j in range(8):
            track = track_ref[group * 8 + j]
            tile = target_buf[track // 4]
            turn = j * POOL + 128 - track % 4 * POOL
            here = lane // POOL == j
            low = jnp.where(here, pltpu.roll(tile, lax.rem(turn, 128), 1), low)
            high = jnp.where(here, pltpu.roll(tile, lax.rem(turn + 64, 128), 1), high)
        tiles.append(jnp.concatenate([low, high], axis=0))
    target = jnp.concatenate(tiles, axis=1)
    total = part_ref[...].astype(jnp.float32) + other_ref[...].astype(jnp.float32)
    error = (total - target).astype(jnp.bfloat16).astype(jnp.float32)
    grad = jnp.dot(
        error.astype(jnp.bfloat16), mean_ref[...], preferred_element_type=jnp.float32
    ).astype(jnp.bfloat16)
    wide = lax.broadcasted_iota(jnp.int32, (chunk, 128), 1)
    for z in range(SIDE):
        out_ref[z, :chunk] = grad
        for half in range(2):
            tile = jnp.zeros((chunk, 128), jnp.float32)
            for q in range(4):
                source = (half * 4 + q) * 2 + z // 4
                row = error[:, source * 128 : source * 128 + 128]
                turn = (q - z % 4) % 4 * 32
                row = pltpu.roll(row, turn, 1) if turn else row
                tile = jnp.where(wide // 32 == q, row, tile)
            out_ref[z, chunk:, half * 128 : half * 128 + 128] = tile.astype(jnp.bfloat16)


def error_messages(tracks, partial, other, both, mean, seq_count):
    chunk = partial.shape[0]
    vmem = pl.BlockSpec(memory_space=pltpu.VMEM)
    return pl.pallas_call(
        error_kernel,
        in_specs=[pl.BlockSpec(memory_space=pltpu.SMEM), vmem, vmem, vmem, vmem],
        out_shape=jax.ShapeDtypeStruct((SIDE, 2 * chunk, mean.shape[1]), jnp.bfloat16),
        scratch_shapes=[pltpu.VMEM((seq_count, 8, 128), jnp.float32)],
        compiler_params=pltpu.CompilerParams(vmem_limit_bytes=VMEM_BYTES),
        name="error_messages",
    )(tracks, partial, other, both, mean)


def relay_kernel(in_ref, out_ref):
    chunk, width = in_ref.shape[1] // 2, in_ref.shape[2]
    for z in range(SIDE):
        span = slice(z * chunk, z * chunk + chunk)
        grad = in_ref[z, :chunk]
        errors = in_ref[z, chunk:].astype(jnp.float32)
        for g in range(SIDE):
            tile = errors[:, g // 4 * 128 : g // 4 * 128 + 128]
            tile = pltpu.roll(tile, 128 - g % 4 * 32, 1) if g % 4 else tile
            out_ref[g, span, :width] = grad
            out_ref[g, span, width:] = tile.astype(jnp.bfloat16)


def relay(x):
    chunk, width = x.shape[1] // 2, x.shape[2]
    return pl.pallas_call(
        relay_kernel,
        out_shape=jax.ShapeDtypeStruct((SIDE, SIDE * chunk, width + 128), jnp.bfloat16),
        compiler_params=pltpu.CompilerParams(vmem_limit_bytes=VMEM_BYTES),
        name="relay",
    )(x)


def finish_kernel(index_ref, final_ref, weight_ref, sel_ref, divisor_ref, grad_ref, context_ref):
    width = weight_ref.shape[0]
    back = sel_ref.shape[0]
    for i in range(final_ref.shape[0] // width):
        span = slice(i * width, i * width + width)
        grad_ref[:, span] = final_ref[span, :width].T
    mean_grad = jnp.dot(
        weight_ref[...], final_ref[:, width:], preferred_element_type=jnp.float32
    ).T[:back]
    track_grad = (mean_grad / divisor_ref[:, :1]).astype(jnp.bfloat16)
    context_ref[...] = lax.dot_general(
        sel_ref[...], track_grad, (((0,), (0,)), ((), ())), preferred_element_type=jnp.float32
    ).astype(jnp.bfloat16)


def finish(index, final, weight, sel, divisor):
    width, target_d = weight.shape
    back, tok_rows = sel.shape
    whole = lambda *shape: pl.BlockSpec(shape, lambda i, at: (0, 0))
    return pl.pallas_call(
        finish_kernel,
        grid_spec=pltpu.PrefetchScalarGridSpec(
            num_scalar_prefetch=1,
            grid=(1,),
            in_specs=[
                whole(*final.shape),
                whole(*weight.shape),
                whole(*sel.shape),
                pl.BlockSpec((back, 128), lambda i, at: (at[0], 0)),
            ],
            out_specs=[whole(width, target_d), whole(tok_rows, width)],
        ),
        out_shape=[
            jax.ShapeDtypeStruct((width, target_d), jnp.bfloat16),
            jax.ShapeDtypeStruct((tok_rows, width), jnp.bfloat16),
        ],
        compiler_params=pltpu.CompilerParams(vmem_limit_bytes=VMEM_BYTES),
        name="finish",
    )(index, final, weight, sel, divisor)


def local(queries, keys, values, residual, reg_weight, targets, block_track, row_count, pool_slot):
    tok_rows, width = queries.shape
    seq_count = lax.axis_size("seq")
    index = lax.axis_index("seq").astype(jnp.int32).reshape(1)
    owned, pool, target_d = targets.shape

    own_kv, wide = lay_out(keys, values, queries)
    pieces = gather_ring(own_kv, seq_count)
    query_all = lax.all_to_all(wide, "seq", 0, 0, axis_index_groups=GROUP_YX)
    query_all = query_all.reshape(SIDE * tok_rows, width)
    carried, selector, slot_rows = prepare(
        row_count, pool_slot, targets.reshape(owned * pool, target_d)
    )

    part = attend(query_all, pieces, carried, slot_rows)
    part, index = lax.optimization_barrier((part, index))
    part = lax.all_to_all(part, "seq", 0, 0, axis_index_groups=GROUP_YX)
    both = merge(part, residual, selector)
    both = lax.all_to_all(both, "seq", 0, 0, axis_index_groups=GROUP_Z)
    back = selector.shape[0]
    pooled = both[:, :back].reshape(SIDE * back, width)
    every = spread(pooled, GROUP_YX)
    mean, partial, divisor = track_means(
        block_track, index, every, both, reg_weight, target_d // seq_count
    )
    core_mate = lax.ppermute(partial, "head", [(0, 1), (1, 0), (2, 3), (3, 2)])
    partial = (partial.astype(jnp.float32) + core_mate.astype(jnp.float32)).astype(jnp.bfloat16)
    other = lax.ppermute(partial, "head", [(0, 2), (2, 0), (1, 3), (3, 1)])
    final = error_messages(block_track, partial, other, both, mean, seq_count)
    final = lax.all_to_all(final, "seq", 0, 0, axis_index_groups=GROUP_Z)
    final = lax.all_to_all(relay(final), "seq", 0, 0, axis_index_groups=GROUP_YX)
    return finish(index, final.reshape(target_d, width + 128), reg_weight, selector, divisor)


def solution(mesh):
    return jax.shard_map(
        local,
        mesh=mesh,
        in_specs=(
            P("seq", "head"),
            P("seq", "head"),
            P("seq", "head"),
            P("seq", "head"),
            P("head", None),
            P("seq", None, None),
            P(),
            P("seq"),
            P("seq", None),
        ),
        out_specs=(P("head", None), P("seq", "head")),
        check_vma=False,
    )
```

```python
import functools

import jax
import jax.numpy as jnp
from jax import lax
from jax.experimental import pallas as pl
from jax.experimental.pallas import tpu as pltpu
from jax.sharding import PartitionSpec as P

HEAD_DIM = 64
BLK = 128
POOL = 16
SIDE = 8
LOG2E = 1.4426950408889634
STAT = 16
EARLIER = 32768.0
VMEM_BYTES = 24 * 1024 * 1024

GROUP_Z = [[g * SIDE + i for i in range(SIDE)] for g in range(SIDE)]
GROUP_YX = [[g * SIDE + i for g in range(SIDE)] for i in range(SIDE)]


def spread(x, groups):
    wide = jnp.broadcast_to(x[None], (SIDE, *x.shape))
    return lax.all_to_all(wide, "seq", 0, 0, axis_index_groups=groups)


def ring(seq_count, step):
    return [
        (g * SIDE + i, g * SIDE + (i + step) % SIDE)
        for g in range(seq_count // SIDE)
        for i in range(SIDE)
    ]


def gather_ring(x, seq_count):
    pieces, up, down = [x], x, x
    for _ in range(SIDE // 2 - 1):
        up = lax.ppermute(up, "seq", ring(seq_count, 1))
        down = lax.ppermute(down, "seq", ring(seq_count, -1))
        pieces += [up, down]
    half = x.shape[0] // 2
    far_keys = lax.ppermute(up[:half], "seq", ring(seq_count, 1))
    far_values = lax.ppermute(down[half:], "seq", ring(seq_count, -1))
    return pieces + [far_keys, far_values]


def lay_out_kernel(k_ref, v_ref, q_ref, kv_ref, wide_ref, sems):
    n = k_ref.shape[0]
    copies = [
        pltpu.make_async_copy(k_ref, kv_ref.at[pl.ds(0, n)], sems.at[0]),
        pltpu.make_async_copy(v_ref, kv_ref.at[pl.ds(n, n)], sems.at[1]),
    ]
    for i in range(SIDE):
        copies.append(pltpu.make_async_copy(q_ref, wide_ref.at[i], sems.at[2 + i]))
    for copy in copies:
        copy.start()
    for copy in copies:
        copy.wait()


def lay_out(keys, values, queries):
    n, width = keys.shape
    anywhere = pl.BlockSpec(memory_space=pl.ANY)
    return pl.pallas_call(
        lay_out_kernel,
        in_specs=[pl.BlockSpec(memory_space=pltpu.VMEM)] * 3,
        out_specs=[anywhere] * 2,
        out_shape=[
            jax.ShapeDtypeStruct((2 * n, width), keys.dtype),
            jax.ShapeDtypeStruct((SIDE, n, width), queries.dtype),
        ],
        scratch_shapes=[pltpu.SemaphoreType.DMA((2 + SIDE,))],
        compiler_params=pltpu.CompilerParams(vmem_limit_bytes=60 * 1024 * 1024),
        name="lay_out",
    )(keys, values, queries)


def prepare_kernel(row_count_ref, slot_ref, target_ref, carried_ref, sel_ref, count_ref):
    here = slot_ref.shape[0]
    slots = slot_ref[...]
    sub = lax.broadcasted_iota(jnp.int32, (POOL, BLK), 0)
    lane = lax.broadcasted_iota(jnp.int32, (POOL, BLK), 1)
    zero = jnp.zeros((POOL, BLK), jnp.float32)
    picks = []
    for b in range(here):
        hit = (slots[b : b + 1] == sub) & (lane < row_count_ref[b])
        hit = jnp.where(hit, 1.0, 0.0)
        picks.append(jnp.concatenate([hit if i == b else zero for i in range(here)], axis=1))
    sel = jnp.concatenate(picks, axis=0)
    sel_ref[...] = sel.astype(jnp.bfloat16)
    counts = jnp.broadcast_to(jnp.sum(sel, axis=1, keepdims=True), (sel.shape[0], 128))
    counts = jnp.concatenate(
        [counts, jnp.zeros((128 - counts.shape[0], 128), jnp.float32)], axis=0
    )
    count_ref[...] = counts.T[:1]
    rows = target_ref.shape[0]
    blank = jnp.zeros((128 - rows, 128), jnp.float32)
    for g in range(SIDE):
        tile = target_ref[:, g * 128 : g * 128 + 128].astype(jnp.float32)
        tile = jnp.concatenate([tile, blank], axis=0).T
        eights = [
            tile[z * 16 : z * 16 + 8] + pltpu.roll(tile[z * 16 + 8 : z * 16 + 16], 64, 1)
            for z in range(SIDE)
        ]
        carried_ref[g] = jnp.concatenate(
            [jnp.concatenate(eights[:4], axis=0), jnp.concatenate(eights[4:], axis=0)], axis=1
        ).astype(jnp.bfloat16)


def prepare(row_count, pool_slot, targets):
    here = pool_slot.shape[0]
    vmem = pl.BlockSpec(memory_space=pltpu.VMEM)
    return pl.pallas_call(
        prepare_kernel,
        in_specs=[pl.BlockSpec(memory_space=pltpu.SMEM), vmem, vmem],
        out_shape=[
            jax.ShapeDtypeStruct((SIDE, 32, 256), jnp.bfloat16),
            jax.ShapeDtypeStruct((here * POOL, here * BLK), jnp.bfloat16),
            jax.ShapeDtypeStruct((1, 128), jnp.float32),
        ],
        compiler_params=pltpu.CompilerParams(vmem_limit_bytes=VMEM_BYTES),
        name="prepare",
    )(row_count, pool_slot, targets)


def attend_kernel(q_ref, piece_ref, count_ref, *refs):
    kv_refs, (o_ref, k_own, v_own) = refs[:-3], refs[-3:]
    rows = q_ref.shape[0] // o_ref.shape[0]
    lane = lax.broadcasted_iota(jnp.int32, (1, 128), 1)
    first = lane < HEAD_DIM

    @pl.when(pl.program_id(1) == 0)
    def _():
        zero = jnp.zeros((), jnp.bfloat16)
        one = jnp.ones((), jnp.bfloat16)
        n = kv_refs[-1].shape[0]
        pairs = [(ref[:n], ref[n:]) for ref in kv_refs[:-2]]
        for i, (k, v) in enumerate(pairs + [(kv_refs[-2][...], kv_refs[-1][...])]):
            span = pl.ds(i * n, n)
            k_own[0, :, span] = jnp.where(first, k, zero).T
            k_own[1, :, span] = jnp.where(first, zero, k).T
            v_own[0, span] = jnp.where(first, v, one)
            v_own[1, span] = jnp.where(first, one, v)

    scale = LOG2E * HEAD_DIM ** (-0.5)
    q = q_ref[...]
    scores = [jnp.dot(q, k_own[h], preferred_element_type=jnp.float32) for h in range(2)]
    tops = [jnp.max(s, axis=1, keepdims=True) for s in scores]
    weights = [
        jnp.exp2((s - top) * scale).astype(jnp.bfloat16) for s, top in zip(scores, tops)
    ]
    sums = [
        jnp.dot(w, v_own[h], preferred_element_type=jnp.float32) for h, w in enumerate(weights)
    ]
    num = jnp.where(first, sums[0], sums[1])
    den_other = jnp.where(first, sums[1], sums[0])
    den = pltpu.roll(den_other, HEAD_DIM, 1)
    context = (num / den).astype(jnp.bfloat16)
    lse = jnp.where(first, tops[1], tops[0]) * scale + jnp.log2(den_other)
    pad = jnp.concatenate([count_ref[...], jnp.zeros((3, 128), jnp.float32)], axis=0)
    for i in range(o_ref.shape[0]):
        span = slice(i * rows, i * rows + rows)
        turned = lse[span].T
        left = jnp.concatenate([turned[HEAD_DIM : HEAD_DIM + 1], turned[0:1]], axis=0)
        left = jnp.concatenate([left[:, :128], left[:, 128:]], axis=0)
        hi = left.astype(jnp.bfloat16)
        rest = left - hi.astype(jnp.float32)
        mid = rest.astype(jnp.bfloat16)
        rest = rest - mid.astype(jnp.float32)
        o_ref[i, :rows] = context[span]
        o_ref[i, rows : rows + STAT] = jnp.concatenate(
            [hi.astype(jnp.float32), mid.astype(jnp.float32), rest, pad], axis=0
        ).astype(jnp.bfloat16)
        o_ref[i, rows + STAT :] = piece_ref[i]


def attend(queries, pieces, carried, counts):
    n, width = queries.shape
    rows = n // SIDE
    keys_n = sum(x.shape[0] for x in pieces) // 2
    pairs = width // 128
    out_rows = rows + STAT + carried.shape[1]
    return pl.pallas_call(
        attend_kernel,
        grid=(pairs, SIDE // 2),
        in_specs=[
            pl.BlockSpec((2 * rows, 128), lambda p, i: (i, p)),
            pl.BlockSpec((2, carried.shape[1], 128), lambda p, i: (i, 0, p)),
            pl.BlockSpec(counts.shape, lambda p, i: (0, 0)),
        ]
        + [pl.BlockSpec((x.shape[0], 128), lambda p, i: (0, p)) for x in pieces],
        out_specs=pl.BlockSpec((2, out_rows, 128), lambda p, i: (i, 0, p)),
        out_shape=jax.ShapeDtypeStruct((SIDE, out_rows, width), jnp.bfloat16),
        scratch_shapes=[
            pltpu.VMEM((2, 128, keys_n), jnp.bfloat16),
            pltpu.VMEM((2, keys_n, 128), jnp.bfloat16),
        ],
        compiler_params=pltpu.CompilerParams(vmem_limit_bytes=40 * 1024 * 1024),
        name="attend",
    )(queries, carried, counts, *pieces)


def merge_kernel(part_ref, residual_ref, sel_ref, out_ref):
    rows, width = residual_ref.shape
    lane = lax.broadcasted_iota(jnp.int32, (1, 128), 1)
    first = lane < HEAD_DIM
    stats = part_ref[:, rows : rows + STAT].astype(jnp.float32)
    merged = stats[:, 0:4] + stats[:, 4:8] + stats[:, 8:12]
    scaled = []
    for p in range(width // 128):
        cols = slice(p * 128, p * 128 + 128)
        for h in range(2):
            x = jnp.concatenate([merged[:, h, cols], merged[:, 2 + h, cols]], axis=1)
            w = jnp.exp2(x - jnp.max(x, axis=0, keepdims=True))
            scaled.append(w / jnp.sum(w, axis=0, keepdims=True))
    weights = jnp.concatenate(scaled, axis=0)
    weights = jnp.concatenate(
        [weights, jnp.zeros((128 - weights.shape[0], rows), jnp.float32)], axis=0
    ).T
    streams = []
    for p in range(width // 128):
        cols = slice(p * 128, p * 128 + 128)
        total = jnp.zeros((rows, 128), jnp.float32)
        for j in range(SIDE):
            a = (2 * p) * SIDE + j
            b = (2 * p + 1) * SIDE + j
            w = jnp.where(first, weights[:, a : a + 1], weights[:, b : b + 1])
            total = total + w * part_ref[j, :rows, cols].astype(jnp.float32)
        context = total.astype(jnp.bfloat16).astype(jnp.float32)
        streams.append(
            (residual_ref[:, cols].astype(jnp.float32) + context).astype(jnp.bfloat16)
        )
    stream = jnp.concatenate(streams, axis=1)
    pooled = jnp.dot(sel_ref[...], stream, preferred_element_type=jnp.float32).astype(jnp.bfloat16)
    back = sel_ref.shape[0]
    for j in range(SIDE):
        out_ref[j, :back] = pooled

    carried = part_ref[:, rows + STAT :].astype(jnp.float32)
    counts = stats[:, 12:13, :128]
    per = 128 // back
    count_tiles = []
    for half in range(SIDE // per):
        tile = jnp.zeros((1, 128), jnp.float32)
        for q in range(per):
            row = counts[half * per + q]
            row = pltpu.roll(row, q * back, 1) if q else row
            tile = jnp.where(lane // back == q, row, tile)
        count_tiles.append(tile)
    count_row = jnp.concatenate(count_tiles, axis=1)
    tail = jnp.concatenate([count_row, jnp.zeros((15, count_row.shape[1]), jnp.float32)], axis=0)
    for g in range(SIDE):
        span = slice(g % 4 * 8, g % 4 * 8 + 8)
        cols = slice(g // 4 * 128, g // 4 * 128 + 128)
        halves = [
            jnp.concatenate([carried[half * 4 + q, span, cols] for q in range(4)], axis=0)
            for half in range(2)
        ]
        out_ref[g, back:] = jnp.concatenate(
            [jnp.concatenate(halves, axis=1), tail], axis=0
        ).astype(jnp.bfloat16)


def merge(part, residual, sel):
    back, width = sel.shape[0], residual.shape[1]
    return pl.pallas_call(
        merge_kernel,
        out_shape=jax.ShapeDtypeStruct((SIDE, back + 48, width), jnp.bfloat16),
        compiler_params=pltpu.CompilerParams(vmem_limit_bytes=VMEM_BYTES),
        name="merge",
    )(part, residual, sel)


def column(row):
    return jnp.broadcast_to(row, (128, row.shape[1])).T[:, :1]


def track_kernel(
    track_ref,
    index_ref,
    every_ref,
    both_ref,
    weight_ref,
    mean_ref,
    part_ref,
    divisor_ref,
    count_buf,
    id_buf,
    weight_buf,
):
    step = every_ref.shape[1]
    at = pl.program_id(0) * 2

    @pl.when(at == 0)
    def _():
        lane = lax.broadcasted_iota(jnp.int32, (1, 128), 1)
        rows = [
            both_ref[z, both_ref.shape[1] - 16 :].astype(jnp.float32)[:1] for z in range(SIDE)
        ]
        for g in range(SIDE):
            for half in range(2):
                tile = jnp.zeros((1, 128), jnp.float32)
                for q in range(4):
                    row = rows[half * 4 + q][:, g // 4 * 128 : g // 4 * 128 + 128]
                    turn = (q - g % 4) % 4 * 32
                    row = pltpu.roll(row, turn, 1) if turn else row
                    tile = jnp.where(lane // 32 == q, row, tile)
                count_buf[g : g + 1, half * 128 : half * 128 + 128] = tile
                track = jnp.zeros((1, 128), jnp.int32)
                for j in range(8):
                    track = jnp.where(lane // POOL == j, track_ref[g * 16 + half * 8 + j], track)
                id_buf[g : g + 1, half * 128 : half * 128 + 128] = (
                    track * POOL + lane % POOL
                ).astype(jnp.float32)
        weight_buf[...] = weight_ref[...].T

    here = jnp.concatenate([column(id_buf[pl.ds(at + i, 1)]) for i in range(2)], axis=0)
    sums = jnp.zeros(mean_ref.shape, jnp.float32)
    counts = jnp.zeros((2 * step, step), jnp.float32)
    for g in range(SIDE):
        match = here == id_buf[g : g + 1]
        sums = sums + jnp.dot(
            jnp.where(match, 1.0, 0.0).astype(jnp.bfloat16),
            every_ref[g],
            preferred_element_type=jnp.float32,
        )
        seen = count_buf[g : g + 1] + jnp.where(g < at, EARLIER, 0.0)
        counts = counts + jnp.where(match, seen, 0.0)
    below = lax.broadcasted_iota(jnp.int32, (2 * step, step), 0) - lax.broadcasted_iota(
        jnp.int32, (2 * step, step), 1
    )
    for i in range(2):
        match = (here == id_buf[pl.ds(at + i, 1)]) & (below > i * step)
        counts = counts + jnp.where(match, EARLIER, 0.0)
    total = jnp.sum(counts, axis=1, keepdims=True)
    before = jnp.floor(total * (1.0 / EARLIER))
    divisor = jnp.maximum(total - before * EARLIER, 1.0)
    divisor_ref[...] = jnp.broadcast_to(divisor, divisor_ref.shape)
    mean = sums / divisor
    mean_ref[...] = jnp.where(before > 0.0, 0.0, mean).astype(jnp.bfloat16)
    chunk = part_ref.shape[0]
    start = pl.multiple_of(lax.rem(index_ref[0], 128 // chunk) * chunk, chunk)
    part_ref[...] = lax.dot_general(
        weight_buf[pl.ds(start, chunk)],
        mean.astype(jnp.bfloat16),
        (((1,), (1,)), ((), ())),
        preferred_element_type=jnp.float32,
    ).astype(jnp.bfloat16)


def track_means(tracks, index, every, both, weight, chunk):
    step, width = every.shape[1:]
    rows = SIDE * step
    return pl.pallas_call(
        track_kernel,
        grid_spec=pltpu.PrefetchScalarGridSpec(
            num_scalar_prefetch=2,
            grid=(SIDE // 2,),
            in_specs=[
                pl.BlockSpec(every.shape, lambda i, t, at: (0, 0, 0)),
                pl.BlockSpec(both.shape, lambda i, t, at: (0, 0, 0)),
                pl.BlockSpec((width, 128), lambda i, t, at: (0, at[0] // (128 // chunk))),
            ],
            out_specs=[
                pl.BlockSpec((2 * step, width), lambda i, t, at: (i, 0)),
                pl.BlockSpec((chunk, 2 * step), lambda i, t, at: (0, i)),
                pl.BlockSpec((2 * step, 128), lambda i, t, at: (i, 0)),
            ],
            scratch_shapes=[
                pltpu.VMEM((SIDE, step), jnp.float32),
                pltpu.VMEM((SIDE, step), jnp.float32),
                pltpu.VMEM((128, width), jnp.bfloat16),
            ],
        ),
        out_shape=[
            jax.ShapeDtypeStruct((rows, width), jnp.bfloat16),
            jax.ShapeDtypeStruct((chunk, rows), jnp.bfloat16),
            jax.ShapeDtypeStruct((rows, 128), jnp.float32),
        ],
        compiler_params=pltpu.CompilerParams(vmem_limit_bytes=VMEM_BYTES),
        name="track_means",
    )(tracks, index, every, both, weight)


def error_kernel(track_ref, part_ref, other_ref, both_ref, mean_ref, out_ref, target_buf):
    chunk = part_ref.shape[0]
    back = part_ref.shape[1] // target_buf.shape[0]
    for z in range(SIDE):
        carried = both_ref[z, back : back + 32].astype(jnp.float32)
        for g in range(SIDE):
            target_buf[g * SIDE + z] = carried[
                g % 4 * 8 : g % 4 * 8 + 8, g // 4 * 128 : g // 4 * 128 + 128
            ]
    lane = lax.broadcasted_iota(jnp.int32, (8, 128), 1)
    tiles = []
    for group in range(part_ref.shape[1] // 128):
        low = jnp.zeros((8, 128), jnp.float32)
        high = jnp.zeros((8, 128), jnp.float32)
        for j in range(8):
            track = track_ref[group * 8 + j]
            tile = target_buf[track // 4]
            turn = j * POOL + 128 - track % 4 * POOL
            here = lane // POOL == j
            low = jnp.where(here, pltpu.roll(tile, lax.rem(turn, 128), 1), low)
            high = jnp.where(here, pltpu.roll(tile, lax.rem(turn + 64, 128), 1), high)
        tiles.append(jnp.concatenate([low, high], axis=0))
    target = jnp.concatenate(tiles, axis=1)
    total = part_ref[...].astype(jnp.float32) + other_ref[...].astype(jnp.float32)
    error = (total - target).astype(jnp.bfloat16).astype(jnp.float32)
    grad = jnp.dot(
        error.astype(jnp.bfloat16), mean_ref[...], preferred_element_type=jnp.float32
    ).astype(jnp.bfloat16)
    wide = lax.broadcasted_iota(jnp.int32, (chunk, 128), 1)
    for z in range(SIDE):
        out_ref[z, :chunk] = grad
        for half in range(2):
            tile = jnp.zeros((chunk, 128), jnp.float32)
            for q in range(4):
                source = (half * 4 + q) * 2 + z // 4
                row = error[:, source * 128 : source * 128 + 128]
                turn = (q - z % 4) % 4 * 32
                row = pltpu.roll(row, turn, 1) if turn else row
                tile = jnp.where(wide // 32 == q, row, tile)
            out_ref[z, chunk:, half * 128 : half * 128 + 128] = tile.astype(jnp.bfloat16)


def error_messages(tracks, partial, other, both, mean, seq_count):
    chunk = partial.shape[0]
    vmem = pl.BlockSpec(memory_space=pltpu.VMEM)
    return pl.pallas_call(
        error_kernel,
        in_specs=[pl.BlockSpec(memory_space=pltpu.SMEM), vmem, vmem, vmem, vmem],
        out_shape=jax.ShapeDtypeStruct((SIDE, 2 * chunk, mean.shape[1]), jnp.bfloat16),
        scratch_shapes=[pltpu.VMEM((seq_count, 8, 128), jnp.float32)],
        compiler_params=pltpu.CompilerParams(vmem_limit_bytes=VMEM_BYTES),
        name="error_messages",
    )(tracks, partial, other, both, mean)


def relay_kernel(in_ref, out_ref):
    chunk, width = in_ref.shape[1] // 2, in_ref.shape[2]
    for z in range(SIDE):
        span = slice(z * chunk, z * chunk + chunk)
        grad = in_ref[z, :chunk]
        errors = in_ref[z, chunk:].astype(jnp.float32)
        for g in range(SIDE):
            tile = errors[:, g // 4 * 128 : g // 4 * 128 + 128]
            tile = pltpu.roll(tile, 128 - g % 4 * 32, 1) if g % 4 else tile
            out_ref[g, span, :width] = grad
            out_ref[g, span, width:] = tile.astype(jnp.bfloat16)


def relay(x):
    chunk, width = x.shape[1] // 2, x.shape[2]
    return pl.pallas_call(
        relay_kernel,
        out_shape=jax.ShapeDtypeStruct((SIDE, SIDE * chunk, width + 128), jnp.bfloat16),
        compiler_params=pltpu.CompilerParams(vmem_limit_bytes=VMEM_BYTES),
        name="relay",
    )(x)


def finish_kernel(index_ref, final_ref, weight_ref, sel_ref, divisor_ref, grad_ref, context_ref):
    width = weight_ref.shape[0]
    back = sel_ref.shape[0]
    for i in range(final_ref.shape[0] // width):
        span = slice(i * width, i * width + width)
        grad_ref[:, span] = final_ref[span, :width].T
    mean_grad = jnp.dot(
        weight_ref[...], final_ref[:, width:], preferred_element_type=jnp.float32
    ).T[:back]
    track_grad = (mean_grad / divisor_ref[:, :1]).astype(jnp.bfloat16)
    context_ref[...] = lax.dot_general(
        sel_ref[...], track_grad, (((0,), (0,)), ((), ())), preferred_element_type=jnp.float32
    ).astype(jnp.bfloat16)


def finish(index, final, weight, sel, divisor):
    width, target_d = weight.shape
    back, tok_rows = sel.shape
    whole = lambda *shape: pl.BlockSpec(shape, lambda i, at: (0, 0))
    return pl.pallas_call(
        finish_kernel,
        grid_spec=pltpu.PrefetchScalarGridSpec(
            num_scalar_prefetch=1,
            grid=(1,),
            in_specs=[
                whole(*final.shape),
                whole(*weight.shape),
                whole(*sel.shape),
                pl.BlockSpec((back, 128), lambda i, at: (at[0], 0)),
            ],
            out_specs=[whole(width, target_d), whole(tok_rows, width)],
        ),
        out_shape=[
            jax.ShapeDtypeStruct((width, target_d), jnp.bfloat16),
            jax.ShapeDtypeStruct((tok_rows, width), jnp.bfloat16),
        ],
        compiler_params=pltpu.CompilerParams(vmem_limit_bytes=VMEM_BYTES),
        name="finish",
    )(index, final, weight, sel, divisor)


def local(queries, keys, values, residual, reg_weight, targets, block_track, row_count, pool_slot):
    tok_rows, width = queries.shape
    seq_count = lax.axis_size("seq")
    index = lax.axis_index("seq").astype(jnp.int32).reshape(1)
    owned, pool, target_d = targets.shape

    own_kv, wide = lay_out(keys, values, queries)
    pieces = gather_ring(own_kv, seq_count)
    query_all = lax.all_to_all(wide, "seq", 0, 0, axis_index_groups=GROUP_YX)
    query_all = query_all.reshape(SIDE * tok_rows, width)
    carried, selector, slot_rows = prepare(
        row_count, pool_slot, targets.reshape(owned * pool, target_d)
    )

    part = attend(query_all, pieces, carried, slot_rows)
    part, index = lax.optimization_barrier((part, index))
    part = lax.all_to_all(part, "seq", 0, 0, axis_index_groups=GROUP_YX)
    both = merge(part, residual, selector)
    both = lax.all_to_all(both, "seq", 0, 0, axis_index_groups=GROUP_Z)
    back = selector.shape[0]
    pooled = both[:, :back].reshape(SIDE * back, width)
    every = spread(pooled, GROUP_YX)
    mean, partial, divisor = track_means(
        block_track, index, every, both, reg_weight, target_d // seq_count
    )
    core_mate = lax.ppermute(partial, "head", [(0, 1), (1, 0), (2, 3), (3, 2)])
    partial = (partial.astype(jnp.float32) + core_mate.astype(jnp.float32)).astype(jnp.bfloat16)
    other = lax.ppermute(partial, "head", [(0, 2), (2, 0), (1, 3), (3, 1)])
    final = error_messages(block_track, partial, other, both, mean, seq_count)
    final = lax.all_to_all(final, "seq", 0, 0, axis_index_groups=GROUP_Z)
    final = lax.all_to_all(relay(final), "seq", 0, 0, axis_index_groups=GROUP_YX)
    return finish(index, final.reshape(target_d, width + 128), reg_weight, selector, divisor)


def solution(mesh):
    return jax.shard_map(
        local,
        mesh=mesh,
        in_specs=(
            P("seq", "head"),
            P("seq", "head"),
            P("seq", "head"),
            P("seq", "head"),
            P("head", None),
            P("seq", None, None),
            P(),
            P("seq"),
            P("seq", None),
        ),
        out_specs=(P("head", None), P("seq", "head")),
        check_vma=False,
    )
```

```python
import functools

import jax
import jax.numpy as jnp
from jax import lax
from jax.experimental import pallas as pl
from jax.experimental.pallas import tpu as pltpu
from jax.sharding import PartitionSpec as P

HEAD_DIM = 64
BLK = 128
POOL = 16
SIDE = 8
LOG2E = 1.4426950408889634
STAT = 16
EARLIER = 32768.0
VMEM_BYTES = 24 * 1024 * 1024

GROUP_Z = [[g * SIDE + i for i in range(SIDE)] for g in range(SIDE)]
GROUP_YX = [[g * SIDE + i for g in range(SIDE)] for i in range(SIDE)]


def spread(x, groups):
    wide = jnp.broadcast_to(x[None], (SIDE, *x.shape))
    return lax.all_to_all(wide, "seq", 0, 0, axis_index_groups=groups)


def ring(seq_count, step):
    return [
        (g * SIDE + i, g * SIDE + (i + step) % SIDE)
        for g in range(seq_count // SIDE)
        for i in range(SIDE)
    ]


def gather_ring(x, seq_count):
    pieces, up, down = [x], x, x
    for _ in range(SIDE // 2 - 1):
        up = lax.ppermute(up, "seq", ring(seq_count, 1))
        down = lax.ppermute(down, "seq", ring(seq_count, -1))
        pieces += [up, down]
    half = x.shape[0] // 2
    far_keys = lax.ppermute(up[:half], "seq", ring(seq_count, 1))
    far_values = lax.ppermute(down[half:], "seq", ring(seq_count, -1))
    return pieces + [far_keys, far_values]


def lay_out_kernel(k_ref, v_ref, q_ref, kv_ref, wide_ref, sems):
    n = k_ref.shape[0]
    copies = [
        pltpu.make_async_copy(k_ref, kv_ref.at[pl.ds(0, n)], sems.at[0]),
        pltpu.make_async_copy(v_ref, kv_ref.at[pl.ds(n, n)], sems.at[1]),
    ]
    for i in range(SIDE):
        copies.append(pltpu.make_async_copy(q_ref, wide_ref.at[i], sems.at[2 + i]))
    for copy in copies:
        copy.start()
    for copy in copies:
        copy.wait()


def lay_out(keys, values, queries):
    n, width = keys.shape
    anywhere = pl.BlockSpec(memory_space=pl.ANY)
    return pl.pallas_call(
        lay_out_kernel,
        in_specs=[pl.BlockSpec(memory_space=pltpu.VMEM)] * 3,
        out_specs=[anywhere] * 2,
        out_shape=[
            jax.ShapeDtypeStruct((2 * n, width), keys.dtype),
            jax.ShapeDtypeStruct((SIDE, n, width), queries.dtype),
        ],
        scratch_shapes=[pltpu.SemaphoreType.DMA((2 + SIDE,))],
        compiler_params=pltpu.CompilerParams(vmem_limit_bytes=60 * 1024 * 1024),
        name="lay_out",
    )(keys, values, queries)


def prepare_kernel(row_count_ref, slot_ref, target_ref, carried_ref, sel_ref, count_ref):
    here = slot_ref.shape[0]
    slots = slot_ref[...]
    sub = lax.broadcasted_iota(jnp.int32, (POOL, BLK), 0)
    lane = lax.broadcasted_iota(jnp.int32, (POOL, BLK), 1)
    zero = jnp.zeros((POOL, BLK), jnp.float32)
    picks = []
    for b in range(here):
        hit = (slots[b : b + 1] == sub) & (lane < row_count_ref[b])
        hit = jnp.where(hit, 1.0, 0.0)
        picks.append(jnp.concatenate([hit if i == b else zero for i in range(here)], axis=1))
    sel = jnp.concatenate(picks, axis=0)
    sel_ref[...] = sel.astype(jnp.bfloat16)
    counts = jnp.broadcast_to(jnp.sum(sel, axis=1, keepdims=True), (sel.shape[0], 128))
    counts = jnp.concatenate(
        [counts, jnp.zeros((128 - counts.shape[0], 128), jnp.float32)], axis=0
    )
    count_ref[...] = counts.T[:1]
    rows = target_ref.shape[0]
    blank = jnp.zeros((128 - rows, 128), jnp.float32)
    for g in range(SIDE):
        tile = target_ref[:, g * 128 : g * 128 + 128].astype(jnp.float32)
        tile = jnp.concatenate([tile, blank], axis=0).T
        eights = [
            tile[z * 16 : z * 16 + 8] + pltpu.roll(tile[z * 16 + 8 : z * 16 + 16], 64, 1)
            for z in range(SIDE)
        ]
        carried_ref[g] = jnp.concatenate(
            [jnp.concatenate(eights[:4], axis=0), jnp.concatenate(eights[4:], axis=0)], axis=1
        ).astype(jnp.bfloat16)


def prepare(row_count, pool_slot, targets):
    here = pool_slot.shape[0]
    vmem = pl.BlockSpec(memory_space=pltpu.VMEM)
    return pl.pallas_call(
        prepare_kernel,
        in_specs=[pl.BlockSpec(memory_space=pltpu.SMEM), vmem, vmem],
        out_shape=[
            jax.ShapeDtypeStruct((SIDE, 32, 256), jnp.bfloat16),
            jax.ShapeDtypeStruct((here * POOL, here * BLK), jnp.bfloat16),
            jax.ShapeDtypeStruct((1, 128), jnp.float32),
        ],
        compiler_params=pltpu.CompilerParams(vmem_limit_bytes=VMEM_BYTES),
        name="prepare",
    )(row_count, pool_slot, targets)


def attend_kernel(q_ref, piece_ref, count_ref, *refs):
    kv_refs, (o_ref, k_own, v_own) = refs[:-3], refs[-3:]
    rows = q_ref.shape[0] // o_ref.shape[0]
    lane = lax.broadcasted_iota(jnp.int32, (1, 128), 1)
    first = lane < HEAD_DIM

    @pl.when(pl.program_id(1) == 0)
    def _():
        zero = jnp.zeros((), jnp.bfloat16)
        one = jnp.ones((), jnp.bfloat16)
        n = kv_refs[-1].shape[0]
        pairs = [(ref[:n], ref[n:]) for ref in kv_refs[:-2]]
        for i, (k, v) in enumerate(pairs + [(kv_refs[-2][...], kv_refs[-1][...])]):
            span = pl.ds(i * n, n)
            k_own[0, :, span] = jnp.where(first, k, zero).T
            k_own[1, :, span] = jnp.where(first, zero, k).T
            v_own[0, span] = jnp.where(first, v, one)
            v_own[1, span] = jnp.where(first, one, v)

    scale = LOG2E * HEAD_DIM ** (-0.5)
    q = q_ref[...]
    scores = [jnp.dot(q, k_own[h], preferred_element_type=jnp.float32) for h in range(2)]
    tops = [jnp.max(s, axis=1, keepdims=True) for s in scores]
    weights = [
        jnp.exp2((s - top) * scale).astype(jnp.bfloat16) for s, top in zip(scores, tops)
    ]
    sums = [
        jnp.dot(w, v_own[h], preferred_element_type=jnp.float32) for h, w in enumerate(weights)
    ]
    num = jnp.where(first, sums[0], sums[1])
    den_other = jnp.where(first, sums[1], sums[0])
    den = pltpu.roll(den_other, HEAD_DIM, 1)
    context = (num / den).astype(jnp.bfloat16)
    lse = jnp.where(first, tops[1], tops[0]) * scale + jnp.log2(den_other)
    pad = jnp.concatenate([count_ref[...], jnp.zeros((3, 128), jnp.float32)], axis=0)
    for i in range(o_ref.shape[0]):
        span = slice(i * rows, i * rows + rows)
        turned = lse[span].T
        left = jnp.concatenate([turned[HEAD_DIM : HEAD_DIM + 1], turned[0:1]], axis=0)
        left = jnp.concatenate([left[:, :128], left[:, 128:]], axis=0)
        hi = left.astype(jnp.bfloat16)
        rest = left - hi.astype(jnp.float32)
        mid = rest.astype(jnp.bfloat16)
        rest = rest - mid.astype(jnp.float32)
        o_ref[i, :rows] = context[span]
        o_ref[i, rows : rows + STAT] = jnp.concatenate(
            [hi.astype(jnp.float32), mid.astype(jnp.float32), rest, pad], axis=0
        ).astype(jnp.bfloat16)
        o_ref[i, rows + STAT :] = piece_ref[i]


def attend(queries, pieces, carried, counts):
    n, width = queries.shape
    rows = n // SIDE
    keys_n = sum(x.shape[0] for x in pieces) // 2
    pairs = width // 128
    out_rows = rows + STAT + carried.shape[1]
    return pl.pallas_call(
        attend_kernel,
        grid=(pairs, SIDE // 2),
        in_specs=[
            pl.BlockSpec((2 * rows, 128), lambda p, i: (i, p)),
            pl.BlockSpec((2, carried.shape[1], 128), lambda p, i: (i, 0, p)),
            pl.BlockSpec(counts.shape, lambda p, i: (0, 0)),
        ]
        + [pl.BlockSpec((x.shape[0], 128), lambda p, i: (0, p)) for x in pieces],
        out_specs=pl.BlockSpec((2, out_rows, 128), lambda p, i: (i, 0, p)),
        out_shape=jax.ShapeDtypeStruct((SIDE, out_rows, width), jnp.bfloat16),
        scratch_shapes=[
            pltpu.VMEM((2, 128, keys_n), jnp.bfloat16),
            pltpu.VMEM((2, keys_n, 128), jnp.bfloat16),
        ],
        compiler_params=pltpu.CompilerParams(vmem_limit_bytes=40 * 1024 * 1024),
        name="attend",
    )(queries, carried, counts, *pieces)


def merge_kernel(part_ref, residual_ref, sel_ref, out_ref):
    rows, width = residual_ref.shape
    lane = lax.broadcasted_iota(jnp.int32, (1, 128), 1)
    first = lane < HEAD_DIM
    stats = part_ref[:, rows : rows + STAT].astype(jnp.float32)
    merged = stats[:, 0:4] + stats[:, 4:8] + stats[:, 8:12]
    scaled = []
    for p in range(width // 128):
        cols = slice(p * 128, p * 128 + 128)
        for h in range(2):
            x = jnp.concatenate([merged[:, h, cols], merged[:, 2 + h, cols]], axis=1)
            w = jnp.exp2(x - jnp.max(x, axis=0, keepdims=True))
            scaled.append(w / jnp.sum(w, axis=0, keepdims=True))
    weights = jnp.concatenate(scaled, axis=0)
    weights = jnp.concatenate(
        [weights, jnp.zeros((128 - weights.shape[0], rows), jnp.float32)], axis=0
    ).T
    streams = []
    for p in range(width // 128):
        cols = slice(p * 128, p * 128 + 128)
        total = jnp.zeros((rows, 128), jnp.float32)
        for j in range(SIDE):
            a = (2 * p) * SIDE + j
            b = (2 * p + 1) * SIDE + j
            w = jnp.where(first, weights[:, a : a + 1], weights[:, b : b + 1])
            total = total + w * part_ref[j, :rows, cols].astype(jnp.float32)
        context = total.astype(jnp.bfloat16).astype(jnp.float32)
        streams.append(
            (residual_ref[:, cols].astype(jnp.float32) + context).astype(jnp.bfloat16)
        )
    stream = jnp.concatenate(streams, axis=1)
    pooled = jnp.dot(sel_ref[...], stream, preferred_element_type=jnp.float32).astype(jnp.bfloat16)
    back = sel_ref.shape[0]
    for j in range(SIDE):
        out_ref[j, :back] = pooled

    carried = part_ref[:, rows + STAT :].astype(jnp.float32)
    counts = stats[:, 12:13, :128]
    per = 128 // back
    count_tiles = []
    for half in range(SIDE // per):
        tile = jnp.zeros((1, 128), jnp.float32)
        for q in range(per):
            row = counts[half * per + q]
            row = pltpu.roll(row, q * back, 1) if q else row
            tile = jnp.where(lane // back == q, row, tile)
        count_tiles.append(tile)
    count_row = jnp.concatenate(count_tiles, axis=1)
    tail = jnp.concatenate([count_row, jnp.zeros((15, count_row.shape[1]), jnp.float32)], axis=0)
    for g in range(SIDE):
        span = slice(g % 4 * 8, g % 4 * 8 + 8)
        cols = slice(g // 4 * 128, g // 4 * 128 + 128)
        halves = [
            jnp.concatenate([carried[half * 4 + q, span, cols] for q in range(4)], axis=0)
            for half in range(2)
        ]
        out_ref[g, back:] = jnp.concatenate(
            [jnp.concatenate(halves, axis=1), tail], axis=0
        ).astype(jnp.bfloat16)


def merge(part, residual, sel):
    back, width = sel.shape[0], residual.shape[1]
    return pl.pallas_call(
        merge_kernel,
        out_shape=jax.ShapeDtypeStruct((SIDE, back + 48, width), jnp.bfloat16),
        compiler_params=pltpu.CompilerParams(vmem_limit_bytes=VMEM_BYTES),
        name="merge",
    )(part, residual, sel)


def column(row):
    return jnp.broadcast_to(row, (128, row.shape[1])).T[:, :1]


def track_kernel(
    track_ref,
    index_ref,
    every_ref,
    both_ref,
    weight_ref,
    mean_ref,
    part_ref,
    divisor_ref,
    count_buf,
    id_buf,
    weight_buf,
):
    step = every_ref.shape[1]
    at = pl.program_id(0) * 2

    @pl.when(at == 0)
    def _():
        lane = lax.broadcasted_iota(jnp.int32, (1, 128), 1)
        rows = [
            both_ref[z, both_ref.shape[1] - 16 :].astype(jnp.float32)[:1] for z in range(SIDE)
        ]
        for g in range(SIDE):
            for half in range(2):
                tile = jnp.zeros((1, 128), jnp.float32)
                for q in range(4):
                    row = rows[half * 4 + q][:, g // 4 * 128 : g // 4 * 128 + 128]
                    turn = (q - g % 4) % 4 * 32
                    row = pltpu.roll(row, turn, 1) if turn else row
                    tile = jnp.where(lane // 32 == q, row, tile)
                count_buf[g : g + 1, half * 128 : half * 128 + 128] = tile
                track = jnp.zeros((1, 128), jnp.int32)
                for j in range(8):
                    track = jnp.where(lane // POOL == j, track_ref[g * 16 + half * 8 + j], track)
                id_buf[g : g + 1, half * 128 : half * 128 + 128] = (
                    track * POOL + lane % POOL
                ).astype(jnp.float32)
        weight_buf[...] = weight_ref[...].T

    here = jnp.concatenate([column(id_buf[pl.ds(at + i, 1)]) for i in range(2)], axis=0)
    sums = jnp.zeros(mean_ref.shape, jnp.float32)
    counts = jnp.zeros((2 * step, step), jnp.float32)
    for g in range(SIDE):
        match = here == id_buf[g : g + 1]
        sums = sums + jnp.dot(
            jnp.where(match, 1.0, 0.0).astype(jnp.bfloat16),
            every_ref[g],
            preferred_element_type=jnp.float32,
        )
        seen = count_buf[g : g + 1] + jnp.where(g < at, EARLIER, 0.0)
        counts = counts + jnp.where(match, seen, 0.0)
    below = lax.broadcasted_iota(jnp.int32, (2 * step, step), 0) - lax.broadcasted_iota(
        jnp.int32, (2 * step, step), 1
    )
    for i in range(2):
        match = (here == id_buf[pl.ds(at + i, 1)]) & (below > i * step)
        counts = counts + jnp.where(match, EARLIER, 0.0)
    total = jnp.sum(counts, axis=1, keepdims=True)
    before = jnp.floor(total * (1.0 / EARLIER))
    divisor = jnp.maximum(total - before * EARLIER, 1.0)
    divisor_ref[...] = jnp.broadcast_to(divisor, divisor_ref.shape)
    mean = sums / divisor
    mean_ref[...] = jnp.where(before > 0.0, 0.0, mean).astype(jnp.bfloat16)
    chunk = part_ref.shape[0]
    start = pl.multiple_of(lax.rem(index_ref[0], 128 // chunk) * chunk, chunk)
    part_ref[...] = lax.dot_general(
        weight_buf[pl.ds(start, chunk)],
        mean.astype(jnp.bfloat16),
        (((1,), (1,)), ((), ())),
        preferred_element_type=jnp.float32,
    ).astype(jnp.bfloat16)


def track_means(tracks, index, every, both, weight, chunk):
    step, width = every.shape[1:]
    rows = SIDE * step
    return pl.pallas_call(
        track_kernel,
        grid_spec=pltpu.PrefetchScalarGridSpec(
            num_scalar_prefetch=2,
            grid=(SIDE // 2,),
            in_specs=[
                pl.BlockSpec(every.shape, lambda i, t, at: (0, 0, 0)),
                pl.BlockSpec(both.shape, lambda i, t, at: (0, 0, 0)),
                pl.BlockSpec((width, 128), lambda i, t, at: (0, at[0] // (128 // chunk))),
            ],
            out_specs=[
                pl.BlockSpec((2 * step, width), lambda i, t, at: (i, 0)),
                pl.BlockSpec((chunk, 2 * step), lambda i, t, at: (0, i)),
                pl.BlockSpec((2 * step, 128), lambda i, t, at: (i, 0)),
            ],
            scratch_shapes=[
                pltpu.VMEM((SIDE, step), jnp.float32),
                pltpu.VMEM((SIDE, step), jnp.float32),
                pltpu.VMEM((128, width), jnp.bfloat16),
            ],
        ),
        out_shape=[
            jax.ShapeDtypeStruct((rows, width), jnp.bfloat16),
            jax.ShapeDtypeStruct((chunk, rows), jnp.bfloat16),
            jax.ShapeDtypeStruct((rows, 128), jnp.float32),
        ],
        compiler_params=pltpu.CompilerParams(vmem_limit_bytes=VMEM_BYTES),
        name="track_means",
    )(tracks, index, every, both, weight)


def error_kernel(track_ref, part_ref, other_ref, both_ref, mean_ref, out_ref, target_buf):
    chunk = part_ref.shape[0]
    back = part_ref.shape[1] // target_buf.shape[0]
    for z in range(SIDE):
        carried = both_ref[z, back : back + 32].astype(jnp.float32)
        for g in range(SIDE):
            target_buf[g * SIDE + z] = carried[
                g % 4 * 8 : g % 4 * 8 + 8, g // 4 * 128 : g // 4 * 128 + 128
            ]
    lane = lax.broadcasted_iota(jnp.int32, (8, 128), 1)
    tiles = []
    for group in range(part_ref.shape[1] // 128):
        low = jnp.zeros((8, 128), jnp.float32)
        high = jnp.zeros((8, 128), jnp.float32)
        for j in range(8):
            track = track_ref[group * 8 + j]
            tile = target_buf[track // 4]
            turn = j * POOL + 128 - track % 4 * POOL
            here = lane // POOL == j
            low = jnp.where(here, pltpu.roll(tile, lax.rem(turn, 128), 1), low)
            high = jnp.where(here, pltpu.roll(tile, lax.rem(turn + 64, 128), 1), high)
        tiles.append(jnp.concatenate([low, high], axis=0))
    target = jnp.concatenate(tiles, axis=1)
    total = part_ref[...].astype(jnp.float32) + other_ref[...].astype(jnp.float32)
    error = (total - target).astype(jnp.bfloat16).astype(jnp.float32)
    grad = jnp.dot(
        error.astype(jnp.bfloat16), mean_ref[...], preferred_element_type=jnp.float32
    ).astype(jnp.bfloat16)
    wide = lax.broadcasted_iota(jnp.int32, (chunk, 128), 1)
    for z in range(SIDE):
        out_ref[z, :chunk] = grad
        for half in range(2):
            tile = jnp.zeros((chunk, 128), jnp.float32)
            for q in range(4):
                source = (half * 4 + q) * 2 + z // 4
                row = error[:, source * 128 : source * 128 + 128]
                turn = (q - z % 4) % 4 * 32
                row = pltpu.roll(row, turn, 1) if turn else row
                tile = jnp.where(wide // 32 == q, row, tile)
            out_ref[z, chunk:, half * 128 : half * 128 + 128] = tile.astype(jnp.bfloat16)


def error_messages(tracks, partial, other, both, mean, seq_count):
    chunk = partial.shape[0]
    vmem = pl.BlockSpec(memory_space=pltpu.VMEM)
    return pl.pallas_call(
        error_kernel,
        in_specs=[pl.BlockSpec(memory_space=pltpu.SMEM), vmem, vmem, vmem, vmem],
        out_shape=jax.ShapeDtypeStruct((SIDE, 2 * chunk, mean.shape[1]), jnp.bfloat16),
        scratch_shapes=[pltpu.VMEM((seq_count, 8, 128), jnp.float32)],
        compiler_params=pltpu.CompilerParams(vmem_limit_bytes=VMEM_BYTES),
        name="error_messages",
    )(tracks, partial, other, both, mean)


def relay_kernel(in_ref, out_ref):
    chunk = in_ref.shape[1] // 2
    lane = lax.broadcasted_iota(jnp.int32, (chunk, 128), 1)
    errors = [in_ref[z, chunk:].astype(jnp.float32) for z in range(SIDE)]
    for g in range(SIDE):
        for z in range(SIDE):
            out_ref[g, z * chunk : z * chunk + chunk] = in_ref[z, :chunk]
        for half in range(2):
            tile = jnp.zeros((chunk, 128), jnp.float32)
            for q in range(4):
                row = errors[half * 4 + q][:, g // 4 * 128 : g // 4 * 128 + 128]
                turn = (q - g % 4) % 4 * 32
                row = pltpu.roll(row, turn, 1) if turn else row
                tile = jnp.where(lane // 32 == q, row, tile)
            out_ref[g, SIDE * chunk :, half * 128 : half * 128 + 128] = tile.astype(jnp.bfloat16)


def relay(x):
    chunk, width = x.shape[1] // 2, x.shape[2]
    return pl.pallas_call(
        relay_kernel,
        out_shape=jax.ShapeDtypeStruct((SIDE, (SIDE + 1) * chunk, width), jnp.bfloat16),
        compiler_params=pltpu.CompilerParams(vmem_limit_bytes=VMEM_BYTES),
        name="relay",
    )(x)


def finish_kernel(index_ref, final_ref, weight_ref, sel_ref, divisor_ref, grad_ref, context_ref):
    back = sel_ref.shape[0]
    chunk = final_ref.shape[1] // (SIDE + 1)
    rows = SIDE * chunk
    tiles = []
    for g in range(SIDE):
        grad_ref[:, g * rows : g * rows + rows] = final_ref[g, :rows].T
        errors = final_ref[g, rows:].astype(jnp.float32)
        for z in range(SIDE):
            tile = errors[:, z // 4 * 128 : z // 4 * 128 + 128]
            tile = pltpu.roll(tile, 128 - z % 4 * 32, 1) if z % 4 else tile
            tiles.append(tile.astype(jnp.bfloat16))
    mean_grad = jnp.dot(
        weight_ref[...], jnp.concatenate(tiles, axis=0), preferred_element_type=jnp.float32
    ).T[:back]
    track_grad = (mean_grad / divisor_ref[:, :1]).astype(jnp.bfloat16)
    context_ref[...] = lax.dot_general(
        sel_ref[...], track_grad, (((0,), (0,)), ((), ())), preferred_element_type=jnp.float32
    ).astype(jnp.bfloat16)


def finish(index, final, weight, sel, divisor):
    width, target_d = weight.shape
    back, tok_rows = sel.shape
    whole = lambda *shape: pl.BlockSpec(shape, lambda i, at: (0, 0))
    return pl.pallas_call(
        finish_kernel,
        grid_spec=pltpu.PrefetchScalarGridSpec(
            num_scalar_prefetch=1,
            grid=(1,),
            in_specs=[
                pl.BlockSpec(final.shape, lambda i, at: (0, 0, 0)),
                whole(*weight.shape),
                whole(*sel.shape),
                pl.BlockSpec((back, 128), lambda i, at: (at[0], 0)),
            ],
            out_specs=[whole(width, target_d), whole(tok_rows, width)],
        ),
        out_shape=[
            jax.ShapeDtypeStruct((width, target_d), jnp.bfloat16),
            jax.ShapeDtypeStruct((tok_rows, width), jnp.bfloat16),
        ],
        compiler_params=pltpu.CompilerParams(vmem_limit_bytes=VMEM_BYTES),
        name="finish",
    )(index, final, weight, sel, divisor)


def local(queries, keys, values, residual, reg_weight, targets, block_track, row_count, pool_slot):
    tok_rows, width = queries.shape
    seq_count = lax.axis_size("seq")
    index = lax.axis_index("seq").astype(jnp.int32).reshape(1)
    owned, pool, target_d = targets.shape

    own_kv, wide = lay_out(keys, values, queries)
    pieces = gather_ring(own_kv, seq_count)
    query_all = lax.all_to_all(wide, "seq", 0, 0, axis_index_groups=GROUP_YX)
    query_all = query_all.reshape(SIDE * tok_rows, width)
    carried, selector, slot_rows = prepare(
        row_count, pool_slot, targets.reshape(owned * pool, target_d)
    )

    part = attend(query_all, pieces, carried, slot_rows)
    part, index = lax.optimization_barrier((part, index))
    part = lax.all_to_all(part, "seq", 0, 0, axis_index_groups=GROUP_YX)
    both = merge(part, residual, selector)
    both = lax.all_to_all(both, "seq", 0, 0, axis_index_groups=GROUP_Z)
    back = selector.shape[0]
    pooled = both[:, :back].reshape(SIDE * back, width)
    every = spread(pooled, GROUP_YX)
    mean, partial, divisor = track_means(
        block_track, index, every, both, reg_weight, target_d // seq_count
    )
    core_mate = lax.ppermute(partial, "head", [(0, 1), (1, 0), (2, 3), (3, 2)])
    partial = (partial.astype(jnp.float32) + core_mate.astype(jnp.float32)).astype(jnp.bfloat16)
    other = lax.ppermute(partial, "head", [(0, 2), (2, 0), (1, 3), (3, 1)])
    final = error_messages(block_track, partial, other, both, mean, seq_count)
    final = lax.all_to_all(final, "seq", 0, 0, axis_index_groups=GROUP_Z)
    final = lax.all_to_all(relay(final), "seq", 0, 0, axis_index_groups=GROUP_YX)
    return finish(index, final, reg_weight, selector, divisor)


def solution(mesh):
    return jax.shard_map(
        local,
        mesh=mesh,
        in_specs=(
            P("seq", "head"),
            P("seq", "head"),
            P("seq", "head"),
            P("seq", "head"),
            P("head", None),
            P("seq", None, None),
            P(),
            P("seq"),
            P("seq", None),
        ),
        out_specs=(P("head", None), P("seq", "head")),
        check_vma=False,
    )
```

```python
import functools

import jax
import jax.numpy as jnp
from jax import lax
from jax.experimental import pallas as pl
from jax.experimental.pallas import tpu as pltpu
from jax.sharding import PartitionSpec as P

HEAD_DIM = 64
BLK = 128
POOL = 16
SIDE = 8
LOG2E = 1.4426950408889634
STAT = 16
EARLIER = 32768.0
VMEM_BYTES = 24 * 1024 * 1024

GROUP_Z = [[g * SIDE + i for i in range(SIDE)] for g in range(SIDE)]
GROUP_YX = [[g * SIDE + i for g in range(SIDE)] for i in range(SIDE)]


def spread(x, groups):
    wide = jnp.broadcast_to(x[None], (SIDE, *x.shape))
    return lax.all_to_all(wide, "seq", 0, 0, axis_index_groups=groups)


def ring(seq_count, step):
    return [
        (g * SIDE + i, g * SIDE + (i + step) % SIDE)
        for g in range(seq_count // SIDE)
        for i in range(SIDE)
    ]


def gather_ring(x, seq_count):
    pieces, up, down = [x], x, x
    for _ in range(SIDE // 2 - 1):
        up = lax.ppermute(up, "seq", ring(seq_count, 1))
        down = lax.ppermute(down, "seq", ring(seq_count, -1))
        pieces += [up, down]
    half = x.shape[0] // 2
    far_keys = lax.ppermute(up[:half], "seq", ring(seq_count, 1))
    far_values = lax.ppermute(down[half:], "seq", ring(seq_count, -1))
    return pieces + [far_keys, far_values]


def lay_out_kernel(k_ref, v_ref, q_ref, kv_ref, wide_ref, sems):
    n = k_ref.shape[0]
    copies = [
        pltpu.make_async_copy(k_ref, kv_ref.at[pl.ds(0, n)], sems.at[0]),
        pltpu.make_async_copy(v_ref, kv_ref.at[pl.ds(n, n)], sems.at[1]),
    ]
    for i in range(SIDE):
        copies.append(pltpu.make_async_copy(q_ref, wide_ref.at[i], sems.at[2 + i]))
    for copy in copies:
        copy.start()
    for copy in copies:
        copy.wait()


def lay_out(keys, values, queries):
    n, width = keys.shape
    anywhere = pl.BlockSpec(memory_space=pl.ANY)
    return pl.pallas_call(
        lay_out_kernel,
        in_specs=[pl.BlockSpec(memory_space=pltpu.VMEM)] * 3,
        out_specs=[anywhere] * 2,
        out_shape=[
            jax.ShapeDtypeStruct((2 * n, width), keys.dtype),
            jax.ShapeDtypeStruct((SIDE, n, width), queries.dtype),
        ],
        scratch_shapes=[pltpu.SemaphoreType.DMA((2 + SIDE,))],
        compiler_params=pltpu.CompilerParams(vmem_limit_bytes=60 * 1024 * 1024),
        name="lay_out",
    )(keys, values, queries)


def prepare_kernel(row_count_ref, slot_ref, target_ref, carried_ref, sel_ref, count_ref):
    here = slot_ref.shape[0]
    slots = slot_ref[...]
    sub = lax.broadcasted_iota(jnp.int32, (POOL, BLK), 0)
    lane = lax.broadcasted_iota(jnp.int32, (POOL, BLK), 1)
    zero = jnp.zeros((POOL, BLK), jnp.float32)
    picks = []
    for b in range(here):
        hit = (slots[b : b + 1] == sub) & (lane < row_count_ref[b])
        hit = jnp.where(hit, 1.0, 0.0)
        picks.append(jnp.concatenate([hit if i == b else zero for i in range(here)], axis=1))
    sel = jnp.concatenate(picks, axis=0)
    sel_ref[...] = sel.astype(jnp.bfloat16)
    counts = jnp.broadcast_to(jnp.sum(sel, axis=1, keepdims=True), (sel.shape[0], 128))
    counts = jnp.concatenate(
        [counts, jnp.zeros((128 - counts.shape[0], 128), jnp.float32)], axis=0
    )
    count_ref[...] = counts.T[:1]
    rows = target_ref.shape[0]
    blank = jnp.zeros((128 - rows, 128), jnp.float32)
    for g in range(SIDE):
        tile = target_ref[:, g * 128 : g * 128 + 128].astype(jnp.float32)
        tile = jnp.concatenate([tile, blank], axis=0).T
        eights = [
            tile[z * 16 : z * 16 + 8] + pltpu.roll(tile[z * 16 + 8 : z * 16 + 16], 64, 1)
            for z in range(SIDE)
        ]
        carried_ref[g] = jnp.concatenate(
            [jnp.concatenate(eights[:4], axis=0), jnp.concatenate(eights[4:], axis=0)], axis=1
        ).astype(jnp.bfloat16)


def prepare(row_count, pool_slot, targets):
    here = pool_slot.shape[0]
    vmem = pl.BlockSpec(memory_space=pltpu.VMEM)
    return pl.pallas_call(
        prepare_kernel,
        in_specs=[pl.BlockSpec(memory_space=pltpu.SMEM), vmem, vmem],
        out_shape=[
            jax.ShapeDtypeStruct((SIDE, 32, 256), jnp.bfloat16),
            jax.ShapeDtypeStruct((here * POOL, here * BLK), jnp.bfloat16),
            jax.ShapeDtypeStruct((1, 128), jnp.float32),
        ],
        compiler_params=pltpu.CompilerParams(vmem_limit_bytes=VMEM_BYTES),
        name="prepare",
    )(row_count, pool_slot, targets)


def attend_kernel(q_ref, piece_ref, count_ref, *refs):
    kv_refs, (o_ref, k_own, v_own) = refs[:-3], refs[-3:]
    rows = q_ref.shape[0] // o_ref.shape[0]
    lane = lax.broadcasted_iota(jnp.int32, (1, 128), 1)
    first = lane < HEAD_DIM

    @pl.when(pl.program_id(1) == 0)
    def _():
        zero = jnp.zeros((), jnp.bfloat16)
        one = jnp.ones((), jnp.bfloat16)
        n = kv_refs[-1].shape[0]
        pairs = [(ref[:n], ref[n:]) for ref in kv_refs[:-2]]
        for i, (k, v) in enumerate(pairs + [(kv_refs[-2][...], kv_refs[-1][...])]):
            span = pl.ds(i * n, n)
            k_own[0, :, span] = jnp.where(first, k, zero).T
            k_own[1, :, span] = jnp.where(first, zero, k).T
            v_own[0, span] = jnp.where(first, v, one)
            v_own[1, span] = jnp.where(first, one, v)

    scale = LOG2E * HEAD_DIM ** (-0.5)
    q = q_ref[...]
    scores = [jnp.dot(q, k_own[h], preferred_element_type=jnp.float32) for h in range(2)]
    tops = [jnp.max(s, axis=1, keepdims=True) for s in scores]
    weights = [
        jnp.exp2((s - top) * scale).astype(jnp.bfloat16) for s, top in zip(scores, tops)
    ]
    sums = [
        jnp.dot(w, v_own[h], preferred_element_type=jnp.float32) for h, w in enumerate(weights)
    ]
    num = jnp.where(first, sums[0], sums[1])
    den_other = jnp.where(first, sums[1], sums[0])
    den = pltpu.roll(den_other, HEAD_DIM, 1)
    context = (num / den).astype(jnp.bfloat16)
    lse = jnp.where(first, tops[1], tops[0]) * scale + jnp.log2(den_other)
    pad = jnp.concatenate([count_ref[...], jnp.zeros((3, 128), jnp.float32)], axis=0)
    for i in range(o_ref.shape[0]):
        span = slice(i * rows, i * rows + rows)
        turned = lse[span].T
        left = jnp.concatenate([turned[HEAD_DIM : HEAD_DIM + 1], turned[0:1]], axis=0)
        left = jnp.concatenate([left[:, :128], left[:, 128:]], axis=0)
        hi = left.astype(jnp.bfloat16)
        rest = left - hi.astype(jnp.float32)
        mid = rest.astype(jnp.bfloat16)
        rest = rest - mid.astype(jnp.float32)
        o_ref[i, :rows] = context[span]
        o_ref[i, rows : rows + STAT] = jnp.concatenate(
            [hi.astype(jnp.float32), mid.astype(jnp.float32), rest, pad], axis=0
        ).astype(jnp.bfloat16)
        o_ref[i, rows + STAT :] = piece_ref[i]


def attend(queries, pieces, carried, counts):
    n, width = queries.shape
    rows = n // SIDE
    keys_n = sum(x.shape[0] for x in pieces) // 2
    pairs = width // 128
    out_rows = rows + STAT + carried.shape[1]
    return pl.pallas_call(
        attend_kernel,
        grid=(pairs, SIDE // 2),
        in_specs=[
            pl.BlockSpec((2 * rows, 128), lambda p, i: (i, p)),
            pl.BlockSpec((2, carried.shape[1], 128), lambda p, i: (i, 0, p)),
            pl.BlockSpec(counts.shape, lambda p, i: (0, 0)),
        ]
        + [pl.BlockSpec((x.shape[0], 128), lambda p, i: (0, p)) for x in pieces],
        out_specs=pl.BlockSpec((2, out_rows, 128), lambda p, i: (i, 0, p)),
        out_shape=jax.ShapeDtypeStruct((SIDE, out_rows, width), jnp.bfloat16),
        scratch_shapes=[
            pltpu.VMEM((2, 128, keys_n), jnp.bfloat16),
            pltpu.VMEM((2, keys_n, 128), jnp.bfloat16),
        ],
        compiler_params=pltpu.CompilerParams(vmem_limit_bytes=40 * 1024 * 1024),
        name="attend",
    )(queries, carried, counts, *pieces)


def merge_kernel(part_ref, residual_ref, sel_ref, out_ref):
    rows, width = residual_ref.shape
    lane = lax.broadcasted_iota(jnp.int32, (1, 128), 1)
    first = lane < HEAD_DIM
    stats = part_ref[:, rows : rows + STAT].astype(jnp.float32)
    merged = stats[:, 0:4] + stats[:, 4:8] + stats[:, 8:12]
    scaled = []
    for p in range(width // 128):
        cols = slice(p * 128, p * 128 + 128)
        for h in range(2):
            x = jnp.concatenate([merged[:, h, cols], merged[:, 2 + h, cols]], axis=1)
            w = jnp.exp2(x - jnp.max(x, axis=0, keepdims=True))
            scaled.append(w / jnp.sum(w, axis=0, keepdims=True))
    weights = jnp.concatenate(scaled, axis=0)
    weights = jnp.concatenate(
        [weights, jnp.zeros((128 - weights.shape[0], rows), jnp.float32)], axis=0
    ).T
    streams = []
    for p in range(width // 128):
        cols = slice(p * 128, p * 128 + 128)
        total = jnp.zeros((rows, 128), jnp.float32)
        for j in range(SIDE):
            a = (2 * p) * SIDE + j
            b = (2 * p + 1) * SIDE + j
            w = jnp.where(first, weights[:, a : a + 1], weights[:, b : b + 1])
            total = total + w * part_ref[j, :rows, cols].astype(jnp.float32)
        context = total.astype(jnp.bfloat16).astype(jnp.float32)
        streams.append(
            (residual_ref[:, cols].astype(jnp.float32) + context).astype(jnp.bfloat16)
        )
    stream = jnp.concatenate(streams, axis=1)
    pooled = jnp.dot(sel_ref[...], stream, preferred_element_type=jnp.float32).astype(jnp.bfloat16)
    back = sel_ref.shape[0]
    for j in range(SIDE):
        out_ref[j, :back] = pooled

    carried = part_ref[:, rows + STAT :].astype(jnp.float32)
    counts = stats[:, 12:13, :128]
    per = 128 // back
    count_tiles = []
    for half in range(SIDE // per):
        tile = jnp.zeros((1, 128), jnp.float32)
        for q in range(per):
            row = counts[half * per + q]
            row = pltpu.roll(row, q * back, 1) if q else row
            tile = jnp.where(lane // back == q, row, tile)
        count_tiles.append(tile)
    count_row = jnp.concatenate(count_tiles, axis=1)
    tail = jnp.concatenate([count_row, jnp.zeros((15, count_row.shape[1]), jnp.float32)], axis=0)
    for g in range(SIDE):
        span = slice(g % 4 * 8, g % 4 * 8 + 8)
        cols = slice(g // 4 * 128, g // 4 * 128 + 128)
        halves = [
            jnp.concatenate([carried[half * 4 + q, span, cols] for q in range(4)], axis=0)
            for half in range(2)
        ]
        out_ref[g, back:] = jnp.concatenate(
            [jnp.concatenate(halves, axis=1), tail], axis=0
        ).astype(jnp.bfloat16)


def merge(part, residual, sel):
    back, width = sel.shape[0], residual.shape[1]
    return pl.pallas_call(
        merge_kernel,
        out_shape=jax.ShapeDtypeStruct((SIDE, back + 48, width), jnp.bfloat16),
        compiler_params=pltpu.CompilerParams(vmem_limit_bytes=VMEM_BYTES),
        name="merge",
    )(part, residual, sel)


def column(row):
    return jnp.broadcast_to(row, (128, row.shape[1])).T[:, :1]


def track_kernel(
    track_ref,
    index_ref,
    every_ref,
    both_ref,
    weight_ref,
    mean_ref,
    part_ref,
    divisor_ref,
    count_buf,
    id_buf,
    weight_buf,
):
    step = every_ref.shape[1]
    at = pl.program_id(0) * 4

    @pl.when(at == 0)
    def _():
        lane = lax.broadcasted_iota(jnp.int32, (1, 128), 1)
        rows = [
            both_ref[z, both_ref.shape[1] - 16 :].astype(jnp.float32)[:1] for z in range(SIDE)
        ]
        for g in range(SIDE):
            for half in range(2):
                tile = jnp.zeros((1, 128), jnp.float32)
                for q in range(4):
                    row = rows[half * 4 + q][:, g // 4 * 128 : g // 4 * 128 + 128]
                    turn = (q - g % 4) % 4 * 32
                    row = pltpu.roll(row, turn, 1) if turn else row
                    tile = jnp.where(lane // 32 == q, row, tile)
                count_buf[g : g + 1, half * 128 : half * 128 + 128] = tile
                track = jnp.zeros((1, 128), jnp.int32)
                for j in range(8):
                    track = jnp.where(lane // POOL == j, track_ref[g * 16 + half * 8 + j], track)
                id_buf[g : g + 1, half * 128 : half * 128 + 128] = (
                    track * POOL + lane % POOL
                ).astype(jnp.float32)
        weight_buf[...] = weight_ref[...].T

    here = jnp.concatenate([column(id_buf[pl.ds(at + i, 1)]) for i in range(4)], axis=0)
    sums = jnp.zeros(mean_ref.shape, jnp.float32)
    counts = jnp.zeros((4 * step, step), jnp.float32)
    for g in range(SIDE):
        match = here == id_buf[g : g + 1]
        sums = sums + jnp.dot(
            jnp.where(match, 1.0, 0.0).astype(jnp.bfloat16),
            every_ref[g],
            preferred_element_type=jnp.float32,
        )
        seen = count_buf[g : g + 1] + jnp.where(g < at, EARLIER, 0.0)
        counts = counts + jnp.where(match, seen, 0.0)
    below = lax.broadcasted_iota(jnp.int32, (4 * step, step), 0) - lax.broadcasted_iota(
        jnp.int32, (4 * step, step), 1
    )
    for i in range(4):
        match = (here == id_buf[pl.ds(at + i, 1)]) & (below > i * step)
        counts = counts + jnp.where(match, EARLIER, 0.0)
    total = jnp.sum(counts, axis=1, keepdims=True)
    before = jnp.floor(total * (1.0 / EARLIER))
    divisor = jnp.maximum(total - before * EARLIER, 1.0)
    divisor_ref[...] = jnp.broadcast_to(divisor, divisor_ref.shape)
    mean = sums / divisor
    mean_ref[...] = jnp.where(before > 0.0, 0.0, mean).astype(jnp.bfloat16)
    chunk = part_ref.shape[0]
    start = pl.multiple_of(lax.rem(index_ref[0], 128 // chunk) * chunk, chunk)
    part_ref[...] = lax.dot_general(
        weight_buf[pl.ds(start, chunk)],
        mean.astype(jnp.bfloat16),
        (((1,), (1,)), ((), ())),
        preferred_element_type=jnp.float32,
    ).astype(jnp.bfloat16)


def track_means(tracks, index, every, both, weight, chunk):
    step, width = every.shape[1:]
    rows = SIDE * step
    return pl.pallas_call(
        track_kernel,
        grid_spec=pltpu.PrefetchScalarGridSpec(
            num_scalar_prefetch=2,
            grid=(SIDE // 4,),
            in_specs=[
                pl.BlockSpec(every.shape, lambda i, t, at: (0, 0, 0)),
                pl.BlockSpec(both.shape, lambda i, t, at: (0, 0, 0)),
                pl.BlockSpec((width, 128), lambda i, t, at: (0, at[0] // (128 // chunk))),
            ],
            out_specs=[
                pl.BlockSpec((4 * step, width), lambda i, t, at: (i, 0)),
                pl.BlockSpec((chunk, 4 * step), lambda i, t, at: (0, i)),
                pl.BlockSpec((4 * step, 128), lambda i, t, at: (i, 0)),
            ],
            scratch_shapes=[
                pltpu.VMEM((SIDE, step), jnp.float32),
                pltpu.VMEM((SIDE, step), jnp.float32),
                pltpu.VMEM((128, width), jnp.bfloat16),
            ],
        ),
        out_shape=[
            jax.ShapeDtypeStruct((rows, width), jnp.bfloat16),
            jax.ShapeDtypeStruct((chunk, rows), jnp.bfloat16),
            jax.ShapeDtypeStruct((rows, 128), jnp.float32),
        ],
        compiler_params=pltpu.CompilerParams(vmem_limit_bytes=VMEM_BYTES),
        name="track_means",
    )(tracks, index, every, both, weight)


def error_kernel(track_ref, part_ref, other_ref, both_ref, mean_ref, out_ref, target_buf):
    chunk = part_ref.shape[0]
    back = part_ref.shape[1] // target_buf.shape[0]
    for z in range(SIDE):
        carried = both_ref[z, back : back + 32].astype(jnp.float32)
        for g in range(SIDE):
            target_buf[g * SIDE + z] = carried[
                g % 4 * 8 : g % 4 * 8 + 8, g // 4 * 128 : g // 4 * 128 + 128
            ]
    lane = lax.broadcasted_iota(jnp.int32, (8, 128), 1)
    tiles = []
    for group in range(part_ref.shape[1] // 128):
        low = jnp.zeros((8, 128), jnp.float32)
        high = jnp.zeros((8, 128), jnp.float32)
        for j in range(8):
            track = track_ref[group * 8 + j]
            tile = target_buf[track // 4]
            turn = j * POOL + 128 - track % 4 * POOL
            here = lane // POOL == j
            low = jnp.where(here, pltpu.roll(tile, lax.rem(turn, 128), 1), low)
            high = jnp.where(here, pltpu.roll(tile, lax.rem(turn + 64, 128), 1), high)
        tiles.append(jnp.concatenate([low, high], axis=0))
    target = jnp.concatenate(tiles, axis=1)
    total = part_ref[...].astype(jnp.float32) + other_ref[...].astype(jnp.float32)
    error = (total - target).astype(jnp.bfloat16).astype(jnp.float32)
    grad = jnp.dot(
        error.astype(jnp.bfloat16), mean_ref[...], preferred_element_type=jnp.float32
    ).astype(jnp.bfloat16)
    wide = lax.broadcasted_iota(jnp.int32, (chunk, 128), 1)
    for z in range(SIDE):
        out_ref[z, :chunk] = grad
        for half in range(2):
            tile = jnp.zeros((chunk, 128), jnp.float32)
            for q in range(4):
                source = (half * 4 + q) * 2 + z // 4
                row = error[:, source * 128 : source * 128 + 128]
                turn = (q - z % 4) % 4 * 32
                row = pltpu.roll(row, turn, 1) if turn else row
                tile = jnp.where(wide // 32 == q, row, tile)
            out_ref[z, chunk:, half * 128 : half * 128 + 128] = tile.astype(jnp.bfloat16)


def error_messages(tracks, partial, other, both, mean, seq_count):
    chunk = partial.shape[0]
    vmem = pl.BlockSpec(memory_space=pltpu.VMEM)
    return pl.pallas_call(
        error_kernel,
        in_specs=[pl.BlockSpec(memory_space=pltpu.SMEM), vmem, vmem, vmem, vmem],
        out_shape=jax.ShapeDtypeStruct((SIDE, 2 * chunk, mean.shape[1]), jnp.bfloat16),
        scratch_shapes=[pltpu.VMEM((seq_count, 8, 128), jnp.float32)],
        compiler_params=pltpu.CompilerParams(vmem_limit_bytes=VMEM_BYTES),
        name="error_messages",
    )(tracks, partial, other, both, mean)


def relay_kernel(in_ref, out_ref):
    chunk = in_ref.shape[1] // 2
    lane = lax.broadcasted_iota(jnp.int32, (chunk, 128), 1)
    errors = [in_ref[z, chunk:].astype(jnp.float32) for z in range(SIDE)]
    for g in range(SIDE):
        for z in range(SIDE):
            out_ref[g, z * chunk : z * chunk + chunk] = in_ref[z, :chunk]
        for half in range(2):
            tile = jnp.zeros((chunk, 128), jnp.float32)
            for q in range(4):
                row = errors[half * 4 + q][:, g // 4 * 128 : g // 4 * 128 + 128]
                turn = (q - g % 4) % 4 * 32
                row = pltpu.roll(row, turn, 1) if turn else row
                tile = jnp.where(lane // 32 == q, row, tile)
            out_ref[g, SIDE * chunk :, half * 128 : half * 128 + 128] = tile.astype(jnp.bfloat16)


def relay(x):
    chunk, width = x.shape[1] // 2, x.shape[2]
    return pl.pallas_call(
        relay_kernel,
        out_shape=jax.ShapeDtypeStruct((SIDE, (SIDE + 1) * chunk, width), jnp.bfloat16),
        compiler_params=pltpu.CompilerParams(vmem_limit_bytes=VMEM_BYTES),
        name="relay",
    )(x)


def finish_kernel(index_ref, final_ref, weight_ref, sel_ref, divisor_ref, grad_ref, context_ref):
    back = sel_ref.shape[0]
    chunk = final_ref.shape[1] // (SIDE + 1)
    rows = SIDE * chunk
    tiles = []
    for g in range(SIDE):
        grad_ref[:, g * rows : g * rows + rows] = final_ref[g, :rows].T
        errors = final_ref[g, rows:].astype(jnp.float32)
        for z in range(SIDE):
            tile = errors[:, z // 4 * 128 : z // 4 * 128 + 128]
            tile = pltpu.roll(tile, 128 - z % 4 * 32, 1) if z % 4 else tile
            tiles.append(tile.astype(jnp.bfloat16))
    mean_grad = jnp.dot(
        weight_ref[...], jnp.concatenate(tiles, axis=0), preferred_element_type=jnp.float32
    ).T[:back]
    track_grad = (mean_grad / divisor_ref[:, :1]).astype(jnp.bfloat16)
    context_ref[...] = lax.dot_general(
        sel_ref[...], track_grad, (((0,), (0,)), ((), ())), preferred_element_type=jnp.float32
    ).astype(jnp.bfloat16)


def finish(index, final, weight, sel, divisor):
    width, target_d = weight.shape
    back, tok_rows = sel.shape
    whole = lambda *shape: pl.BlockSpec(shape, lambda i, at: (0, 0))
    return pl.pallas_call(
        finish_kernel,
        grid_spec=pltpu.PrefetchScalarGridSpec(
            num_scalar_prefetch=1,
            grid=(1,),
            in_specs=[
                pl.BlockSpec(final.shape, lambda i, at: (0, 0, 0)),
                whole(*weight.shape),
                whole(*sel.shape),
                pl.BlockSpec((back, 128), lambda i, at: (at[0], 0)),
            ],
            out_specs=[whole(width, target_d), whole(tok_rows, width)],
        ),
        out_shape=[
            jax.ShapeDtypeStruct((width, target_d), jnp.bfloat16),
            jax.ShapeDtypeStruct((tok_rows, width), jnp.bfloat16),
        ],
        compiler_params=pltpu.CompilerParams(vmem_limit_bytes=VMEM_BYTES),
        name="finish",
    )(index, final, weight, sel, divisor)


def local(queries, keys, values, residual, reg_weight, targets, block_track, row_count, pool_slot):
    tok_rows, width = queries.shape
    seq_count = lax.axis_size("seq")
    index = lax.axis_index("seq").astype(jnp.int32).reshape(1)
    owned, pool, target_d = targets.shape

    own_kv, wide = lay_out(keys, values, queries)
    pieces = gather_ring(own_kv, seq_count)
    query_all = lax.all_to_all(wide, "seq", 0, 0, axis_index_groups=GROUP_YX)
    query_all = query_all.reshape(SIDE * tok_rows, width)
    carried, selector, slot_rows = prepare(
        row_count, pool_slot, targets.reshape(owned * pool, target_d)
    )

    part = attend(query_all, pieces, carried, slot_rows)
    part, index = lax.optimization_barrier((part, index))
    part = lax.all_to_all(part, "seq", 0, 0, axis_index_groups=GROUP_YX)
    both = merge(part, residual, selector)
    both = lax.all_to_all(both, "seq", 0, 0, axis_index_groups=GROUP_Z)
    back = selector.shape[0]
    pooled = both[:, :back].reshape(SIDE * back, width)
    every = spread(pooled, GROUP_YX)
    mean, partial, divisor = track_means(
        block_track, index, every, both, reg_weight, target_d // seq_count
    )
    core_mate = lax.ppermute(partial, "head", [(0, 1), (1, 0), (2, 3), (3, 2)])
    partial = (partial.astype(jnp.float32) + core_mate.astype(jnp.float32)).astype(jnp.bfloat16)
    other = lax.ppermute(partial, "head", [(0, 2), (2, 0), (1, 3), (3, 1)])
    final = error_messages(block_track, partial, other, both, mean, seq_count)
    final = lax.all_to_all(final, "seq", 0, 0, axis_index_groups=GROUP_Z)
    final = lax.all_to_all(relay(final), "seq", 0, 0, axis_index_groups=GROUP_YX)
    return finish(index, final, reg_weight, selector, divisor)


def solution(mesh):
    return jax.shard_map(
        local,
        mesh=mesh,
        in_specs=(
            P("seq", "head"),
            P("seq", "head"),
            P("seq", "head"),
            P("seq", "head"),
            P("head", None),
            P("seq", None, None),
            P(),
            P("seq"),
            P("seq", None),
        ),
        out_specs=(P("head", None), P("seq", "head")),
        check_vma=False,
    )
```
